32 devices in a mesh: img: 8 (over z, y), strip: 4 (over x, core).
Axes of the slice: x: 2, y: 2, z: 4, core: 2. Of those that a mesh axis runs over, the one named last changes fastest.
Arguments:
- tokens: bfloat16 [32, 256, 2048], P('img', 'strip'), may hold values from -6 to 6
- cotangent: bfloat16 [32, 256, 2048], P('img', 'strip'), may hold values from -6 to 6
- bin_ids: int32 [32], replicated, may hold values from 0 to 1023
- level_table: float32 [1024, 2048], P(('img', 'strip')), may hold values from -6 to 6
- table_moment: float32 [1024, 2048], P(('img', 'strip')), may hold values from -2048 to 2048
- matrices: float32 [2048, 18, 2048], P(('img', 'strip')), may hold values from -2 to 2
- matrix_moment: float32 [2048, 18, 2048], P(('img', 'strip')), may hold values from -16384 to 16384
- modulation_bias: float32 [6, 2048], P(None, ('img', 'strip')), may hold values from -1 to 1
- bias_moment: float32 [6, 2048], P(None, ('img', 'strip')), may hold values from -32768 to 32768
Outputs:
- block_out: bfloat16 [32, 256, 2048], P('img', 'strip')
- input_grad: bfloat16 [32, 256, 2048], P('img', 'strip')
- table_grad: float32 [1024, 2048], P(('img', 'strip'))
- table_momentum: float32 [1024, 2048], P(('img', 'strip'))
- table_new: float32 [1024, 2048], P(('img', 'strip'))
- matrix_momentum: float32 [2048, 18, 2048], P(('img', 'strip'))
- matrix_new: float32 [2048, 18, 2048], P(('img', 'strip'))
- bias_momentum: float32 [6, 2048], P(None, ('img', 'strip'))
- bias_new: float32 [6, 2048], P(None, ('img', 'strip'))
The draws below stay inside these ranges and needn't reach their ends.
All inputs are finite; a program needn't handle non-finite values.
Results may differ from the reference program's by a relative error of at most 0.017.
The reference program's roundings to bfloat16 on the way count: a program that leaves them out, or rounds other values in their place, can miss the bound.
Values may be sent and summed in bfloat16 or wider, within the bound.
No kernel may reach another device: no remote copies, remote signals or barrier semaphores. Data moves between devices by JAX's collectives and lax.ppermute only.
A program may use at most 832 MiB of HBM per device.

```python
import math
import jax
import jax.numpy as jnp
import numpy as np
from jax import lax

D = 2048
HEADS = 16
HD = 128
FF = 8192
L = 256
BINS = 1024
NS_STEPS = 2
IMAGES = 32
UNITS = 18


def scaled_sample(key, shape, spread_values, bound):
    return jax.random.truncated_normal(key, -bound, bound, shape, jnp.float32) * spread_values


def draw_matrices(key, part):
    key = jax.random.fold_in(key, 11)
    blocks = FF // D
    factors = [1.2, 1.2, 1.0, 5.0] + [1.0] * blocks + [1.4 * math.sqrt(D / FF)] * blocks + [0.8] * 6
    spread_values = (jnp.array(factors, jnp.float32) / math.sqrt(D))[None, :, None]
    return scaled_sample(key, (D, UNITS, D), spread_values, 4.0)


def draw_matrix_moment(key, part):
    key = jax.random.fold_in(key, 12)
    blocks = FF // D
    factors = [0.3] * (4 + 2 * blocks) + [0.5] * 6
    spread_values = (jnp.array(factors, jnp.float32) * math.sqrt(IMAGES * L))[None, :, None]
    return scaled_sample(key, (D, UNITS, D), spread_values, 4.0)


def draw_bias_moment(key, part):
    key = jax.random.fold_in(key, 13)
    spread_values = math.sqrt(IMAGES * L)
    return scaled_sample(key, (6, D), spread_values, 4.0)


def draw_table_moment(key, part):
    key = jax.random.fold_in(key, 14)
    spread_values = 2.0 * math.sqrt(L)
    return scaled_sample(key, (BINS, D), spread_values, 4.0)


def with_ends(values, rng, smallest, largest):
    index_at = [jax.random.randint(jax.random.fold_in(rng, axis), (), 0, length) for axis, length in enumerate(values.shape)]
    longest = values.shape.index(max(values.shape))
    next_to = index_at[:longest] + [(index_at[longest] + 1) % values.shape[longest]] + index_at[longest + 1:]
    return values.at[tuple(index_at)].set(smallest).at[tuple(next_to)].set(largest)


def steps_of(rng, dims, split, smallest, top_value):
    loudness, own = 1.0, jax.random.fold_in(rng, 6)
    for position, shards_of in split:
        heights = jnp.exp(jax.random.uniform(jax.random.fold_in(own, position), (shards_of,), jnp.float32, smallest / len(split), top_value / len(split)))
        loudness = loudness * jnp.repeat(heights, dims[position] // shards_of).reshape([-1 if axis == position else 1 for axis in range(len(dims))])
    return loudness


def rank_table(number_of, lean):
    loads = [(1 << 20) // math.isqrt(standing ** lean) + 1 for standing in range(1, number_of + 1)]
    deviation = 1 + sum(loads) // (1 << 30)
    return np.cumsum(np.array([max(1, weight // deviation) for weight in loads]))


def ranked(key, shape, number_of, slope):
    table = rank_table(number_of, slope)
    lot = jax.random.randint(jax.random.fold_in(key, 1), shape, 0, int(table[number_of - 1]))
    rank = jnp.searchsorted(jnp.asarray(table, jnp.int32), lot, side="right")
    return jax.random.permutation(jax.random.fold_in(key, 2), number_of)[rank].astype(jnp.int32)


def normal_values(own_key, shape, width, most, pieces=(), held_as=jnp.bfloat16):
    loudness = steps_of(own_key, shape, pieces, -0.22, 0.18) if pieces else 1.0
    entries = jax.random.normal(own_key, shape, jnp.float32) * width * loudness
    return jnp.minimum(jnp.maximum(entries, -most), most).astype(held_as)


def setup_inputs(seed: int = 0) -> dict:
    key_of = jax.random.split(jax.random.key(seed), 10)
    return {
        "tokens": normal_values(key_of[0], (IMAGES, L, D), 1.0, 6.0, ((0, 8), (1, 4))),
        "cotangent": normal_values(key_of[1], (IMAGES, L, D), 1.0, 6.0, ((0, 8), (1, 4))),
        "bin_ids": with_ends(ranked(key_of[2], (IMAGES,), BINS, 2), jax.random.fold_in(key_of[2], 3), 0, BINS - 1).astype(jnp.int32),
        "level_table": normal_values(key_of[3], (BINS, D), 1.0, 6.0, ((0, 32),), jnp.float32),
        "table_moment": draw_table_moment(jax.random.fold_in(key_of[9], 71), 0),
        "matrices": draw_matrices(jax.random.fold_in(key_of[9], 71), 0),
        "matrix_moment": draw_matrix_moment(jax.random.fold_in(key_of[9], 71), 0),
        "modulation_bias": jnp.clip(jax.random.uniform(key_of[7], (6, D), jnp.float32, -1.0, 1.0) * steps_of(key_of[7], (6, D), ((1, 32),), -0.4, 0.0), -1.0, 1.0),
        "bias_moment": draw_bias_moment(jax.random.fold_in(key_of[9], 71), 0),
    }


@jax.custom_vjp
def low(v):
    return lax.optimization_barrier(v.astype(jnp.bfloat16)).astype(jnp.float32)

@jax.custom_vjp
def low_back(v):
    return v

def low_keep(v):
    return (low(v), None)

def low_pass(kept, grad):
    return (grad,)

def back_keep(v):
    return (v, None)

def back_low(kept, grad):
    return (low(grad),)
low.defvjp(low_keep, low_pass)
low_back.defvjp(back_keep, back_low)
highest = lax.Precision.HIGHEST
norm_eps = 1e-06
coef_one = 3.4445
coef_two = -4.775
coef_three = 2.0315
matrix_decay = 0.95
vector_decay = 0.9
matrix_rate = 0.5
bias_rate = 0.003
table_rate = 0.02

def round_low(values):
    return lax.optimization_barrier(values.astype(jnp.bfloat16)).astype(jnp.float32)

def normalize(values):
    center = values - lax.optimization_barrier(jnp.mean(values, axis=-1, keepdims=True))
    return center * lax.rsqrt(lax.optimization_barrier(jnp.mean(center * center, axis=-1, keepdims=True)) + norm_eps)

def image_block(inputs, modulation, attention, up_weight, down_weight):
    group_size = inputs.shape[0]
    shift_one = modulation[:, 0][:, None, :]
    scale_one = modulation[:, 1][:, None, :]
    gate_one = modulation[:, 2][:, None, :]
    shift_two = modulation[:, 3][:, None, :]
    scale_two = modulation[:, 4][:, None, :]
    gate_two = modulation[:, 5][:, None, :]
    first_in = low(normalize(inputs) * (1.0 + scale_one) + shift_one)
    projected = jnp.einsum('ntk,juk->ntuj', first_in, attention[:, :3, :], precision=highest)
    projected = low_back(low(projected))
    query = projected[:, :, 0, :].reshape(group_size, L, HEADS, HD)
    keys_all = projected[:, :, 1, :].reshape(group_size, L, HEADS, HD)
    values_all = projected[:, :, 2, :].reshape(group_size, L, HEADS, HD)
    scores = jnp.einsum('nthe,nshe->nhts', query, keys_all, precision=highest) * HD ** (-0.5)
    scores = low_back(scores)
    probs = jax.nn.softmax(scores, axis=-1)
    mixed = jnp.einsum('nhts,nshe->nthe', low(probs), values_all, precision=highest)
    mixed = low_back(low(mixed.reshape(group_size, L, D)))
    branch = low_back(jnp.einsum('ntj,jk->ntk', mixed, attention[:, 3, :], precision=highest))
    middle = inputs + gate_one * branch
    second_in = low(normalize(middle) * (1.0 + scale_two) + shift_two)
    preact = low_back(jnp.einsum('ntk,rbk->ntbr', second_in, up_weight, precision=highest))
    hidden = low(jax.nn.gelu(preact, approximate=False))
    mlp_out = low_back(jnp.einsum('ntbr,rbk->ntk', hidden, down_weight, precision=highest))
    return middle + gate_two * mlp_out

def reference(tokens, cotangent, bin_ids, level_table, table_moment, matrices, matrix_moment, modulation_bias, bias_moment):
    blocks = FF // D
    group = math.gcd(IMAGES, max(1, 4096 // L))

    def forward(inputs, weights, table_values, bias_values):
        condition = table_values[bin_ids]
        active = low(jax.nn.silu(condition))
        ada_weight = low(weights[:, 4 + 2 * blocks:, :])
        modulation = jnp.einsum('nk,ruk->nur', active, ada_weight, precision=highest) + bias_values[None]
        attention = low(weights[:, :4, :])
        up_weight = low(weights[:, 4:4 + blocks, :])
        down_weight = low(weights[:, 4 + blocks:4 + 2 * blocks, :])
        checked = jax.checkpoint(image_block)

        def scan_step(carry, items):
            return (carry, checked(items[0], items[1], attention, up_weight, down_weight))
        grouped = (inputs.reshape(IMAGES // group, group, L, D), modulation.reshape(IMAGES // group, group, 6, D))
        _, outputs = lax.scan(scan_step, jnp.zeros((), jnp.float32), grouped)
        return outputs.reshape(IMAGES, L, D)
    total, pullback = jax.vjp(forward, tokens.astype(jnp.float32), matrices, level_table, modulation_bias)
    grad_input, grad_weights, grad_table, grad_bias = pullback(cotangent.astype(jnp.float32))
    matrix_momentum = matrix_decay * matrix_moment + grad_weights

    def orthogonalize(unit):
        current = round_low(unit)
        result = unit
        for iteration in range(NS_STEPS):
            gram = jnp.dot(current.T, current, precision=highest)
            if iteration == 0:
                factor = 1.0 / (jnp.sqrt(jnp.trace(gram)) + 1e-07)
                gram_low = round_low(gram * factor * factor)
                product = jnp.dot(current, gram_low, precision=highest) * factor
                square = jnp.dot(round_low(product), gram_low, precision=highest)
                result = coef_one * factor * current + coef_two * product + coef_three * square
            else:
                gram_low = round_low(gram)
                product = jnp.dot(current, gram_low, precision=highest)
                square = jnp.dot(round_low(product), gram_low, precision=highest)
                result = coef_one * current + coef_two * product + coef_three * square
            current = round_low(result)
        return result
    ortho = lax.map(orthogonalize, jnp.moveaxis(matrix_momentum, 1, 0))
    step_size = matrix_rate * 0.2 * math.sqrt(D)
    matrix_new = matrices - step_size * jnp.moveaxis(ortho, 0, 1)
    bias_momentum = vector_decay * bias_moment + grad_bias
    bias_new = modulation_bias - bias_rate * bias_momentum
    table_momentum = vector_decay * table_moment + grad_table
    table_new = level_table - table_rate * table_momentum
    return (total.astype(jnp.bfloat16), grad_input.astype(jnp.bfloat16), grad_table, table_momentum, table_new, matrix_momentum, matrix_new, bias_momentum, bias_new)
```

```python
import math

import jax
import jax.numpy as jnp
from jax import lax
from jax.sharding import PartitionSpec as P

HEADS = 16
HD = 128

highest = lax.Precision.HIGHEST
norm_eps = 1e-06
coef_one = 3.4445
coef_two = -4.775
coef_three = 2.0315
matrix_decay = 0.95
vector_decay = 0.9
matrix_rate = 0.5
bias_rate = 0.003
table_rate = 0.02

WORLD = ("img", "strip")
CORE, ALONG_X, ALONG_Y = 1, 2, 4
TEAM = 8
low = jnp.bfloat16
wide = jnp.float32


def dot(spec, left, right):
    return jnp.einsum(spec, left, right, preferred_element_type=wide)


def add(left, right):
    return left.astype(wide) + right.astype(wide)


def normalize(values):
    center = values - jnp.mean(values, axis=-1, keepdims=True)
    inverse = lax.rsqrt(jnp.mean(center * center, axis=-1, keepdims=True) + norm_eps)
    return (center * inverse, inverse)


def norm_back(grad_hat, normed, inverse):
    mean_grad = jnp.mean(grad_hat, axis=-1, keepdims=True)
    mean_cross = jnp.mean(grad_hat * normed, axis=-1, keepdims=True)
    return inverse * (grad_hat - mean_grad - normed * mean_cross)


def gelu_slope(values):
    cumulative = 0.5 * (1.0 + lax.erf(values * 0.7071067811865476))
    density = jnp.exp(-0.5 * values * values) * 0.3989422804014327
    return cumulative + values * density


def silu_slope(values):
    logistic = jax.nn.sigmoid(values)
    return logistic * (1.0 + values * (1.0 - logistic))


class Fabric:
    def __init__(self):
        self.count = lax.axis_size("img") * lax.axis_size("strip")
        self.planes = self.count // TEAM
        self.me = lax.axis_index(WORLD)
        self.plane = self.me // TEAM
        self.seat = self.me % TEAM

    def swap(self, value, bit):
        return lax.ppermute(value, WORLD, [(d, d ^ bit) for d in range(self.count)])

    def hop(self, value, step, first, last):
        pairs = [(d, d + step * TEAM) for d in range(first * TEAM, (last + 1) * TEAM)]
        return lax.ppermute(value, WORLD, pairs)

    def turn(self, value, offset, limit=None):
        pairs = []
        for d in range(self.count):
            target = (d // TEAM + offset) % self.planes
            if limit is None or target < limit:
                pairs.append((d, target * TEAM + d % TEAM))
        return lax.ppermute(value, WORLD, pairs)

    def back(self, value, offset, limit):
        pairs = []
        for d in range(self.count):
            if d // TEAM < limit:
                pairs.append((d, (d // TEAM - offset) % self.planes * TEAM + d % TEAM))
        return lax.ppermute(value, WORLD, pairs)

    def gather_planes(self, shard):
        count = self.planes
        right, left = [shard], [shard]
        for k in range(1, count):
            right.append(self.hop(right[-1], 1, k - 1, count - 2))
            left.append(self.hop(left[-1], -1, 1, count - k))
        slots = [shard]
        for j in range(1, count):
            slots.append(jnp.where(self.plane >= j, right[j], left[count - j]))
        return jnp.concatenate(slots, axis=0)

    def reduce_planes(self, slots):
        count = self.planes
        right = left = None
        for k in range(1, count):
            onward = slots[k] if right is None else add(slots[k], right).astype(low)
            right = self.hop(onward, 1, 0, k - 1)
            onward = slots[count - k] if left is None else add(slots[count - k], left).astype(low)
            left = self.hop(onward, -1, count - k, count - 1)
        return slots[0].astype(wide) + right.astype(wide) + left.astype(wide)

    def share(self, first, second):
        first_x = self.swap(first, ALONG_X)
        second_y = self.swap(second, ALONG_Y)
        first_y = self.swap(first, ALONG_Y)
        second_x = self.swap(second, ALONG_X)
        first_xy = self.swap(first_x, ALONG_Y)
        second_yx = self.swap(second_y, ALONG_X)
        own_first = [first, first_y, first_x, first_xy]
        own_second = [second, second_x, second_y, second_yx]
        far_first = [self.swap(piece, CORE) for piece in own_first]
        far_second = [self.swap(piece, CORE) for piece in own_second]
        return (
            jnp.concatenate(own_first + far_first, axis=0),
            jnp.concatenate(own_second + far_second, axis=0),
        )

    def settle(self, first, second):
        def halves(near, far, bit):
            return add(near, self.swap(far, bit))

        def chain(parts, one, two):
            parts = parts.reshape((2, 2, 2) + (parts.shape[0] // 8,) + parts.shape[1:])
            parts = halves(parts[0], parts[1], CORE).astype(low)
            parts = halves(parts[0], parts[1], one).astype(low)
            return halves(parts[0], parts[1], two)

        return chain(first, ALONG_X, ALONG_Y), chain(second, ALONG_Y, ALONG_X)


def to_images(rows, second):
    inner = rows.shape[0] // 16
    rows = rows.reshape((2, 2, 2, 2, inner) + rows.shape[1:])
    tail = tuple(range(5, rows.ndim))
    order = (1, 3, 0, 2, 4) if second else (2, 3, 0, 1, 4)
    return rows.transpose(order + tail).reshape((4, 4 * inner) + rows.shape[5:])


def to_rows(images, second):
    inner = images.shape[1] // 4
    images = images.reshape((2, 2, 2, 2, inner) + images.shape[2:])
    tail = tuple(range(5, images.ndim))
    order = (2, 0, 3, 1, 4) if second else (2, 3, 0, 1, 4)
    return images.transpose(order + tail).reshape((16 * inner,) + images.shape[5:])


def spread(values, second):
    if second:
        return values[None, :, None, :, None]
    return values[None, None, :, :, None]


def attend(projected):
    query, keys_all, values_all = projected[:, :, 0], projected[:, :, 1], projected[:, :, 2]
    scores = dot("nthe,nshe->nhts", query, keys_all) * HD ** (-0.5)
    summit = jnp.max(scores, axis=-1, keepdims=True)
    exponent = jnp.exp(scores - summit)
    totals = jnp.sum(exponent, axis=-1, keepdims=True)
    probs = exponent / totals
    mixed = dot("nhts,nshe->nthe", probs.astype(low), values_all)
    return mixed.astype(low), probs


def attend_back(projected, probs, grad_heads):
    factor = HD ** (-0.5)
    query, keys_all, values_all = projected[:, :, 0], projected[:, :, 1], projected[:, :, 2]
    grad_probs = dot("nthe,nshe->nhts", grad_heads, values_all)
    grad_scores = (
        probs * (grad_probs - jnp.sum(probs * grad_probs, axis=-1, keepdims=True))
    ).astype(low)
    grad_query = dot("nhts,nshe->nthe", grad_scores, keys_all) * factor
    grad_keys = dot("nhts,nthe->nshe", grad_scores, query) * factor
    grad_values = dot("nhts,nthe->nshe", probs.astype(low), grad_heads)
    return jnp.stack([grad_query, grad_keys, grad_values], axis=2).astype(low)


def on_device(
    tokens,
    cotangent,
    bin_ids,
    level_table,
    table_moment,
    matrices,
    matrix_moment,
    modulation_bias,
    bias_moment,
):
    fabric = Fabric()
    planes, plane, seat = fabric.planes, fabric.plane, fabric.seat
    strips = lax.axis_size("strip")
    here, inner, width = tokens.shape
    shard_rows, units, _ = matrices.shape
    images = bin_ids.shape[0]
    table_rows = level_table.shape[0]
    blocks = (units - 10) // 2
    start_down = 4 + blocks
    start_ada = 4 + 2 * blocks
    slot_rows = planes * shard_rows

    by_unit = matrices.astype(low).transpose(1, 0, 2)

    def gathered(first, last):
        rows = by_unit[first:last].reshape((last - first) * shard_rows, width)
        return fabric.gather_planes(rows)

    attention = gathered(0, 4)
    up_weight = gathered(4, start_down)
    down_weight = gathered(start_down, start_ada)

    def token_halves(values):
        half = here // 2
        return (
            values[:half].reshape(half * inner, width),
            values[half:].reshape(half * inner, width),
        )

    whole_tokens = fabric.share(*token_halves(tokens))
    whole_upstream = fabric.share(*token_halves(cotangent))

    row_ids = fabric.me * table_rows + jnp.arange(table_rows, dtype=jnp.int32)
    selector = (bin_ids[:, None] == row_ids[None, :]).astype(wide)
    active_rows = jax.nn.silu(level_table).astype(low)
    active = jnp.dot(selector.astype(low), active_rows, preferred_element_type=wide).astype(low)
    others = [fabric.turn(active, offset) for offset in range(1, planes)]
    for other in others:
        active = active + other
    for bit in (CORE, ALONG_X, ALONG_Y):
        active = active + fabric.swap(active, bit)
    ada_weight = matrices[:, start_ada:, :].astype(low)
    mod_columns = dot("nk,ruk->nur", active, ada_weight) + modulation_bias[None]
    in_plane = images // planes
    mod_parts = jnp.broadcast_to(
        mod_columns.reshape(planes, 1, in_plane, 6, shard_rows),
        (planes, TEAM, in_plane, 6, shard_rows),
    ).reshape(fabric.count, in_plane, 6, shard_rows)
    mod_parts = lax.all_to_all(mod_parts, WORLD, split_axis=0, concat_axis=0, tiled=True)
    modulation = mod_parts.transpose(1, 2, 0, 3).reshape(2, here, 6, width)
    side = seat // 4
    modulation = jnp.where(side == 0, modulation, modulation[::-1])
    local = modulation[0][:, :, None, :]
    shift_one, scale_one, gate_one = local[:, 0], local[:, 1], local[:, 2]
    shift_two, scale_two, gate_two = local[:, 3], local[:, 4], local[:, 5]

    def half_modulation(which, second):
        half = here // 2
        chosen = modulation[:, half:] if second else modulation[:, :half]
        return spread(chosen[:, :, which], second)

    def open_rows(rows):
        return rows.reshape(2, 2, 2, 2, inner, width)

    first_in = []
    for second in (0, 1):
        normed, _ = normalize(open_rows(whole_tokens[second]).astype(wide))
        value = normed * (1.0 + half_modulation(1, second)) + half_modulation(0, second)
        first_in.append(value.astype(low).reshape(-1, width))
    grad_mlp = [
        (open_rows(whole_upstream[second]).astype(wide) * half_modulation(5, second))
        .astype(low)
        .reshape(-1, width)
        for second in (0, 1)
    ]

    peers = HD // shard_rows
    heads = planes // peers
    attention = attention.reshape(planes, 4, shard_rows, width)
    place = fabric.me % peers

    def mates(offset):
        return [
            (d, d // peers * peers + (d % peers + offset) % peers) for d in range(fabric.count)
        ]

    pieces = [lax.dynamic_slice_in_dim(attention, place * heads, heads, 0)]
    for offset in range(1, peers):
        target = (place + offset) % peers
        payload = lax.dynamic_slice_in_dim(attention, target * heads, heads, 0)
        pieces.append(lax.ppermute(payload, WORLD, mates(offset)))
    attention = jnp.stack(pieces).transpose(2, 1, 0, 3, 4).reshape(4, heads * HD, width)
    weight_in = attention[:3].reshape(3 * heads * HD, width)
    weight_out = attention[3]

    projected, probs, mixed, branch_parts = [], [], [], []
    for second in (0, 1):
        rows = dot("tk,jk->tj", first_in[second], weight_in).astype(low)
        whole = to_images(rows, second).reshape(4, 4 * inner, 3, heads, HD)
        blend, kept = attend(whole)
        blend = to_rows(blend.reshape(4, 4 * inner, heads * HD), second)
        projected.append(whole)
        probs.append(kept)
        mixed.append(blend)
        branch_parts.append(dot("tj,jk->tk", blend, weight_out).astype(low))

    def joined(parts):
        return jnp.concatenate(
            [part.reshape(here // 2, inner, width) for part in fabric.settle(*parts)], axis=0
        )

    branch = joined(branch_parts)
    inputs = tokens.astype(wide)
    middle = inputs + gate_one * branch
    normed_two, inverse_two = normalize(middle)
    second_in = fabric.share(
        *token_halves((normed_two * (1.0 + scale_two) + shift_two).astype(low))
    )
    preact = [dot("tk,jk->tj", rows, up_weight) for rows in second_in]
    hidden = [jax.nn.gelu(rows, approximate=False).astype(low) for rows in preact]
    mlp_parts = [dot("tj,jk->tk", rows, down_weight).astype(low) for rows in hidden]
    mlp_out = joined(mlp_parts)
    block_out = (middle + gate_two * mlp_out).astype(low)

    def over_halves(left, right):
        return dot("tj,tk->jk", jnp.concatenate(left, 0), jnp.concatenate(right, 0)).astype(low)

    down_grad = over_halves(hidden, grad_mlp)
    grad_pre = [
        (dot("tk,jk->tj", grad_mlp[s], down_weight) * gelu_slope(preact[s])).astype(low)
        for s in (0, 1)
    ]
    grad_in = joined([dot("tj,jk->tk", rows, up_weight).astype(low) for rows in grad_pre])
    up_grad = over_halves(grad_pre, second_in)

    grad_total = cotangent.astype(wide)
    grad_gate_two = jnp.sum(grad_total * mlp_out, axis=1)
    grad_shift_two = jnp.sum(grad_in, axis=1)
    grad_scale_two = jnp.sum(grad_in * normed_two, axis=1)
    grad_middle = grad_total + norm_back(grad_in * (1.0 + scale_two), normed_two, inverse_two)
    grad_gate_one = jnp.sum(grad_middle * branch, axis=1)
    grad_branch = fabric.share(*token_halves((grad_middle * gate_one).astype(low)))

    grad_project, grad_first_parts = [], []
    for second in (0, 1):
        grad_mixed = dot("tk,jk->tj", grad_branch[second], weight_out).astype(low)
        grad_heads = to_images(grad_mixed, second).reshape(4, 4 * inner, heads, HD)
        whole = attend_back(projected[second], probs[second], grad_heads)
        whole = to_rows(whole.reshape(4, 4 * inner, 3 * heads * HD), second)
        grad_project.append(whole)
        grad_first_parts.append(dot("tj,jk->tk", whole, weight_in).astype(low))
    in_grad = over_halves(grad_project, first_in).reshape(3, heads * HD, width)
    out_grad = over_halves(mixed, list(grad_branch)).reshape(1, heads * HD, width)
    attention_grad = jnp.concatenate([in_grad, out_grad], axis=0)
    attention_grad = attention_grad.reshape(4, heads, peers, shard_rows, width)
    attention_grad = attention_grad.transpose(2, 1, 0, 3, 4)
    returned = [attention_grad[0]]
    for offset in range(1, peers):
        returned.append(lax.ppermute(attention_grad[offset], WORLD, mates(peers - offset)))
    attention_grad = jnp.concatenate(returned + returned[:-1], axis=0)
    attention_grad = lax.dynamic_slice_in_dim(
        attention_grad, (peers - place) % peers * heads, planes, 0
    ).reshape(planes, 4 * shard_rows, width)

    grad_first = joined(grad_first_parts)
    normed_one, inverse_one = normalize(inputs)
    grad_shift_one = jnp.sum(grad_first, axis=1)
    grad_scale_one = jnp.sum(grad_first * normed_one, axis=1)
    input_grad = (
        grad_middle + norm_back(grad_first * (1.0 + scale_one), normed_one, inverse_one)
    ).astype(low)

    def to_holders(parts):
        stacked = jnp.stack(parts, axis=1).astype(low)
        held = lax.all_to_all(stacked, WORLD, split_axis=2, concat_axis=0, tiled=True)
        held = held.reshape(fabric.count // strips, strips, here, len(parts), shard_rows)
        return jnp.sum(held.astype(wide), axis=1).reshape(images, len(parts), shard_rows)

    late_mod = to_holders([grad_gate_one, grad_shift_two, grad_scale_two, grad_gate_two])
    early_mod = to_holders([grad_shift_one, grad_scale_one])
    grad_mod_all = jnp.concatenate([early_mod, late_mod], axis=1)
    active_wide = active.astype(wide)

    def ada_grad(grads):
        return jnp.einsum("nur,nk->urk", grads, active_wide, precision=highest)

    bias_grad = jnp.sum(grad_mod_all, axis=0)
    grad_active = lax.psum(
        jnp.einsum("nur,ruk->nk", grad_mod_all, ada_weight.astype(wide), precision=highest), WORLD
    )
    table_grad = jnp.dot(selector.T, grad_active, precision=highest) * silu_slope(level_table)

    def summed(grad):
        return fabric.reduce_planes(grad.reshape(planes, -1, width)).reshape(
            -1, shard_rows, width
        )

    moment = matrix_moment.transpose(1, 0, 2)

    def fresh(first, grad):
        return matrix_decay * moment[first : first + grad.shape[0]] + grad

    def orthogonal(batch):
        count = batch.shape[0]
        own = batch.astype(low)
        if count < planes:
            own = jnp.concatenate(
                [own, jnp.zeros((planes - count, shard_rows, width), low)], axis=0
            )
        rows = [lax.dynamic_index_in_dim(own, plane, 0, keepdims=False)]
        for offset in range(1, planes):
            payload = lax.dynamic_index_in_dim(own, (plane + offset) % planes, 0, keepdims=False)
            rows.append(fabric.turn(payload, offset, count))
        rows = jnp.concatenate(rows, axis=0)
        half = slot_rows // 2
        first, second = fabric.share(rows[:half], rows[half:])
        current = jnp.concatenate([first, second], axis=0)
        trace_sum = jnp.sum(jnp.square(current.astype(wide)))
        scaling = 1.0 / (jnp.sqrt(trace_sum) + 1e-07)
        gram_low = (dot("rk,rl->kl", current, current) * scaling * scaling).astype(low)
        product = dot("rk,kl->rl", current, gram_low) * scaling
        square = dot("rk,kl->rl", product.astype(low), gram_low)
        result = (coef_one * scaling) * current.astype(wide) + coef_two * product
        current = (result + coef_three * square).astype(low)
        gram_low = dot("rk,rl->kl", current, current).astype(low)
        mine = jnp.concatenate([current[:half], current[slot_rows * 4 : slot_rows * 4 + half]], 0)
        product = dot("rk,kl->rl", mine, gram_low)
        square = dot("rk,kl->rl", product.astype(low), gram_low)
        result = coef_one * mine.astype(wide) + coef_two * product + coef_three * square
        result = result.astype(low).reshape(planes, shard_rows, width)
        done = [result[0]]
        for offset in range(1, planes):
            done.append(fabric.back(result[offset], offset, count))
        done = jnp.concatenate([jnp.stack(done), jnp.stack(done[:-1])], axis=0)
        start = (planes - plane) % planes
        return lax.dynamic_slice_in_dim(done, start, planes, 0)[:count]

    down_momentum = fresh(start_down, summed(down_grad))
    up_momentum = fresh(4, summed(up_grad))
    late_momentum = fresh(start_ada + 2, ada_grad(late_mod))
    attention_momentum = fresh(0, summed(attention_grad))
    early_momentum = fresh(start_ada, ada_grad(early_mod))
    down_ortho = orthogonal(down_momentum)
    up_ortho = orthogonal(up_momentum)
    late_ortho = orthogonal(late_momentum)
    attention_ortho = orthogonal(attention_momentum)
    early_ortho = orthogonal(early_momentum)
    momentum = jnp.concatenate(
        [attention_momentum, up_momentum, down_momentum, early_momentum, late_momentum], axis=0
    ).transpose(1, 0, 2)
    ortho = jnp.concatenate(
        [attention_ortho, up_ortho, down_ortho, early_ortho, late_ortho], axis=0
    ).transpose(1, 0, 2)
    step_size = matrix_rate * 0.2 * math.sqrt(width)
    matrix_new = matrices - step_size * ortho.astype(wide)
    bias_momentum = vector_decay * bias_moment + bias_grad
    bias_new = modulation_bias - bias_rate * bias_momentum
    table_momentum = vector_decay * table_moment + table_grad
    table_new = level_table - table_rate * table_momentum
    return (
        block_out,
        input_grad,
        table_grad,
        table_momentum,
        table_new,
        momentum,
        matrix_new,
        bias_momentum,
        bias_new,
    )


def solution(mesh):
    whole = P(("img", "strip"), None, None)
    table = P(("img", "strip"), None)
    strip = P("img", "strip", None)
    bias = P(None, ("img", "strip"))
    return jax.shard_map(
        on_device,
        mesh=mesh,
        in_specs=(strip, strip, P(), table, table, whole, whole, bias, bias),
        out_specs=(strip, strip, table, table, table, whole, whole, bias, bias),
        check_vma=False,
    )
```

```python
import functools
import math

import jax
import jax.numpy as jnp
from jax import lax
from jax.experimental import pallas as pl
from jax.experimental.pallas import tpu as pltpu
from jax.sharding import PartitionSpec as P

HEADS = 16
HD = 128

highest = lax.Precision.HIGHEST
norm_eps = 1e-06
coef_one = 3.4445
coef_two = -4.775
coef_three = 2.0315
matrix_decay = 0.95
vector_decay = 0.9
matrix_rate = 0.5
bias_rate = 0.003
table_rate = 0.02

WORLD = ("img", "strip")
CORE, ALONG_X, ALONG_Y = 1, 2, 4
TEAM = 8
low = jnp.bfloat16
wide = jnp.float32


def dot(spec, left, right):
    return jnp.einsum(spec, left, right, preferred_element_type=wide)


def after(value, *earlier):
    return lax.optimization_barrier((value, *earlier))[0]


def after_all(values, *earlier):
    return lax.optimization_barrier((*values, *earlier))[: len(values)]


def hold(*values):
    return lax.optimization_barrier(values)


def fence(flag, body, *operands):
    shapes = jax.eval_shape(body, *operands)
    empty = lambda *_: jax.tree.map(lambda leaf: jnp.zeros(leaf.shape, leaf.dtype), shapes)
    return lax.cond(flag, body, empty, *operands)


def add(left, right):
    return left.astype(wide) + right.astype(wide)


def normalize(values):
    center = values - jnp.mean(values, axis=-1, keepdims=True)
    inverse = lax.rsqrt(jnp.mean(center * center, axis=-1, keepdims=True) + norm_eps)
    return (center * inverse, inverse)


def norm_back(grad_hat, normed, inverse):
    mean_grad = jnp.mean(grad_hat, axis=-1, keepdims=True)
    mean_cross = jnp.mean(grad_hat * normed, axis=-1, keepdims=True)
    return inverse * (grad_hat - mean_grad - normed * mean_cross)


def gelu_slope(values):
    cumulative = 0.5 * (1.0 + lax.erf(values * 0.7071067811865476))
    density = jnp.exp(-0.5 * values * values) * 0.3989422804014327
    return cumulative + values * density


def silu_slope(values):
    logistic = jax.nn.sigmoid(values)
    return logistic * (1.0 + values * (1.0 - logistic))


class Fabric:
    def __init__(self):
        self.count = lax.axis_size("img") * lax.axis_size("strip")
        self.planes = self.count // TEAM
        self.me = lax.axis_index(WORLD)
        self.plane = self.me // TEAM
        self.seat = self.me % TEAM
        self.lines = [
            [plane * TEAM + seat for plane in range(self.planes)] for seat in range(TEAM)
        ]

    def swap(self, value, bit):
        return lax.ppermute(value, WORLD, [(d, d ^ bit) for d in range(self.count)])

    def turn(self, value, offset):
        pairs = [(d, (d + offset * TEAM) % self.count) for d in range(self.count)]
        return lax.ppermute(value, WORLD, pairs)

    def gather_planes(self, shard):
        return lax.all_gather(shard, WORLD, axis=0, tiled=True, axis_index_groups=self.lines)

    def reduce_planes(self, parts):
        return lax.psum_scatter(
            parts, WORLD, scatter_dimension=0, tiled=True, axis_index_groups=self.lines
        )

    def trade_planes(self, blocks):
        return lax.all_to_all(
            blocks, WORLD, split_axis=0, concat_axis=0, tiled=True, axis_index_groups=self.lines
        )

    def team_total(self, value):
        for bit in (CORE, ALONG_X, ALONG_Y):
            value = value + self.swap(value, bit)
        return value

    def plane_total(self, value):
        others = [self.turn(value, offset) for offset in range(1, self.planes)]
        for other in others:
            value = value + other
        return value

    def share(self, rows, between=()):
        half = rows.shape[0] // 2
        first, second = rows[:half], rows[half:]
        first_x = self.swap(first, ALONG_X)
        second_y = self.swap(second, ALONG_Y)
        first_y = self.swap(first, ALONG_Y)
        second_x = self.swap(second, ALONG_X)
        first_xy = self.swap(after(first_x, *between), ALONG_Y)
        second_xy = self.swap(after(second_y, *between), ALONG_X)
        return jnp.concatenate(
            [rows, first_x, second_x, first_y, second_y, first_xy, second_xy], axis=0
        )

    def settle(self, near, near_too, beside=None):
        width = near.shape[-1]
        size = near.shape[0] // 8
        near = add(near, near_too).astype(low).reshape(2, 2, 2, size, width)
        first, second = near[:, :, 0], near[:, :, 1]
        first_x = self.swap(first[:, 1], ALONG_X)
        second_y = self.swap(second[1], ALONG_Y)
        done = None
        if beside is not None:
            first, second, first_x, second_y, done = hold(
                first, second, first_x, second_y, beside()
            )
        first = add(first[:, 0], first_x).astype(low)
        second = add(second[0], second_y).astype(low)
        first = add(first[0], self.swap(first[1], ALONG_Y))
        second = add(second[0], self.swap(second[1], ALONG_X))
        total = jnp.concatenate([first, second], axis=0)
        return total if beside is None else (total, done)


VMEM_BYTES = 60 * 2**20
QUICK = pl.CostEstimate(flops=1, bytes_accessed=1, transcendentals=0)


def attend_body(projected_ref, mixed_ref):
    size = mixed_ref.shape[-1]
    shape = mixed_ref.shape[:-1] + (HD,)
    tokens = math.prod(shape[:-1])
    for first in range(0, size, HD):

        def read(unit):
            block = projected_ref[..., unit * size + first : unit * size + first + HD]
            return block.reshape(tokens, HD)

        scores = lax.dot_general(
            read(0), read(1), (((1,), (1,)), ((), ())), preferred_element_type=wide
        ) * HD ** (-0.5)
        exponent = jnp.exp(scores - jnp.max(scores, axis=-1, keepdims=True))
        probs = (exponent / jnp.sum(exponent, axis=-1, keepdims=True)).astype(low)
        mixed = jnp.dot(probs, read(2), preferred_element_type=wide).astype(low)
        mixed_ref[..., first : first + HD] = mixed.reshape(shape)


def attend_back_body(projected_ref, grad_ref, out_ref):
    size = grad_ref.shape[-1]
    shape = grad_ref.shape[:-1] + (HD,)
    tokens = math.prod(shape[:-1])
    factor = HD ** (-0.5)
    across = (((1,), (1,)), ((), ()))
    down = (((0,), (0,)), ((), ()))
    for first in range(0, size, HD):

        def read(unit):
            block = projected_ref[..., unit * size + first : unit * size + first + HD]
            return block.reshape(tokens, HD)

        def write(unit, value):
            part = slice(unit * size + first, unit * size + first + HD)
            out_ref[..., part] = value.astype(low).reshape(shape)

        query, keys_all, values_all = read(0), read(1), read(2)
        grad_heads = grad_ref[..., first : first + HD].reshape(tokens, HD)
        scores = lax.dot_general(query, keys_all, across, preferred_element_type=wide) * factor
        exponent = jnp.exp(scores - jnp.max(scores, axis=-1, keepdims=True))
        probs = exponent / jnp.sum(exponent, axis=-1, keepdims=True)
        grad_probs = lax.dot_general(grad_heads, values_all, across, preferred_element_type=wide)
        cross = jnp.sum(probs * grad_probs, axis=-1, keepdims=True)
        grad_scores = (probs * (grad_probs - cross)).astype(low)
        write(0, jnp.dot(grad_scores, keys_all, preferred_element_type=wide) * factor)
        write(1, lax.dot_general(grad_scores, query, down, preferred_element_type=wide) * factor)
        write(2, lax.dot_general(probs.astype(low), grad_heads, down, preferred_element_type=wide))


def over_images(body, here, inner, arrays, out_features):
    def block(features):
        return pl.BlockSpec(
            (2, 1, 2, 1, inner, features), lambda side, image: (0, side, 0, image, 0, 0)
        )

    arrays = [rows.reshape(2, 2, 2, here, inner, rows.shape[-1]) for rows in arrays]
    result = pl.pallas_call(
        body,
        grid=(2, here),
        in_specs=[block(rows.shape[-1]) for rows in arrays],
        out_specs=block(out_features),
        out_shape=jax.ShapeDtypeStruct((2, 2, 2, here, inner, out_features), low),
        compiler_params=pltpu.CompilerParams(vmem_limit_bytes=32 * 2**20),
        cost_estimate=QUICK,
    )(*arrays)
    return result.reshape(-1, out_features)


def modulate_body(rows_ref, modulation_ref, out_ref):
    values = rows_ref[0, 0].astype(wide)
    center = values - jnp.mean(values, axis=-1, keepdims=True)
    inverse = lax.rsqrt(jnp.mean(center * center, axis=-1, keepdims=True) + norm_eps)
    shift = modulation_ref[0, :, 0:1, :]
    scale = modulation_ref[0, :, 1:2, :]
    out_ref[0, 0] = (center * inverse * (1.0 + scale) + shift).astype(low)


def modulate(rows, modulation):
    sides, seats, here, inner, width = rows.shape
    block = pl.BlockSpec((1, 1, here, inner, width), lambda y, x: (y, x, 0, 0, 0))
    return pl.pallas_call(
        modulate_body,
        grid=(sides, seats),
        in_specs=[
            block,
            pl.BlockSpec((1, here) + modulation.shape[2:], lambda y, x: (y, 0, 0, 0)),
        ],
        out_specs=block,
        out_shape=jax.ShapeDtypeStruct(rows.shape, low),
        compiler_params=pltpu.CompilerParams(vmem_limit_bytes=48 * 2**20),
        cost_estimate=QUICK,
    )(rows, modulation)


def gate_body(hidden_ref, weight_ref, upstream_ref, part_ref, cross_ref):
    part = jnp.dot(hidden_ref[...], weight_ref[...], preferred_element_type=wide)
    part_ref[...] = part.astype(low)
    here, inner, width = upstream_ref.shape[2:]
    cross = upstream_ref[0, 0].astype(wide) * part.reshape(here, inner, width)
    cross = jnp.sum(cross, axis=1)[None]

    @pl.when(pl.program_id(1) == 0)
    def _():
        cross_ref[...] = cross

    @pl.when(pl.program_id(1) > 0)
    def _():
        cross_ref[...] += cross


def gate_sums(hidden, weight, upstream):
    sides, seats, here, inner, width = upstream.shape
    size = here * inner
    return pl.pallas_call(
        gate_body,
        grid=(sides, seats),
        in_specs=[
            pl.BlockSpec((size, hidden.shape[1]), lambda y, x: (y * seats + x, 0)),
            pl.BlockSpec(weight.shape, lambda y, x: (0, 0)),
            pl.BlockSpec((1, 1, here, inner, width), lambda y, x: (y, x, 0, 0, 0)),
        ],
        out_specs=[
            pl.BlockSpec((size, width), lambda y, x: (y * seats + x, 0)),
            pl.BlockSpec((1, here, width), lambda y, x: (y, 0, 0)),
        ],
        out_shape=[
            jax.ShapeDtypeStruct((hidden.shape[0], width), low),
            jax.ShapeDtypeStruct((sides, here, width), wide),
        ],
        compiler_params=pltpu.CompilerParams(vmem_limit_bytes=VMEM_BYTES),
        cost_estimate=QUICK,
    )(hidden, weight, upstream)


GRAM_TILE = 512
ROW_BLOCK = 256
COLUMN_TILE = 512


def gram_body(core_ref, near_ref, far_ref, out_ref, factor_ref, kept_ref, *, scaled):
    half = near_ref.shape[1] // 2
    tile = out_ref.shape[0]
    step = pl.program_id(0)
    if scaled:

        @pl.when(step == 0)
        def _():
            near, far = near_ref[...].astype(wide), far_ref[...].astype(wide)
            trace = jnp.sum(near * near) + jnp.sum(far * far)
            kept_ref[0] = 1.0 / (jnp.sqrt(trace) + 1e-07)

        factor = kept_ref[0]
    else:
        factor = jnp.float32(1.0)
    factor_ref[0] = factor
    start = pl.multiple_of(core_ref[0] * half + step * tile, tile)
    rows = (((0,), (0,)), ((), ()))
    total = lax.dot_general(
        near_ref[:, pl.ds(start, tile)], near_ref[...], rows, preferred_element_type=wide
    )
    total += lax.dot_general(
        far_ref[:, pl.ds(start, tile)], far_ref[...], rows, preferred_element_type=wide
    )
    if scaled:
        total = total * factor * factor
    out_ref[...] = total.astype(low)


def half_gram(core, near, far, scaled):
    rows, width = near.shape
    full = pl.BlockSpec((rows, width), lambda i: (0, 0))
    scalar = pl.BlockSpec(memory_space=pltpu.SMEM)
    return pl.pallas_call(
        functools.partial(gram_body, scaled=scaled),
        grid=(width // 2 // GRAM_TILE,),
        in_specs=[scalar, full, full],
        out_specs=[pl.BlockSpec((GRAM_TILE, width), lambda i: (i, 0)), scalar],
        out_shape=[
            jax.ShapeDtypeStruct((width // 2, width), low),
            jax.ShapeDtypeStruct((1,), wide),
        ],
        scratch_shapes=[pltpu.SMEM((1,), wide)],
        compiler_params=pltpu.CompilerParams(vmem_limit_bytes=VMEM_BYTES),
        cost_estimate=QUICK,
    )(core, near, far)


def polynomial_body(core_ref, factor_ref, rows_ref, mine_ref, other_ref, out_ref, wide_ref, low_ref):
    width = rows_ref.shape[1]
    half = width // 2
    core = core_ref[0]
    factor = factor_ref[0]
    here = pl.ds(pl.multiple_of(core * half, half), half)
    there = pl.ds(pl.multiple_of((1 - core) * half, half), half)

    def times_gram(left_ref, part):
        result = jnp.dot(left_ref[:, here], mine_ref[:, part], preferred_element_type=wide)
        return result + jnp.dot(left_ref[:, there], other_ref[:, part], preferred_element_type=wide)

    tiles = [slice(start, start + COLUMN_TILE) for start in range(0, width, COLUMN_TILE)]
    for part in tiles:
        product = times_gram(rows_ref, part) * factor
        wide_ref[:, part] = product
        low_ref[:, part] = product.astype(low)
    for part in tiles:
        square = times_gram(low_ref, part)
        lead = (coef_one * factor) * rows_ref[:, part].astype(wide)
        out_ref[:, part] = (lead + coef_two * wide_ref[:, part] + coef_three * square).astype(low)


def polynomial(core, factor, rows, mine, other):
    count, width = rows.shape
    full = pl.BlockSpec((width // 2, width), lambda i: (0, 0))
    block = pl.BlockSpec((ROW_BLOCK, width), lambda i: (i, 0))
    scalar = pl.BlockSpec(memory_space=pltpu.SMEM)
    return pl.pallas_call(
        polynomial_body,
        grid=(count // ROW_BLOCK,),
        in_specs=[scalar, scalar, block, full, full],
        out_specs=block,
        out_shape=jax.ShapeDtypeStruct((count, width), low),
        scratch_shapes=[pltpu.VMEM((ROW_BLOCK, width), wide), pltpu.VMEM((ROW_BLOCK, width), low)],
        compiler_params=pltpu.CompilerParams(vmem_limit_bytes=VMEM_BYTES),
        cost_estimate=QUICK,
    )(core, factor, rows, mine, other)


def on_device(
    tokens,
    cotangent,
    bin_ids,
    level_table,
    table_moment,
    matrices,
    matrix_moment,
    modulation_bias,
    bias_moment,
):
    fabric = Fabric()
    planes, plane, seat = fabric.planes, fabric.plane, fabric.seat
    strips = lax.axis_size("strip")
    here, inner, width = tokens.shape
    shard_rows, units, _ = matrices.shape
    images = bin_ids.shape[0]
    table_rows = level_table.shape[0]
    blocks = (units - 10) // 2
    start_down = 4 + blocks
    start_ada = 4 + 2 * blocks
    slot_rows = planes * shard_rows
    valid = bin_ids[0] >= 0
    core = (fabric.me % 2).astype(jnp.int32).reshape(1)
    side = seat // 2 % 2
    peers = HD // shard_rows
    heads = planes // peers
    place = fabric.me % peers

    def flat(values):
        return values.reshape(here * inner, width)

    def whole(pair):
        return jnp.concatenate(pair, axis=0)

    def halves(rows):
        return [rows[: rows.shape[0] // 2], rows[rows.shape[0] // 2 :]]

    def parts(rows, weight):
        near, far = [dot("tj,jk->tk", piece, weight).astype(low) for piece in rows]
        return near, fabric.swap(far, CORE)

    def settled(pair):
        return fabric.settle(*pair).reshape(here, inner, width)

    def both(near):
        return [near, fabric.swap(near, CORE)]

    def over_tokens(left, right):
        return dot("tj,tk->jk", whole(left), whole(right)).astype(low)

    row_ids = fabric.me * table_rows + jnp.arange(table_rows, dtype=jnp.int32)
    selector = (bin_ids[:, None] == row_ids[None, :]).astype(wide)
    in_plane = images // planes
    ada_weight = matrices[:, start_ada:, :].astype(low)

    def modulated(modulation, which):
        return modulation[None, :, None, :, None, which]

    def open_rows(rows):
        return rows.reshape(1, 2, 2, here, inner, width).astype(wide)

    active_rows = jax.nn.silu(level_table).astype(low)
    active = jnp.dot(selector.astype(low), active_rows, preferred_element_type=wide)
    active = fabric.plane_total(active.astype(low))

    def gathered(first, last):
        rows = matrices[:, first:last].astype(low).transpose(1, 0, 2)
        rows = after(rows.reshape((last - first) * shard_rows, width), active)
        return fabric.gather_planes(rows)

    attention = gathered(0, 4)
    up_weight = gathered(4, start_down)
    down_weight = gathered(start_down, start_ada)

    def begin(active):
        active = fabric.team_total(active)
        rows, active = hold(flat(tokens), active)
        half = rows.shape[0] // 2
        first, second = rows[:half], rows[half:]
        mod_columns = dot("nk,ruk->nur", active, ada_weight) + modulation_bias[None]
        mod_parts = jnp.broadcast_to(
            mod_columns.reshape(planes, 1, in_plane, 6, shard_rows),
            (planes, TEAM, in_plane, 6, shard_rows),
        ).reshape(fabric.count, in_plane, 6, shard_rows)
        mod_parts = lax.all_to_all(mod_parts, WORLD, split_axis=0, concat_axis=0, tiled=True)
        first_x, second_y, mod_parts = hold(
            fabric.swap(first, ALONG_X), fabric.swap(second, ALONG_Y), mod_parts
        )
        modulation = mod_parts.transpose(1, 2, 0, 3).reshape(2, here, 6, width)
        modulation = jnp.where(seat // 4 == 0, modulation, modulation[::-1])
        first_y, second_x, first_xy, second_xy, modulation = hold(
            fabric.swap(first, ALONG_Y),
            fabric.swap(second, ALONG_X),
            fabric.swap(first_x, ALONG_Y),
            fabric.swap(second_y, ALONG_X),
            modulation,
        )
        near = jnp.concatenate(
            [rows, first_x, second_x, first_y, second_y, first_xy, second_xy], axis=0
        )
        first_in = modulate(near.reshape(2, 2, here, inner, width), modulation)
        return active, modulation, first_in.reshape(-1, width)

    active, modulation, first_in = fence(valid, begin, active)
    local = modulation[0][:, :, None, :]
    shift_one, scale_one, gate_one = local[:, 0], local[:, 1], local[:, 2]
    shift_two, scale_two, gate_two = local[:, 3], local[:, 4], local[:, 5]

    def mates(offset):
        return [
            (d, d // peers * peers + (d % peers + offset) % peers) for d in range(fabric.count)
        ]

    def attention_forward(attention, first_in):
        first_in = both(first_in)
        attention = attention.reshape(planes, 4, shard_rows, width)
        pieces = [lax.dynamic_slice_in_dim(attention, place * heads, heads, 0)]
        for offset in range(1, peers):
            target = (place + offset) % peers
            payload = lax.dynamic_slice_in_dim(attention, target * heads, heads, 0)
            pieces.append(lax.ppermute(payload, WORLD, mates(offset)))
        attention = jnp.stack(pieces).transpose(2, 1, 0, 3, 4).reshape(4, heads * HD, width)
        weight_in = attention[:3].reshape(3 * heads * HD, width)
        weight_out = attention[3]
        projected = whole([dot("tk,jk->tj", rows, weight_in).astype(low) for rows in first_in])
        upstream = fabric.share(flat(cotangent), (projected,))
        mixed = over_images(attend_body, here, inner, [projected], heads * HD)
        return weight_in, weight_out, first_in, projected, mixed, upstream

    weight_in, weight_out, first_in, projected, mixed, upstream = fence(
        valid, attention_forward, attention, first_in
    )

    moment = matrix_moment.transpose(1, 0, 2)

    def padded(batch, count):
        spare = count - batch.shape[0]
        if spare == 0:
            return batch
        return jnp.concatenate([batch, jnp.zeros((spare,) + batch.shape[1:], batch.dtype)], axis=0)

    def to_owner(batch, each):
        batch = padded(batch, planes * each)
        return fabric.trade_planes(batch.reshape(planes, each * shard_rows, width))

    def to_rows(batch, count):
        return fabric.trade_planes(batch).reshape(-1, shard_rows, width)[:count]

    def middle_forward(mixed, upstream):
        def gated():
            grad_mlp = open_rows(upstream) * modulated(modulation, 5)
            return grad_mlp.astype(low).reshape(-1, width)

        branch, grad_mlp = fabric.settle(*parts(halves(mixed), weight_out), gated)
        branch = branch.reshape(here, inner, width)
        middle = tokens.astype(wide) + gate_one * branch
        normed_two, inverse_two = normalize(middle)
        second_in = flat((normed_two * (1.0 + scale_two) + shift_two).astype(low))
        second_in = fabric.share(second_in)
        return (
            branch, middle, normed_two, inverse_two, both(upstream), both(grad_mlp), second_in,
        )

    (
        branch, middle, normed_two, inverse_two, upstream, grad_mlp, second_in,
    ) = fence(valid, middle_forward, mixed, upstream)

    second_in = both(after(second_in, down_weight))
    hidden, slope = [], []
    for rows in second_in:
        preact = dot("tk,jk->tj", rows, up_weight)
        cumulative = 0.5 * (1.0 + lax.erf(preact * 0.7071067811865476))
        density = jnp.exp(-0.5 * preact * preact) * 0.3989422804014327
        hidden.append((preact * cumulative).astype(low))
        slope.append(cumulative + preact * density)
    down_grad = over_tokens(hidden, grad_mlp)
    down_sum = fabric.reduce_planes(down_grad)
    grad_pre = [
        (dot("tk,jk->tj", after(grad_mlp[s], down_grad), down_weight) * slope[s]).astype(low)
        for s in (0, 1)
    ]
    grad_pre = list(lax.optimization_barrier(grad_pre))
    up_grad = over_tokens(grad_pre, second_in)
    up_sum = fabric.reduce_planes(up_grad)
    grad_total = cotangent.astype(wide)
    grad_in_parts = parts(
        [after(rows, up_grad) for rows in grad_pre], up_weight
    )

    def middle_back(grad_in_parts):
        def gate():
            sums = [
                gate_sums(hidden[s], down_weight, upstream[s].reshape(2, 2, here, inner, width))
                for s in (0, 1)
            ]
            return [part for part, _ in sums], sums[0][1] + sums[1][1]

        grad_in, (mlp_parts, grad_gate_two) = fabric.settle(*grad_in_parts, gate)
        grad_in = grad_in.reshape(here, inner, width)
        grad_gate_two = grad_gate_two[0] + fabric.swap(grad_gate_two[1], ALONG_Y)
        grad_gate_two += fabric.swap(grad_gate_two, ALONG_X)
        grad_gate_two += fabric.swap(grad_gate_two, CORE)
        grad_shift_two = jnp.sum(grad_in, axis=1)
        grad_scale_two = jnp.sum(grad_in * normed_two, axis=1)
        grad_middle = grad_total + norm_back(grad_in * (1.0 + scale_two), normed_two, inverse_two)
        grad_gate_one = jnp.sum(grad_middle * branch, axis=1)
        grad_branch = fabric.share(flat((grad_middle * gate_one).astype(low)))
        return (
            mlp_parts, grad_shift_two, grad_scale_two, grad_middle, grad_gate_one,
            grad_gate_two / strips, grad_branch,
        )

    (
        mlp_parts, grad_shift_two, grad_scale_two, grad_middle, grad_gate_one, grad_gate_two,
        grad_branch,
    ) = fence(valid, middle_back, grad_in_parts)

    ada_moment = to_owner(after(moment[start_ada:].astype(low), up_grad), 2)
    grad_branch, ada_moment = hold(grad_branch, ada_moment)

    def attention_back(grad_branch, down_sum):
        grad_branch = both(grad_branch)
        grad_mixed = whole([dot("tk,jk->tj", rows, weight_out).astype(low) for rows in grad_branch])
        grad_project = over_images(
            attend_back_body, here, inner, [projected, grad_mixed], 3 * heads * HD
        )
        return grad_branch, grad_project

    grad_branch, grad_project = fence(valid, attention_back, grad_branch, down_sum)

    def fresh(first, grad):
        grad = grad.astype(wide).reshape(-1, shard_rows, width)
        return matrix_decay * moment[first : first + grad.shape[0]] + grad

    def attention_grads(grad_branch, grad_project, up_sum):
        dense_momentum = jnp.concatenate([fresh(4, up_sum), fresh(start_down, down_sum)], axis=0)
        dense_rows = to_owner(dense_momentum.astype(low), 2)
        grad_first_parts = hold(*parts(halves(grad_project), weight_in))

        def weights():
            in_grad = over_tokens([grad_project], first_in).reshape(3, heads * HD, width)
            out_grad = over_tokens([mixed], grad_branch).reshape(1, heads * HD, width)
            attention_grad = jnp.concatenate([in_grad, out_grad], axis=0)
            attention_grad = attention_grad.reshape(4, heads, peers, shard_rows, width)
            return attention_grad.transpose(2, 1, 0, 3, 4)

        grad_first, attention_grad = fabric.settle(*grad_first_parts, weights)
        returned = [attention_grad[0]]
        for offset in range(1, peers):
            returned.append(lax.ppermute(attention_grad[offset], WORLD, mates(peers - offset)))
        attention_grad = jnp.concatenate(returned + returned[:-1], axis=0)
        attention_grad = lax.dynamic_slice_in_dim(
            attention_grad, (peers - place) % peers * heads, planes, 0
        )
        attention_grad = attention_grad.reshape(planes * 4 * shard_rows, width)
        return attention_grad, dense_momentum, dense_rows, grad_first

    attention_grad, dense_momentum, dense_rows, grad_first = fence(
        valid, attention_grads, grad_branch, grad_project, up_sum
    )
    attention_sum = fabric.reduce_planes(attention_grad)

    def two_of(rows):
        rows = rows.reshape(planes, 2, shard_rows, width)
        mine = lax.dynamic_index_in_dim(rows, side, 1, keepdims=False)
        other = lax.dynamic_index_in_dim(rows, 1 - side, 1, keepdims=False)
        return mine.reshape(slot_rows, width), other.reshape(slot_rows, width)

    def two_back(mine, other):
        mine = mine.reshape(planes, 1, shard_rows, width)
        other = other.reshape(planes, 1, shard_rows, width)
        both_sides = jnp.where(
            side == 0,
            jnp.concatenate([mine, other], axis=1),
            jnp.concatenate([other, mine], axis=1),
        )
        return both_sides.reshape(planes, 2 * shard_rows, width)

    def to_holders(stacked):
        held = lax.all_to_all(stacked, WORLD, split_axis=2, concat_axis=0, tiled=True)
        held = held.reshape(fabric.count // strips, strips, here, 6, shard_rows)
        return jnp.sum(held.astype(wide), axis=1).reshape(images, 6, shard_rows)

    def to_owners(stacked):
        spare = 2 * planes - 6
        stacked = jnp.concatenate(
            [stacked, jnp.zeros((here, spare, width), stacked.dtype)], axis=1
        ).reshape(here, planes, 2, planes, TEAM, shard_rows)
        stacked = stacked.transpose(1, 4, 0, 2, 3, 5)
        stacked = stacked.reshape(fabric.count, here, 2, planes, shard_rows)
        held = lax.all_to_all(stacked, WORLD, split_axis=0, concat_axis=0, tiled=True)
        held = held.reshape(fabric.count // strips, strips, here, 2, planes, shard_rows)
        return jnp.sum(held.astype(wide), axis=1).reshape(images, 2, planes, shard_rows)

    def enter(dense_rows, grad_first):
        normed_one, inverse_one = normalize(tokens.astype(wide))
        grad_first = grad_first.reshape(here, inner, width)
        grad_shift_one = jnp.sum(grad_first, axis=1)
        grad_scale_one = jnp.sum(grad_first * normed_one, axis=1)
        stacked = jnp.stack(
            [
                grad_shift_one,
                grad_scale_one,
                grad_gate_one,
                grad_shift_two,
                grad_scale_two,
                grad_gate_two,
            ],
            axis=1,
        ).astype(low)
        mine, other = two_of(dense_rows)
        mine, mine_x, mine_y, owned = hold(
            mine, fabric.swap(other, ALONG_X), fabric.swap(mine, ALONG_Y), to_owners(stacked)
        )
        ada = jnp.einsum("nuzr,nk->zurk", owned, active.astype(wide), precision=highest)
        ada += matrix_decay * ada_moment.astype(wide).reshape(ada.shape)
        ada_mine, ada_other = two_of(ada.astype(low))
        mine_xy, ada_mine, ada_other = hold(fabric.swap(mine_x, ALONG_Y), ada_mine, ada_other)
        near = jnp.concatenate([mine, mine_x, mine_y, mine_xy], axis=0)
        return near, ada_mine, ada_other, stacked

    dense_near, ada_mine, ada_other, stacked = fence(valid, enter, dense_rows, grad_first)

    d, d_far, ada_mine = hold(dense_near, fabric.swap(dense_near, CORE), ada_mine)
    a_x = fabric.swap(ada_other, ALONG_X)
    d_half, d_factor = half_gram(core, d, d_far, True)
    d, d_half, d_factor, a_x, attention_sum = hold(d, d_half, d_factor, a_x, attention_sum)
    attention_momentum = fresh(0, attention_sum)
    a_y = fabric.swap(ada_mine, ALONG_Y)
    t_rows = to_owner(attention_momentum.astype(low), 1)
    d, d_half, d_other = hold(d, d_half, fabric.swap(d_half, CORE))
    d = polynomial(core, d_factor, d, d_half, d_other)
    d, a_y, a_x = hold(d, a_y, a_x)
    a_xy = fabric.swap(a_x, ALONG_Y)
    d, d_far = hold(d, fabric.swap(d, CORE))
    d_half, one = half_gram(core, d, d_far, False)
    d, d_half, a_xy, t_rows = hold(d, d_half, a_xy, t_rows)
    a = jnp.concatenate([ada_mine, a_x, a_y, a_xy], axis=0)
    t_rows = t_rows.reshape(slot_rows, width)
    t_first, t_second = halves(t_rows)
    t_first_x, t_second_y = fabric.swap(t_first, ALONG_X), fabric.swap(t_second, ALONG_Y)
    a, a_far, d_other = hold(a, fabric.swap(a, CORE), fabric.swap(d_half, CORE))
    d_rows = polynomial(core, one, d[: 2 * slot_rows], d_half, d_other)
    d_rows, a, a_far, t_first_x, t_second_y = hold(d_rows, a, a_far, t_first_x, t_second_y)
    t_first_y, t_second_x = fabric.swap(t_first, ALONG_Y), fabric.swap(t_second, ALONG_X)
    t_first_xy, t_second_xy = fabric.swap(t_first_x, ALONG_Y), fabric.swap(t_second_y, ALONG_X)
    a_half, a_factor = half_gram(core, a, a_far, True)
    d_rows, a, a_half, a_factor, t_first_y, t_second_x, t_first_xy, t_second_xy = hold(
        d_rows, a, a_half, a_factor, t_first_y, t_second_x, t_first_xy, t_second_xy
    )
    t = jnp.concatenate(
        [t_rows, t_first_x, t_second_x, t_first_y, t_second_y, t_first_xy, t_second_xy], axis=0
    )
    d_x = fabric.swap(d_rows[slot_rows:], ALONG_X)
    a_half, a_other, t, t_far = hold(
        a_half, fabric.swap(a_half, CORE), t, fabric.swap(t, CORE)
    )
    t_half, t_factor = half_gram(core, t, t_far, True)
    a_half, a_other, t, t_half, d_x = hold(a_half, a_other, t, t_half, d_x)
    dense_ortho = fabric.trade_planes(two_back(d_rows[:slot_rows], d_x))
    t_other = fabric.swap(t_half, CORE)
    a = polynomial(core, a_factor, a, a_half, a_other)
    a, t, t_half, t_other = hold(a, t, t_half, t_other)
    a_far = fabric.swap(a, CORE)
    t = polynomial(core, t_factor, t, t_half, t_other)
    a, a_far, t = hold(a, a_far, t)
    t_far = fabric.swap(t, CORE)
    a_half, one = half_gram(core, a, a_far, False)
    a, a_half, t, t_far = hold(a, a_half, t, t_far)
    a_other = fabric.swap(a_half, CORE)
    t_half, one = half_gram(core, t, t_far, False)
    a, a_half, a_other, t, t_half, dense_ortho = hold(a, a_half, a_other, t, t_half, dense_ortho)
    t_other = fabric.swap(t_half, CORE)
    a_rows = polynomial(core, one, a[: 2 * slot_rows], a_half, a_other)
    a_rows, t, t_half, t_other = hold(a_rows, t, t_half, t_other)
    a_x = fabric.swap(a_rows[slot_rows:], ALONG_X)
    t_rows = polynomial(core, one, t[:slot_rows], t_half, t_other)
    a_rows, a_x, t_rows = hold(a_rows, a_x, t_rows)
    attention_ortho = fabric.trade_planes(t_rows.reshape(planes, shard_rows, width))
    ada_ortho = fabric.trade_planes(two_back(a_rows[:slot_rows], a_x))

    near, far = mlp_parts
    near, far, grad_first, stacked = after_all((near, far, grad_first, stacked), a)
    mlp_out = settled((near, fabric.swap(far, CORE)))
    block_out = (middle + gate_two * mlp_out).astype(low)
    normed_one, inverse_one = normalize(tokens.astype(wide))
    input_grad = grad_middle + norm_back(
        grad_first.reshape(here, inner, width) * (1.0 + scale_one), normed_one, inverse_one
    )
    input_grad = input_grad.astype(low)
    grad_mod_all = to_holders(stacked)
    grad_active = jnp.einsum(
        "nur,ruk->nk", grad_mod_all, ada_weight.astype(wide), precision=highest
    )
    grad_active = fabric.plane_total(fabric.team_total(grad_active))
    dense_ortho = dense_ortho.reshape(-1, shard_rows, width)[: 2 * blocks]
    ada_ortho = ada_ortho.reshape(-1, shard_rows, width)[:6]
    attention_ortho = attention_ortho.reshape(-1, shard_rows, width)[:4]

    active_wide = active.astype(wide)
    ada_grad = jnp.einsum("nur,nk->urk", grad_mod_all, active_wide, precision=highest)
    bias_grad = jnp.sum(grad_mod_all, axis=0)
    table_grad = jnp.dot(selector.T, grad_active, precision=highest) * silu_slope(level_table)
    momentum = jnp.concatenate(
        [
            attention_momentum,
            dense_momentum,
            matrix_decay * moment[start_ada:] + ada_grad,
        ],
        axis=0,
    ).transpose(1, 0, 2)
    ortho = jnp.concatenate([attention_ortho, dense_ortho, ada_ortho], axis=0).transpose(1, 0, 2)
    step_size = matrix_rate * 0.2 * math.sqrt(width)
    matrix_new = matrices - step_size * ortho.astype(wide)
    bias_momentum = vector_decay * bias_moment + bias_grad
    bias_new = modulation_bias - bias_rate * bias_momentum
    table_momentum = vector_decay * table_moment + table_grad
    table_new = level_table - table_rate * table_momentum
    return (
        block_out,
        input_grad,
        table_grad,
        table_momentum,
        table_new,
        momentum,
        matrix_new,
        bias_momentum,
        bias_new,
    )


def solution(mesh):
    whole = P(("img", "strip"), None, None)
    table = P(("img", "strip"), None)
    strip = P("img", "strip", None)
    bias = P(None, ("img", "strip"))
    return jax.shard_map(
        on_device,
        mesh=mesh,
        in_specs=(strip, strip, P(), table, table, whole, whole, bias, bias),
        out_specs=(strip, strip, table, table, table, whole, whole, bias, bias),
        check_vma=False,
    )
```

```python
import functools
import math

import jax
import jax.numpy as jnp
from jax import lax
from jax.experimental import pallas as pl
from jax.experimental.pallas import tpu as pltpu
from jax.sharding import PartitionSpec as P

HEADS = 16
HD = 128

highest = lax.Precision.HIGHEST
norm_eps = 1e-06
coef_one = 3.4445
coef_two = -4.775
coef_three = 2.0315
matrix_decay = 0.95
vector_decay = 0.9
matrix_rate = 0.5
bias_rate = 0.003
table_rate = 0.02

WORLD = ("img", "strip")
CORE, ALONG_X, ALONG_Y = 1, 2, 4
TEAM = 8
low = jnp.bfloat16
wide = jnp.float32


def dot(spec, left, right):
    return jnp.einsum(spec, left, right, preferred_element_type=wide)


def after(value, *earlier):
    return lax.optimization_barrier((value, *earlier))[0]


def after_all(values, *earlier):
    return lax.optimization_barrier((*values, *earlier))[: len(values)]


def hold(*values):
    return lax.optimization_barrier(values)


def fence(flag, body, *operands):
    shapes = jax.eval_shape(body, *operands)
    empty = lambda *_: jax.tree.map(lambda leaf: jnp.zeros(leaf.shape, leaf.dtype), shapes)
    return lax.cond(flag, body, empty, *operands)


def add(left, right):
    return left.astype(wide) + right.astype(wide)


def normalize(values):
    center = values - jnp.mean(values, axis=-1, keepdims=True)
    inverse = lax.rsqrt(jnp.mean(center * center, axis=-1, keepdims=True) + norm_eps)
    return (center * inverse, inverse)


def norm_back(grad_hat, normed, inverse):
    mean_grad = jnp.mean(grad_hat, axis=-1, keepdims=True)
    mean_cross = jnp.mean(grad_hat * normed, axis=-1, keepdims=True)
    return inverse * (grad_hat - mean_grad - normed * mean_cross)


def gelu_slope(values):
    cumulative = 0.5 * (1.0 + lax.erf(values * 0.7071067811865476))
    density = jnp.exp(-0.5 * values * values) * 0.3989422804014327
    return cumulative + values * density


def silu_slope(values):
    logistic = jax.nn.sigmoid(values)
    return logistic * (1.0 + values * (1.0 - logistic))


class Fabric:
    def __init__(self):
        self.count = lax.axis_size("img") * lax.axis_size("strip")
        self.planes = self.count // TEAM
        self.me = lax.axis_index(WORLD)
        self.plane = self.me // TEAM
        self.seat = self.me % TEAM
        self.lines = [
            [plane * TEAM + seat for plane in range(self.planes)] for seat in range(TEAM)
        ]

    def swap(self, value, bit):
        return lax.ppermute(value, WORLD, [(d, d ^ bit) for d in range(self.count)])

    def turn(self, value, offset):
        pairs = [(d, (d + offset * TEAM) % self.count) for d in range(self.count)]
        return lax.ppermute(value, WORLD, pairs)

    def gather_planes(self, shard):
        return lax.all_gather(shard, WORLD, axis=0, tiled=True, axis_index_groups=self.lines)

    def reduce_planes(self, parts):
        return lax.psum_scatter(
            parts, WORLD, scatter_dimension=0, tiled=True, axis_index_groups=self.lines
        )

    def trade_planes(self, blocks):
        return lax.all_to_all(
            blocks, WORLD, split_axis=0, concat_axis=0, tiled=True, axis_index_groups=self.lines
        )

    def pieces(self):
        distances = list(range(1, self.planes))
        return [distances[:1], distances[-1:], distances[1:-1]]

    def to_owners(self, blocks, group):
        return {
            distance: self.turn(
                lax.dynamic_index_in_dim(
                    blocks, (self.plane + distance) % self.planes, 0, keepdims=False
                ),
                distance,
            )
            for distance in self.pieces()[group]
        }

    def from_owners(self, slots, group):
        return {distance: self.turn(slots[distance], -distance) for distance in self.pieces()[group]}

    def slots_of(self, blocks):
        return [
            lax.dynamic_index_in_dim(blocks, (self.plane - j) % self.planes, 0, keepdims=False)
            for j in range(self.planes)
        ]

    def by_plane(self, own, came):
        came = {0: own, **came}
        result = jnp.zeros((self.planes,) + own.shape, own.dtype)
        for distance, block in came.items():
            result = lax.dynamic_update_index_in_dim(
                result, block, (self.plane + distance) % self.planes, 0
            )
        return result

    def team_total(self, value):
        for bit in (CORE, ALONG_X, ALONG_Y):
            value = value + self.swap(value, bit)
        return value

    def plane_total(self, value):
        others = [self.turn(value, offset) for offset in range(1, self.planes)]
        for other in others:
            value = value + other
        return value

    def share(self, rows, between=()):
        half = rows.shape[0] // 2
        first, second = rows[:half], rows[half:]
        first_x = self.swap(first, ALONG_X)
        second_y = self.swap(second, ALONG_Y)
        first_y = self.swap(first, ALONG_Y)
        second_x = self.swap(second, ALONG_X)
        first_xy = self.swap(after(first_x, *between), ALONG_Y)
        second_xy = self.swap(after(second_y, *between), ALONG_X)
        return jnp.concatenate(
            [rows, first_x, second_x, first_y, second_y, first_xy, second_xy], axis=0
        )

    def settle(self, near, near_too, beside=None):
        if beside is None:
            return self.settle_end(self.settle_begin(near, near_too))
        parts = self.settle_begin(near, near_too)
        *parts, done = hold(*parts, beside())
        return self.settle_end(parts), done

    def settle_begin(self, near, near_too):
        width = near.shape[-1]
        size = near.shape[0] // 8
        near = add(near, near_too).astype(low).reshape(2, 2, 2, size, width)
        first, second = near[:, :, 0], near[:, :, 1]
        first_x = self.swap(first[:, 1], ALONG_X)
        second_y = self.swap(second[1], ALONG_Y)
        return first[:, 0], second[0], first_x, second_y

    def settle_end(self, parts):
        first, second, first_x, second_y = parts
        first = add(first, first_x).astype(low)
        second = add(second, second_y).astype(low)
        first = add(first[0], self.swap(first[1], ALONG_Y))
        second = add(second[0], self.swap(second[1], ALONG_X))
        return jnp.concatenate([first, second], axis=0)


VMEM_BYTES = 60 * 2**20
QUICK = pl.CostEstimate(flops=1, bytes_accessed=1, transcendentals=0)


def attend_body(projected_ref, mixed_ref):
    size = mixed_ref.shape[-1]
    shape = mixed_ref.shape[:-1] + (HD,)
    tokens = math.prod(shape[:-1])
    for first in range(0, size, HD):

        def read(unit):
            block = projected_ref[..., unit * size + first : unit * size + first + HD]
            return block.reshape(tokens, HD)

        scores = lax.dot_general(
            read(0), read(1), (((1,), (1,)), ((), ())), preferred_element_type=wide
        ) * HD ** (-0.5)
        exponent = jnp.exp(scores - jnp.max(scores, axis=-1, keepdims=True))
        probs = (exponent / jnp.sum(exponent, axis=-1, keepdims=True)).astype(low)
        mixed = jnp.dot(probs, read(2), preferred_element_type=wide).astype(low)
        mixed_ref[..., first : first + HD] = mixed.reshape(shape)


def attend_back_body(projected_ref, grad_ref, out_ref):
    size = grad_ref.shape[-1]
    shape = grad_ref.shape[:-1] + (HD,)
    tokens = math.prod(shape[:-1])
    factor = HD ** (-0.5)
    across = (((1,), (1,)), ((), ()))
    down = (((0,), (0,)), ((), ()))
    for first in range(0, size, HD):

        def read(unit):
            block = projected_ref[..., unit * size + first : unit * size + first + HD]
            return block.reshape(tokens, HD)

        def write(unit, value):
            part = slice(unit * size + first, unit * size + first + HD)
            out_ref[..., part] = value.astype(low).reshape(shape)

        query, keys_all, values_all = read(0), read(1), read(2)
        grad_heads = grad_ref[..., first : first + HD].reshape(tokens, HD)
        scores = lax.dot_general(query, keys_all, across, preferred_element_type=wide) * factor
        exponent = jnp.exp(scores - jnp.max(scores, axis=-1, keepdims=True))
        probs = exponent / jnp.sum(exponent, axis=-1, keepdims=True)
        grad_probs = lax.dot_general(grad_heads, values_all, across, preferred_element_type=wide)
        cross = jnp.sum(probs * grad_probs, axis=-1, keepdims=True)
        grad_scores = (probs * (grad_probs - cross)).astype(low)
        write(0, jnp.dot(grad_scores, keys_all, preferred_element_type=wide) * factor)
        write(1, lax.dot_general(grad_scores, query, down, preferred_element_type=wide) * factor)
        write(2, lax.dot_general(probs.astype(low), grad_heads, down, preferred_element_type=wide))


def over_images(body, here, inner, arrays, out_features):
    def block(features):
        return pl.BlockSpec(
            (2, 1, 2, 1, inner, features), lambda side, image: (0, side, 0, image, 0, 0)
        )

    arrays = [rows.reshape(2, 2, 2, here, inner, rows.shape[-1]) for rows in arrays]
    result = pl.pallas_call(
        body,
        grid=(2, here),
        in_specs=[block(rows.shape[-1]) for rows in arrays],
        out_specs=block(out_features),
        out_shape=jax.ShapeDtypeStruct((2, 2, 2, here, inner, out_features), low),
        compiler_params=pltpu.CompilerParams(vmem_limit_bytes=32 * 2**20),
        cost_estimate=QUICK,
    )(*arrays)
    return result.reshape(-1, out_features)


def modulate_body(rows_ref, modulation_ref, out_ref):
    values = rows_ref[0, 0].astype(wide)
    center = values - jnp.mean(values, axis=-1, keepdims=True)
    inverse = lax.rsqrt(jnp.mean(center * center, axis=-1, keepdims=True) + norm_eps)
    shift = modulation_ref[0, :, 0:1, :]
    scale = modulation_ref[0, :, 1:2, :]
    out_ref[0, 0] = (center * inverse * (1.0 + scale) + shift).astype(low)


def modulate(rows, modulation):
    sides, seats, here, inner, width = rows.shape
    block = pl.BlockSpec((1, 1, here, inner, width), lambda y, x: (y, x, 0, 0, 0))
    return pl.pallas_call(
        modulate_body,
        grid=(sides, seats),
        in_specs=[
            block,
            pl.BlockSpec((1, here) + modulation.shape[2:], lambda y, x: (y, 0, 0, 0)),
        ],
        out_specs=block,
        out_shape=jax.ShapeDtypeStruct(rows.shape, low),
        compiler_params=pltpu.CompilerParams(vmem_limit_bytes=48 * 2**20),
        cost_estimate=QUICK,
    )(rows, modulation)


def gate_body(hidden_ref, weight_ref, upstream_ref, part_ref, cross_ref):
    part = jnp.dot(hidden_ref[...], weight_ref[...], preferred_element_type=wide)
    part_ref[...] = part.astype(low)
    here, inner, width = upstream_ref.shape[2:]
    cross = upstream_ref[0, 0].astype(wide) * part.reshape(here, inner, width)
    cross = jnp.sum(cross, axis=1)[None]

    @pl.when(pl.program_id(1) == 0)
    def _():
        cross_ref[...] = cross

    @pl.when(pl.program_id(1) > 0)
    def _():
        cross_ref[...] += cross


def gate_sums(hidden, weight, upstream):
    sides, seats, here, inner, width = upstream.shape
    size = here * inner
    return pl.pallas_call(
        gate_body,
        grid=(sides, seats),
        in_specs=[
            pl.BlockSpec((size, hidden.shape[1]), lambda y, x: (y * seats + x, 0)),
            pl.BlockSpec(weight.shape, lambda y, x: (0, 0)),
            pl.BlockSpec((1, 1, here, inner, width), lambda y, x: (y, x, 0, 0, 0)),
        ],
        out_specs=[
            pl.BlockSpec((size, width), lambda y, x: (y * seats + x, 0)),
            pl.BlockSpec((1, here, width), lambda y, x: (y, 0, 0)),
        ],
        out_shape=[
            jax.ShapeDtypeStruct((hidden.shape[0], width), low),
            jax.ShapeDtypeStruct((sides, here, width), wide),
        ],
        compiler_params=pltpu.CompilerParams(vmem_limit_bytes=VMEM_BYTES),
        cost_estimate=QUICK,
    )(hidden, weight, upstream)


def norm_sums_body(grad_ref, weight_ref, rows_ref, part_ref, sums_ref):
    part = jnp.dot(grad_ref[...], weight_ref[...], preferred_element_type=wide)
    part_ref[...] = part.astype(low)
    here, inner, width = rows_ref.shape[2:]
    part = part.reshape(here, inner, width)
    values = rows_ref[0, 0].astype(wide)
    center = values - jnp.mean(values, axis=-1, keepdims=True)
    inverse = lax.rsqrt(jnp.mean(center * center, axis=-1, keepdims=True) + norm_eps)
    shift = jnp.sum(part, axis=1)[None, None]
    scale = jnp.sum(part * (center * inverse), axis=1)[None, None]

    @pl.when(pl.program_id(1) == 0)
    def _():
        sums_ref[0:1] = shift
        sums_ref[1:2] = scale

    @pl.when(pl.program_id(1) > 0)
    def _():
        sums_ref[0:1] += shift
        sums_ref[1:2] += scale


def norm_sums(grads, weight, rows):
    sides, seats, here, inner, width = rows.shape
    size = here * inner
    return pl.pallas_call(
        norm_sums_body,
        grid=(sides, seats),
        in_specs=[
            pl.BlockSpec((size, grads.shape[1]), lambda y, x: (y * seats + x, 0)),
            pl.BlockSpec(weight.shape, lambda y, x: (0, 0)),
            pl.BlockSpec((1, 1, here, inner, width), lambda y, x: (y, x, 0, 0, 0)),
        ],
        out_specs=[
            pl.BlockSpec((size, width), lambda y, x: (y * seats + x, 0)),
            pl.BlockSpec((2, 1, here, width), lambda y, x: (0, y, 0, 0)),
        ],
        out_shape=[
            jax.ShapeDtypeStruct((grads.shape[0], width), low),
            jax.ShapeDtypeStruct((2, sides, here, width), wide),
        ],
        compiler_params=pltpu.CompilerParams(vmem_limit_bytes=VMEM_BYTES),
        cost_estimate=QUICK,
    )(grads, weight, rows)


CHUNK = 512
ROW_BLOCK = 256


def gram_body(core_ref, *refs, near_count, far_count):
    pieces = refs[: near_count + far_count]
    out_ref, near_ref, x_ref, sem, near_sem = refs[near_count + far_count :]
    width = x_ref.shape[1]
    half = width // 2
    tile = out_ref.shape[0]
    step = pl.program_id(0)
    start = core_ref[0] * half

    def column(j):
        return pl.multiple_of((start + j * CHUNK) % width, CHUNK)

    def copies(j):
        part = pl.ds(column(j), CHUNK)
        result, row = [], 0
        for k, piece in enumerate(pieces):
            rows = pl.ds(row, piece.shape[0])
            result.append(
                pltpu.make_async_copy(piece.at[:, part], x_ref.at[rows, part], sem.at[j, k])
            )
            row += piece.shape[0]
        return result

    joined = pltpu.make_async_copy(x_ref.at[pl.ds(0, near_ref.shape[0])], near_ref, near_sem)

    @pl.when(step == 0)
    def _():
        for j in range(width // CHUNK):
            for copy in copies(j):
                copy.start()

    left = pl.ds(pl.multiple_of(start + step * tile, tile), tile)
    for j in range(width // CHUNK):

        @pl.when(step == 0)
        def _():
            for copy in copies(j):
                copy.wait()
            if j == width // CHUNK - 1 and near_count > 1:
                joined.start()

        part = pl.ds(column(j), CHUNK)
        total = lax.dot_general(
            x_ref[:, left], x_ref[:, part], (((0,), (0,)), ((), ())), preferred_element_type=wide
        )
        out_ref[:, part] = total.astype(low)

    if near_count > 1:

        @pl.when(step == pl.num_programs(0) - 1)
        def _():
            joined.wait()


def half_gram(core, near, far):
    width = near[0].shape[1]
    near_rows = sum(piece.shape[0] for piece in near)
    far_rows = sum(piece.shape[0] for piece in far)
    anywhere = pl.BlockSpec(memory_space=pl.ANY)
    kept = near_rows if len(near) > 1 else 16
    half, joined = pl.pallas_call(
        functools.partial(gram_body, near_count=len(near), far_count=len(far)),
        grid=(width // 2 // CHUNK,),
        in_specs=[pl.BlockSpec(memory_space=pltpu.SMEM)] + [anywhere] * (len(near) + len(far)),
        out_specs=[pl.BlockSpec((CHUNK, width), lambda i: (i, 0)), anywhere],
        out_shape=[
            jax.ShapeDtypeStruct((width // 2, width), low),
            jax.ShapeDtypeStruct((kept, width), low),
        ],
        scratch_shapes=[
            pltpu.VMEM((near_rows + far_rows, width), low),
            pltpu.SemaphoreType.DMA((width // CHUNK, len(near) + len(far))),
            pltpu.SemaphoreType.DMA,
        ],
        compiler_params=pltpu.CompilerParams(vmem_limit_bytes=VMEM_BYTES),
        cost_estimate=QUICK,
    )(core, *near, *far)
    return half, joined if len(near) > 1 else near[0]


def polynomial_body(core_ref, rows_ref, mine_ref, other_ref, *refs, scaled):
    *outs, gram_ref, wide_ref, low_ref, factor_ref, sem = refs
    width = rows_ref.shape[1]
    half = width // 2
    first = pl.program_id(0) == 0
    core = core_ref[0]
    places = [pl.multiple_of(core * half, half), pl.multiple_of((1 - core) * half, half)]

    def copies(j):
        part = pl.ds(j * CHUNK, CHUNK)
        return [
            pltpu.make_async_copy(
                source.at[:, part], gram_ref.at[pl.ds(places[k], half), part], sem.at[j, k]
            )
            for k, source in enumerate((mine_ref, other_ref))
        ]

    @pl.when(first)
    def _():
        for j in range(width // CHUNK):
            for copy in copies(j):
                copy.start()

    tiles = [slice(start, start + CHUNK) for start in range(0, width, CHUNK)]
    for j, part in enumerate(tiles):

        @pl.when(first)
        def _():
            for copy in copies(j):
                copy.wait()

        wide_ref[:, part] = jnp.dot(
            rows_ref[...], gram_ref[:, part], preferred_element_type=wide
        )
        if not scaled:
            low_ref[:, part] = wide_ref[:, part].astype(low)

    if scaled:

        @pl.when(first)
        def _():
            trace = jnp.float32(0.0)
            size = 256
            row = lax.broadcasted_iota(jnp.int32, (size, size), 0)
            column = lax.broadcasted_iota(jnp.int32, (size, size), 1)
            for start in range(0, width, size):
                block = gram_ref[start : start + size, start : start + size].astype(wide)
                trace += jnp.sum(jnp.where(row == column, block, 0.0))
            factor_ref[0] = 1.0 / (jnp.sqrt(trace) + 1e-07)

        factor = factor_ref[0]
        cube, squared = factor * factor * factor, factor * factor
        for part in tiles:
            product = wide_ref[:, part] * cube
            wide_ref[:, part] = product
            low_ref[:, part] = product.astype(low)
    else:
        factor = squared = jnp.float32(1.0)
    for part in tiles:
        square = jnp.dot(low_ref[...], gram_ref[:, part], preferred_element_type=wide) * squared
        lead = (coef_one * factor) * rows_ref[:, part].astype(wide)
        result = (lead + coef_two * wide_ref[:, part] + coef_three * square).astype(low)
        if len(outs) == 1:
            outs[0][:, part] = result
        else:
            for k, out_ref in enumerate(outs):

                @pl.when(pl.program_id(0) == k)
                def _():
                    out_ref[:, part] = result


def polynomial(core, rows, mine, other, scaled, blocks=None):
    count, width = rows.shape
    if blocks is not None:
        count = blocks * ROW_BLOCK
    anywhere = pl.BlockSpec(memory_space=pl.ANY)
    block = pl.BlockSpec((ROW_BLOCK, width), lambda i: (i, 0))
    if blocks is None:
        out_specs, out_shape = block, jax.ShapeDtypeStruct((count, width), low)
    else:
        out_specs = [pl.BlockSpec((ROW_BLOCK, width), lambda i: (0, 0))] * blocks
        out_shape = [jax.ShapeDtypeStruct((ROW_BLOCK, width), low)] * blocks
    return pl.pallas_call(
        functools.partial(polynomial_body, scaled=scaled),
        grid=(count // ROW_BLOCK,),
        in_specs=[pl.BlockSpec(memory_space=pltpu.SMEM), block, anywhere, anywhere],
        out_specs=out_specs,
        out_shape=out_shape,
        scratch_shapes=[
            pltpu.VMEM((width, width), low),
            pltpu.VMEM((ROW_BLOCK, width), wide),
            pltpu.VMEM((ROW_BLOCK, width), low),
            pltpu.SMEM((1,), wide),
            pltpu.SemaphoreType.DMA((width // CHUNK, 2)),
        ],
        compiler_params=pltpu.CompilerParams(vmem_limit_bytes=VMEM_BYTES),
        cost_estimate=QUICK,
    )(core, rows, mine, other)


def on_device(
    tokens,
    cotangent,
    bin_ids,
    level_table,
    table_moment,
    matrices,
    matrix_moment,
    modulation_bias,
    bias_moment,
):
    fabric = Fabric()
    planes, plane, seat = fabric.planes, fabric.plane, fabric.seat
    strips = lax.axis_size("strip")
    here, inner, width = tokens.shape
    shard_rows, units, _ = matrices.shape
    images = bin_ids.shape[0]
    table_rows = level_table.shape[0]
    blocks = (units - 10) // 2
    start_down = 4 + blocks
    start_ada = 4 + 2 * blocks
    slot_rows = planes * shard_rows
    valid = bin_ids[0] >= 0
    core = (fabric.me % 2).astype(jnp.int32).reshape(1)
    side = seat // 2 % 2
    peers = HD // shard_rows
    heads = planes // peers
    place = fabric.me % peers

    def flat(values):
        return values.reshape(here * inner, width)

    def whole(pair):
        return jnp.concatenate(pair, axis=0)

    def halves(rows):
        return [rows[: rows.shape[0] // 2], rows[rows.shape[0] // 2 :]]

    def parts(rows, weight):
        near, far = [dot("tj,jk->tk", piece, weight).astype(low) for piece in rows]
        return near, fabric.swap(far, CORE)

    def settled(pair):
        return fabric.settle(*pair).reshape(here, inner, width)

    def both(near):
        return [near, fabric.swap(near, CORE)]

    def over_tokens(left, right):
        return dot("tj,tk->jk", whole(left), whole(right)).astype(low)

    row_ids = fabric.me * table_rows + jnp.arange(table_rows, dtype=jnp.int32)
    selector = (bin_ids[:, None] == row_ids[None, :]).astype(wide)
    in_plane = images // planes
    ada_weight = matrices[:, start_ada:, :].astype(low)

    def modulated(modulation, which):
        return modulation[None, :, None, :, None, which]

    def open_rows(rows):
        return rows.reshape(1, 2, 2, here, inner, width).astype(wide)

    active_rows = jax.nn.silu(level_table).astype(low)
    active = jnp.dot(selector.astype(low), active_rows, preferred_element_type=wide)
    active = fabric.plane_total(active.astype(low))

    def gathered(first, last):
        rows = matrices[:, first:last].astype(low).transpose(1, 0, 2)
        rows = after(rows.reshape((last - first) * shard_rows, width), active)
        return fabric.gather_planes(rows)

    attention = gathered(0, 4)
    up_weight = gathered(4, start_down)
    down_weight = gathered(start_down, start_ada)

    def begin(active):
        active = fabric.team_total(active)
        rows, active = hold(flat(tokens), active)
        half = rows.shape[0] // 2
        first, second = rows[:half], rows[half:]
        mod_columns = dot("nk,ruk->nur", active, ada_weight) + modulation_bias[None]
        mod_parts = jnp.broadcast_to(
            mod_columns.reshape(planes, 1, in_plane, 6, shard_rows),
            (planes, TEAM, in_plane, 6, shard_rows),
        ).reshape(fabric.count, in_plane, 6, shard_rows)
        mod_parts = lax.all_to_all(mod_parts, WORLD, split_axis=0, concat_axis=0, tiled=True)
        first_x, second_y, mod_parts = hold(
            fabric.swap(first, ALONG_X), fabric.swap(second, ALONG_Y), mod_parts
        )
        modulation = mod_parts.transpose(1, 2, 0, 3).reshape(2, here, 6, width)
        modulation = jnp.where(seat // 4 == 0, modulation, modulation[::-1])
        first_y, second_x, first_xy, second_xy, modulation = hold(
            fabric.swap(first, ALONG_Y),
            fabric.swap(second, ALONG_X),
            fabric.swap(first_x, ALONG_Y),
            fabric.swap(second_y, ALONG_X),
            modulation,
        )
        near = jnp.concatenate(
            [rows, first_x, second_x, first_y, second_y, first_xy, second_xy], axis=0
        )
        first_in = modulate(near.reshape(2, 2, here, inner, width), modulation)
        return active, modulation, both(first_in.reshape(-1, width)), near

    active, modulation, first_in, tokens_near = fence(valid, begin, active)
    local = modulation[0][:, :, None, :]
    shift_one, scale_one, gate_one = local[:, 0], local[:, 1], local[:, 2]
    shift_two, scale_two, gate_two = local[:, 3], local[:, 4], local[:, 5]

    def mates(offset):
        return [
            (d, d // peers * peers + (d % peers + offset) % peers) for d in range(fabric.count)
        ]

    def attention_forward(attention):
        attention = attention.reshape(planes, 4, shard_rows, width)
        pieces = [lax.dynamic_slice_in_dim(attention, place * heads, heads, 0)]
        for offset in range(1, peers):
            target = (place + offset) % peers
            payload = lax.dynamic_slice_in_dim(attention, target * heads, heads, 0)
            pieces.append(lax.ppermute(payload, WORLD, mates(offset)))
        attention = jnp.stack(pieces).transpose(2, 1, 0, 3, 4).reshape(4, heads * HD, width)
        weight_in = attention[:3].reshape(3 * heads * HD, width)
        weight_out = attention[3]
        projected = whole([dot("tk,jk->tj", rows, weight_in).astype(low) for rows in first_in])
        upstream = fabric.share(after(flat(cotangent), weight_in), (projected,))
        mixed = over_images(attend_body, here, inner, [projected], heads * HD)
        return weight_in, weight_out, projected, mixed, upstream

    weight_in, weight_out, projected, mixed, upstream = fence(valid, attention_forward, attention)

    moment = matrix_moment.transpose(1, 0, 2)

    def padded(batch, count):
        spare = count - batch.shape[0]
        if spare == 0:
            return batch
        return jnp.concatenate([batch, jnp.zeros((spare,) + batch.shape[1:], batch.dtype)], axis=0)

    def to_owner(batch, each):
        batch = padded(batch, planes * each)
        return fabric.trade_planes(batch.reshape(planes, each * shard_rows, width))

    def to_rows(batch, count):
        return fabric.trade_planes(batch).reshape(-1, shard_rows, width)[:count]

    ada_moment = to_owner(after(moment[start_ada:], mixed).astype(low), 2)

    def middle_forward(mixed, upstream):
        def gated():
            grad_mlp = open_rows(upstream) * modulated(modulation, 5)
            return grad_mlp.astype(low).reshape(-1, width)

        branch, grad_mlp = fabric.settle(*parts(halves(mixed), weight_out), gated)
        branch = branch.reshape(here, inner, width)
        middle = tokens.astype(wide) + gate_one * branch
        normed_two, inverse_two = normalize(middle)
        second_in = flat((normed_two * (1.0 + scale_two) + shift_two).astype(low))
        second_in = fabric.share(second_in)
        return (
            branch, middle, normed_two, inverse_two, both(upstream), both(grad_mlp), second_in,
        )

    (
        branch, middle, normed_two, inverse_two, upstream, grad_mlp, second_in,
    ) = fence(valid, middle_forward, mixed, upstream)
    second_in, ada_moment = hold(second_in, ada_moment)

    second_in = both(second_in)
    hidden, slope = [], []
    for rows in second_in:
        preact = dot("tk,jk->tj", rows, up_weight)
        cumulative = 0.5 * (1.0 + lax.erf(preact * 0.7071067811865476))
        density = jnp.exp(-0.5 * preact * preact) * 0.3989422804014327
        hidden.append((preact * cumulative).astype(low))
        slope.append(cumulative + preact * density)
    *hidden, down_weight = hold(*hidden, down_weight)
    down_grad = over_tokens(hidden, grad_mlp)
    grad_total = cotangent.astype(wide)

    *grad_mlp, down_grad = hold(*grad_mlp, down_grad)

    down_sum = fabric.reduce_planes(down_grad)

    def turn_back(grad_mlp):
        grad_pre = [
            (dot("tk,jk->tj", grad_mlp[s], down_weight) * slope[s]).astype(low) for s in (0, 1)
        ]
        grad_pre = hold(*grad_pre)

        near, near_too = hold(*parts(grad_pre, up_weight))
        grad_in = fabric.settle_begin(near, near_too)
        return hold(*grad_in, over_tokens(grad_pre, second_in))

    *grad_in, up_grad = fence(valid, turn_back, grad_mlp)
    up_sum = fabric.reduce_planes(up_grad)

    def middle_back(grad_in):
        grad_in = fabric.settle_end(grad_in).reshape(here, inner, width)
        grad_shift_two = jnp.sum(grad_in, axis=1)
        grad_scale_two = jnp.sum(grad_in * normed_two, axis=1)
        grad_middle = grad_total + norm_back(grad_in * (1.0 + scale_two), normed_two, inverse_two)
        grad_gate_one = jnp.sum(grad_middle * branch, axis=1)
        grad_branch = flat((grad_middle * gate_one).astype(low))
        *ready, grad_branch = hold(*hidden, grad_branch)
        seats = [rows.reshape(2, 2, here, inner, width) for rows in upstream]
        mlp_far, far_gate = gate_sums(ready[1], down_weight, seats[1])
        grad_branch = fabric.share(grad_branch, (mlp_far,))
        mlp_near, near_gate = gate_sums(after(ready[0], mlp_far), down_weight, seats[0])
        grad_branch, mlp_near, mlp_too = hold(grad_branch, mlp_near, fabric.swap(mlp_far, CORE))
        grad_gate_two = far_gate + near_gate
        return (
            grad_shift_two, grad_scale_two, grad_middle, grad_gate_one, grad_gate_two, grad_branch,
            mlp_near, mlp_too,
        )

    *grad_in, down_sum = hold(*grad_in, down_sum)
    (
        grad_shift_two, grad_scale_two, grad_middle, grad_gate_one, grad_gate_two, grad_branch,
        mlp_near, mlp_too,
    ) = fence(valid, middle_back, grad_in)

    def fresh(first, grad):
        grad = grad.astype(wide).reshape(-1, shard_rows, width)
        return matrix_decay * moment[first : first + grad.shape[0]] + grad

    up_sum, down_sum, grad_branch = hold(up_sum, down_sum, grad_branch)
    dense_momentum = jnp.concatenate([fresh(4, up_sum), fresh(start_down, down_sum)], axis=0)
    dense_rows, grad_branch = hold(dense_momentum.astype(low), grad_branch)
    dense_rows = to_owner(dense_rows, 2)

    def attention_back(grad_branch, mlp_near, mlp_too):
        grad_branch = both(grad_branch)
        mlp_sums = fabric.settle_begin(mlp_near, mlp_too)
        grad_mixed = whole([dot("tk,jk->tj", rows, weight_out).astype(low) for rows in grad_branch])
        grad_project = over_images(
            attend_back_body, here, inner, [projected, grad_mixed], 3 * heads * HD
        )
        grad_project, *mlp_sums = hold(grad_project, *mlp_sums)
        mlp_out = fabric.settle_end(mlp_sums)
        in_grad = over_tokens([grad_project], first_in).reshape(3, heads * HD, width)
        out_grad = over_tokens([mixed], grad_branch).reshape(1, heads * HD, width)
        attention_grad = jnp.concatenate([in_grad, out_grad], axis=0)
        attention_grad = attention_grad.reshape(4, heads, peers, shard_rows, width)
        attention_grad = attention_grad.transpose(2, 1, 0, 3, 4)
        returned = [attention_grad[0]]
        for offset in range(1, peers):
            returned.append(lax.ppermute(attention_grad[offset], WORLD, mates(peers - offset)))
        attention_grad = jnp.concatenate(returned + returned[:-1], axis=0)
        attention_grad = lax.dynamic_slice_in_dim(
            attention_grad, (peers - place) % peers * heads, planes, 0
        )
        return grad_project, attention_grad.reshape(planes * 4 * shard_rows, width), mlp_out

    grad_project, attention_grad, mlp_out = fence(
        valid, attention_back, grad_branch, mlp_near, mlp_too
    )
    mlp_out = mlp_out.reshape(here, inner, width)
    attention_grad, dense_rows = hold(attention_grad, dense_rows)
    attention_sum = fabric.reduce_planes(attention_grad)

    def two_of(rows):
        rows = rows.reshape(planes, 2, shard_rows, width)
        mine = lax.dynamic_index_in_dim(rows, side, 1, keepdims=False)
        other = lax.dynamic_index_in_dim(rows, 1 - side, 1, keepdims=False)
        return mine.reshape(slot_rows, width), other.reshape(slot_rows, width)

    def joined(mine, other):
        mine = mine.reshape(planes, 1, shard_rows, width)
        other = other.reshape(planes, 1, shard_rows, width)
        return fabric.slots_of(jnp.concatenate([mine, other], axis=1))

    def two_units(own, came):
        rows = fabric.by_plane(own, came)
        rows = jnp.where(side == 0, rows, rows[:, ::-1])
        return rows.reshape(2 * planes, shard_rows, width)

    def to_owners(stacked):
        spare = 2 * planes - 6
        stacked = jnp.concatenate(
            [stacked, jnp.zeros((2 * here, spare, width), stacked.dtype)], axis=1
        ).reshape(2 * here, planes, 2, planes, TEAM, shard_rows)
        stacked = stacked.transpose(1, 4, 0, 2, 3, 5)
        stacked = stacked.reshape(fabric.count, 2 * here, 2, planes, shard_rows)
        held = lax.all_to_all(stacked, WORLD, split_axis=0, concat_axis=0, tiled=True)
        held = held.reshape(planes, TEAM, 2 * here, 2, planes, shard_rows)
        return jnp.sum(held.astype(wide), axis=1).reshape(images, 2, planes, shard_rows)

    def enter(grad_project, dense_rows):
        d, d_other = two_of(dense_rows)
        grads = halves(grad_project)
        seats = [rows.reshape(2, 2, here, inner, width) for rows in both(tokens_near)]
        d, d_x, d_y, near, far = hold(
            d,
            fabric.swap(d_other, ALONG_X),
            fabric.swap(d, ALONG_Y),
            norm_sums(grads[0], weight_in, seats[0]),
            norm_sums(grads[1], weight_in, seats[1]),
        )
        sums = near[1] + far[1]
        own = jnp.stack([grad_gate_one, grad_shift_two, grad_scale_two], axis=0)
        own = jnp.stack([own, jnp.zeros_like(own)], axis=1)
        stacked = jnp.concatenate([sums, own, grad_gate_two[None]], axis=0)
        stacked = jnp.where(seat // 4 == 0, stacked, stacked[:, ::-1])
        stacked = stacked.reshape(6, 2 * here, width).transpose(1, 0, 2).astype(low)
        owned = to_owners(stacked)
        d_near = [d, d_x, d_y]
        d_far = [fabric.swap(piece, CORE) for piece in d_near]
        d_xy = fabric.swap(d_x, ALONG_Y)
        d_xy, owned, *d_far = hold(d_xy, owned, *d_far)
        d_far_xy = fabric.swap(d_xy, CORE)
        ada = jnp.einsum("nuzr,nk->zurk", owned, active.astype(wide), precision=highest)
        ada += matrix_decay * ada_moment.astype(wide).reshape(ada.shape)
        a, a_other = two_of(ada.astype(low))
        d_far_xy, a, a_other = hold(d_far_xy, a, a_other)
        block_out = (middle + gate_two * mlp_out).astype(low)
        return near[0], far[0], owned, d_near + [d_xy], d_far + [d_far_xy], a, a_other, block_out

    first_near, first_far, owned, d, d_far, a, a_other, block_out = fence(
        valid, enter, grad_project, dense_rows
    )

    def steps_one(d, d_far, a, a_other, owned):
        a_x, a_y = fabric.swap(a_other, ALONG_X), fabric.swap(a, ALONG_Y)
        grad_mod_all = fabric.trade_planes(owned.transpose(2, 0, 1, 3))
        d_half, d = half_gram(core, d, d_far)
        a_far = fabric.swap(a, CORE)
        d, d_half, grad_mod_all = hold(d, d_half, grad_mod_all)
        grad_mod_all = grad_mod_all.transpose(1, 0, 2, 3)
        grad_mod_all = grad_mod_all.reshape(images, 2 * planes, shard_rows)[:, :6]
        grad_active = jnp.einsum(
            "nur,ruk->nk", grad_mod_all, ada_weight.astype(wide), precision=highest
        )
        d_half, d_other, a_far, grad_active = hold(
            d_half, fabric.swap(d_half, CORE), a_far, grad_active
        )
        d = polynomial(core, d, d_half, d_other, True)
        grad_active += fabric.swap(grad_active, CORE)
        return hold(d, a_x, a_y, a_far, grad_mod_all, grad_active)

    d, a_x, a_y, a_far, grad_mod_all, grad_active = fence(
        valid, steps_one, d, d_far, a, a_other, owned
    )
    d, a_x, a_y, attention_sum = hold(d, a_x, a_y, attention_sum)
    attention_momentum = fresh(0, attention_sum)

    def steps_two(
        d, a, a_x, a_y, a_far, attention_momentum, first_near, first_far, grad_active
    ):
        t_own = padded(attention_momentum.astype(low), planes)
        a_xy = fabric.swap(a_x, ALONG_Y)
        a_far = [a_far, fabric.swap(a_x, CORE), fabric.swap(a_y, CORE)]
        d, d_far, t_own = hold(d, fabric.swap(d, CORE), t_own)
        t_slots = {0: lax.dynamic_index_in_dim(t_own, plane, 0, keepdims=False)}
        t_slots.update(fabric.to_owners(t_own, 0))
        t_slots.update(fabric.to_owners(t_own, 1))
        d_half, _ = half_gram(core, [d], [d_far])
        d, d_half, a_xy, t_slots, a_far = hold(d, d_half, a_xy, t_slots, a_far)
        t_slots.update(fabric.to_owners(t_own, 2))
        d_other = fabric.swap(d_half, CORE)
        a_near, a_far_xy = hold([a, a_x, a_y, a_xy], fabric.swap(a_xy, CORE))
        grad_active_x = fabric.swap(grad_active, ALONG_X)
        a_half, a = half_gram(core, a_near, a_far + [a_far_xy])
        a, a_half, d_half, d_other, t_slots, grad_active_x = hold(
            a, a_half, d_half, d_other, t_slots, grad_active_x
        )
        grad_active += grad_active_x
        t_slots = [t_slots[j] for j in range(planes)]
        t_first = jnp.concatenate(t_slots[: planes // 2], axis=0)
        t_second = jnp.concatenate(t_slots[planes // 2 :], axis=0)
        t_first_x, t_second_y = fabric.swap(t_first, ALONG_X), fabric.swap(t_second, ALONG_Y)
        t_far = [fabric.swap(t_first, CORE), fabric.swap(t_second, CORE)]
        a_other = fabric.swap(a_half, CORE)
        d_rows, d_beside = polynomial(core, d, d_half, d_other, False, 2)
        d_rows, d_beside, a_half, a_other, t_first_x, t_second_y, t_far = hold(
            d_rows, d_beside, a_half, a_other, t_first_x, t_second_y, t_far
        )
        t_second_x, t_first_y = fabric.swap(t_second, ALONG_X), fabric.swap(t_first, ALONG_Y)
        t_second_xy, t_first_xy = fabric.swap(t_second_y, ALONG_X), fabric.swap(t_first_x, ALONG_Y)
        a = polynomial(core, a, a_half, a_other, True)
        a, t_second_x, t_first_y, t_second_xy, t_first_xy = hold(
            a, t_second_x, t_first_y, t_second_xy, t_first_xy
        )
        t_near = [t_first, t_second, t_first_x, t_second_x, t_first_y, t_second_y]
        t_near = t_near + [t_first_xy, t_second_xy]
        d_x = fabric.swap(d_beside, ALONG_X)
        first_too = fabric.swap(first_far, CORE)
        a, a_far = hold(a, fabric.swap(a, CORE))
        t_far = t_far + [fabric.swap(piece, CORE) for piece in t_near[2:]]
        first_sums = fabric.settle_begin(first_near, first_too)
        a_half, _ = half_gram(core, [a], [a_far])
        a, a_half, t_far, d_x = hold(a, a_half, t_far, d_x)
        d_slots = joined(d_rows, d_x)
        d_came = fabric.from_owners(d_slots, 0)
        a_other = fabric.swap(a_half, CORE)
        t_half, t = half_gram(core, t_near, t_far)
        t, t_half, a_half, a_other, d_came = hold(t, t_half, a_half, a_other, d_came)
        d_came.update(fabric.from_owners(d_slots, 1))
        t_other = fabric.swap(t_half, CORE)
        a_rows, a_beside = polynomial(core, a, a_half, a_other, False, 2)
        a_rows, a_beside, t_half, t_other, d_came, first_sums = hold(
            a_rows, a_beside, t_half, t_other, d_came, first_sums
        )
        d_came.update(fabric.from_owners(d_slots, 2))
        a_x = fabric.swap(a_beside, ALONG_X)
        grad_active_y = fabric.swap(grad_active, ALONG_Y)
        t = polynomial(core, t, t_half, t_other, True)
        t, a_x, d_came, grad_active_y = hold(t, a_x, d_came, grad_active_y)
        grad_active += grad_active_y
        a_slots = joined(a_rows, a_x)
        a_came = fabric.from_owners(a_slots, 0)
        a_came.update(fabric.from_owners(a_slots, 1))
        t, t_far = hold(t, fabric.swap(t, CORE))
        grad_first = fabric.settle_end(first_sums).reshape(here, inner, width)
        t_half, _ = half_gram(core, [t], [t_far])
        t, t_half, a_came, grad_first = hold(t, t_half, a_came, grad_first)
        a_came.update(fabric.from_owners(a_slots, 2))
        t_half, t_other = hold(t_half, fabric.swap(t_half, CORE))
        (t_rows,) = polynomial(core, t, t_half, t_other, False, 1)
        t_rows, a_came = hold(t_rows, a_came)
        return t_rows, d_slots[0], d_came, a_slots[0], a_came, grad_first, grad_active

    t_rows, d_own, d_came, a_own, a_came, grad_first, grad_active = fence(
        valid, steps_two, d, a, a_x, a_y, a_far, attention_momentum, first_near, first_far,
        grad_active,
    )
    t_slots = [t_rows[j * shard_rows : (j + 1) * shard_rows] for j in range(planes)]
    t_came = {}
    for group in range(3):
        t_came.update(fabric.from_owners(t_slots, group))
    dense_ortho = two_units(d_own, d_came)
    ada_ortho = two_units(a_own, a_came)
    attention_ortho = fabric.by_plane(t_slots[0], t_came)
    grad_active = fabric.plane_total(grad_active)
    ada_momentum = matrix_decay * moment[start_ada:] + jnp.einsum(
        "nur,nk->urk", grad_mod_all, active.astype(wide), precision=highest
    )

    normed_one, inverse_one = normalize(tokens.astype(wide))
    input_grad = grad_middle + norm_back(
        grad_first * (1.0 + scale_one), normed_one, inverse_one
    )
    input_grad = input_grad.astype(low)
    dense_ortho, ada_ortho = dense_ortho[: 2 * blocks], ada_ortho[:6]
    attention_ortho = attention_ortho[:4]

    bias_grad = jnp.sum(grad_mod_all, axis=0)
    table_grad = jnp.dot(selector.T, grad_active, precision=highest) * silu_slope(level_table)
    momentum = jnp.concatenate(
        [
            attention_momentum,
            dense_momentum,
            ada_momentum,
        ],
        axis=0,
    ).transpose(1, 0, 2)
    ortho = jnp.concatenate([attention_ortho, dense_ortho, ada_ortho], axis=0).transpose(1, 0, 2)
    step_size = matrix_rate * 0.2 * math.sqrt(width)
    matrix_new = matrices - step_size * ortho.astype(wide)
    bias_momentum = vector_decay * bias_moment + bias_grad
    bias_new = modulation_bias - bias_rate * bias_momentum
    table_momentum = vector_decay * table_moment + table_grad
    table_new = level_table - table_rate * table_momentum
    return (
        block_out,
        input_grad,
        table_grad,
        table_momentum,
        table_new,
        momentum,
        matrix_new,
        bias_momentum,
        bias_new,
    )


def solution(mesh):
    whole = P(("img", "strip"), None, None)
    table = P(("img", "strip"), None)
    strip = P("img", "strip", None)
    bias = P(None, ("img", "strip"))
    return jax.shard_map(
        on_device,
        mesh=mesh,
        in_specs=(strip, strip, P(), table, table, whole, whole, bias, bias),
        out_specs=(strip, strip, table, table, table, whole, whole, bias, bias),
        check_vma=False,
    )
```

```python
import functools
import math

import jax
import jax.numpy as jnp
from jax import lax
from jax.experimental import pallas as pl
from jax.experimental.pallas import tpu as pltpu
from jax.sharding import PartitionSpec as P

HEADS = 16
HD = 128

highest = lax.Precision.HIGHEST
norm_eps = 1e-06
coef_one = 3.4445
coef_two = -4.775
coef_three = 2.0315
matrix_decay = 0.95
vector_decay = 0.9
matrix_rate = 0.5
bias_rate = 0.003
table_rate = 0.02

WORLD = ("img", "strip")
CORE, ALONG_X, ALONG_Y = 1, 2, 4
TEAM = 8
low = jnp.bfloat16
wide = jnp.float32


def dot(spec, left, right):
    return jnp.einsum(spec, left, right, preferred_element_type=wide)


def after(value, *earlier):
    return lax.optimization_barrier((value, *earlier))[0]


def after_all(values, *earlier):
    return lax.optimization_barrier((*values, *earlier))[: len(values)]


def hold(*values):
    return lax.optimization_barrier(values)


def fence(flag, body, *operands):
    shapes = jax.eval_shape(body, *operands)
    empty = lambda *_: jax.tree.map(lambda leaf: jnp.zeros(leaf.shape, leaf.dtype), shapes)
    return lax.cond(flag, body, empty, *operands)


def add(left, right):
    return left.astype(wide) + right.astype(wide)


def normalize(values):
    center = values - jnp.mean(values, axis=-1, keepdims=True)
    inverse = lax.rsqrt(jnp.mean(center * center, axis=-1, keepdims=True) + norm_eps)
    return (center * inverse, inverse)


def norm_back(grad_hat, normed, inverse):
    mean_grad = jnp.mean(grad_hat, axis=-1, keepdims=True)
    mean_cross = jnp.mean(grad_hat * normed, axis=-1, keepdims=True)
    return inverse * (grad_hat - mean_grad - normed * mean_cross)


def gelu_slope(values):
    cumulative = 0.5 * (1.0 + lax.erf(values * 0.7071067811865476))
    density = jnp.exp(-0.5 * values * values) * 0.3989422804014327
    return cumulative + values * density


def silu_slope(values):
    logistic = jax.nn.sigmoid(values)
    return logistic * (1.0 + values * (1.0 - logistic))


class Fabric:
    def __init__(self):
        self.count = lax.axis_size("img") * lax.axis_size("strip")
        self.planes = self.count // TEAM
        self.me = lax.axis_index(WORLD)
        self.plane = self.me // TEAM
        self.seat = self.me % TEAM
        self.lines = [
            [plane * TEAM + seat for plane in range(self.planes)] for seat in range(TEAM)
        ]

    def swap(self, value, bit):
        return lax.ppermute(value, WORLD, [(d, d ^ bit) for d in range(self.count)])

    def turn(self, value, offset):
        pairs = [(d, (d + offset * TEAM) % self.count) for d in range(self.count)]
        return lax.ppermute(value, WORLD, pairs)

    def gather_planes(self, shard):
        return lax.all_gather(shard, WORLD, axis=0, tiled=True, axis_index_groups=self.lines)

    def reduce_planes(self, parts):
        return lax.psum_scatter(
            parts, WORLD, scatter_dimension=0, tiled=True, axis_index_groups=self.lines
        )

    def trade_planes(self, blocks):
        return lax.all_to_all(
            blocks, WORLD, split_axis=0, concat_axis=0, tiled=True, axis_index_groups=self.lines
        )

    def pieces(self):
        distances = list(range(1, self.planes))
        return [distances[:1], distances[-1:], distances[1:-1]]

    def to_owners(self, blocks, group):
        return {
            distance: self.turn(
                lax.dynamic_index_in_dim(
                    blocks, (self.plane + distance) % self.planes, 0, keepdims=False
                ),
                distance,
            )
            for distance in self.pieces()[group]
        }

    def from_owners(self, slots, group):
        return {distance: self.turn(slots[distance], -distance) for distance in self.pieces()[group]}

    def slots_of(self, blocks):
        return [
            lax.dynamic_index_in_dim(blocks, (self.plane - j) % self.planes, 0, keepdims=False)
            for j in range(self.planes)
        ]

    def by_plane(self, own, came):
        came = {0: own, **came}
        result = jnp.zeros((self.planes,) + own.shape, own.dtype)
        for distance, block in came.items():
            result = lax.dynamic_update_index_in_dim(
                result, block, (self.plane + distance) % self.planes, 0
            )
        return result

    def team_total(self, value):
        for bit in (CORE, ALONG_X, ALONG_Y):
            value = value + self.swap(value, bit)
        return value

    def planes_over(self, value):
        distance = 2
        while distance < self.planes:
            value = value + self.swap(value, distance * TEAM)
            distance *= 2
        return value

    def plane_total(self, value):
        others = [self.turn(value, offset) for offset in range(1, self.planes)]
        for other in others:
            value = value + other
        return value

    def share(self, rows, between=()):
        parts = self.share_begin(rows)
        if between:
            first_x, second_y = after_all(parts[3:5], *between)
            parts = (*parts[:3], first_x, second_y, *parts[5:])
        return self.share_end(parts)

    def share_begin(self, rows):
        half = rows.shape[0] // 2
        first, second = rows[:half], rows[half:]
        return (
            rows,
            self.swap(first, ALONG_Y),
            self.swap(second, ALONG_X),
            self.swap(first, ALONG_X),
            self.swap(second, ALONG_Y),
        )

    def share_end(self, parts):
        return jnp.concatenate(self.share_last(parts), axis=0)

    def share_last(self, parts):
        rows, first_y, second_x, first_x, second_y = parts
        first_xy = self.swap(first_x, ALONG_Y)
        second_xy = self.swap(second_y, ALONG_X)
        return [rows, first_x, second_x, first_y, second_y, first_xy, second_xy]

    def settle(self, near, near_too, beside=None):
        if beside is None:
            return self.settle_end(self.settle_begin(near, near_too))
        parts = self.settle_begin(near, near_too)
        *parts, done = hold(*parts, beside())
        return self.settle_end(parts), done

    def settle_begin(self, near, near_too):
        return self.settle_hops(add(near, near_too).astype(low))

    def settle_pieces(self, near):
        size, width = near.shape[0] // 8, near.shape[-1]
        near = near.reshape(2, 2, 2, size, width)
        first, second = near[:, :, 0], near[:, :, 1]
        return (first[:, 0], second[0]), [(first[k, 1], second[1, k]) for k in (0, 1)]

    def settle_split(self, near):
        size, width = near.shape[0] // 8, near.shape[-1]
        near = near.reshape(2, 2, 2, size, width)
        first, second = near[:, :, 0], near[:, :, 1]
        return (first[:, 0], second[0]), (first[:, 1], second[1])

    def settle_hop(self, first, second):
        return self.swap(first, ALONG_X), self.swap(second, ALONG_Y)

    def settle_joined(self, kept, hops):
        first, second = kept
        (first_a, second_a), (first_b, second_b) = hops
        return (
            (add(first[0], first_a).astype(low), add(first[1], first_b).astype(low)),
            (add(second[0], second_a).astype(low), add(second[1], second_b).astype(low)),
        )

    def settle_hops(self, near):
        size, width = near.shape[0] // 8, near.shape[-1]
        near = near.reshape(2, 2, 2, size, width)
        first, second = near[:, :, 0], near[:, :, 1]
        first_x = self.swap(first[:, 1], ALONG_X)
        second_y = self.swap(second[1], ALONG_Y)
        return first[:, 0], second[0], first_x, second_y

    def settle_end(self, parts):
        return self.settle_sum(self.settle_last(self.settle_add(parts)))

    def settle_add(self, parts):
        first, second, first_x, second_y = parts
        return (
            [add(first[k], first_x[k]).astype(low) for k in (0, 1)],
            [add(second[k], second_y[k]).astype(low) for k in (0, 1)],
        )

    def settle_last(self, parts):
        first, second = parts
        first_y, second_x = self.swap(first[1], ALONG_Y), self.swap(second[1], ALONG_X)
        return first[0], second[0], first_y, second_x

    def settle_sum(self, parts):
        first, second, first_y, second_x = parts
        return jnp.concatenate([add(first, first_y), add(second, second_x)], axis=0)


VMEM_BYTES = 60 * 2**20
QUICK = pl.CostEstimate(flops=1, bytes_accessed=1, transcendentals=0)


def attend_body(projected_ref, mixed_ref):
    size = mixed_ref.shape[-1]
    shape = mixed_ref.shape[:-1] + (HD,)
    tokens = math.prod(shape[:-1])
    for first in range(0, size, HD):

        def read(unit):
            block = projected_ref[..., unit * size + first : unit * size + first + HD]
            return block.reshape(tokens, HD)

        scores = lax.dot_general(
            read(0), read(1), (((1,), (1,)), ((), ())), preferred_element_type=wide
        ) * HD ** (-0.5)
        exponent = jnp.exp(scores - jnp.max(scores, axis=-1, keepdims=True))
        probs = (exponent / jnp.sum(exponent, axis=-1, keepdims=True)).astype(low)
        mixed = jnp.dot(probs, read(2), preferred_element_type=wide).astype(low)
        mixed_ref[..., first : first + HD] = mixed.reshape(shape)


def attend_back_body(projected_ref, grad_ref, out_ref):
    size = grad_ref.shape[-1]
    shape = grad_ref.shape[:-1] + (HD,)
    tokens = math.prod(shape[:-1])
    factor = HD ** (-0.5)
    across = (((1,), (1,)), ((), ()))
    down = (((0,), (0,)), ((), ()))
    for first in range(0, size, HD):

        def read(unit):
            block = projected_ref[..., unit * size + first : unit * size + first + HD]
            return block.reshape(tokens, HD)

        def write(unit, value):
            part = slice(unit * size + first, unit * size + first + HD)
            out_ref[..., part] = value.astype(low).reshape(shape)

        query, keys_all, values_all = read(0), read(1), read(2)
        grad_heads = grad_ref[..., first : first + HD].reshape(tokens, HD)
        scores = lax.dot_general(query, keys_all, across, preferred_element_type=wide) * factor
        exponent = jnp.exp(scores - jnp.max(scores, axis=-1, keepdims=True))
        probs = exponent / jnp.sum(exponent, axis=-1, keepdims=True)
        grad_probs = lax.dot_general(grad_heads, values_all, across, preferred_element_type=wide)
        cross = jnp.sum(probs * grad_probs, axis=-1, keepdims=True)
        grad_scores = (probs * (grad_probs - cross)).astype(low)
        write(0, jnp.dot(grad_scores, keys_all, preferred_element_type=wide) * factor)
        write(1, lax.dot_general(grad_scores, query, down, preferred_element_type=wide) * factor)
        write(2, lax.dot_general(probs.astype(low), grad_heads, down, preferred_element_type=wide))


def over_images(body, here, inner, arrays, out_features):
    def block(features):
        return pl.BlockSpec(
            (2, 1, 2, 1, inner, features), lambda side, image: (0, side, 0, image, 0, 0)
        )

    arrays = [rows.reshape(2, 2, 2, here, inner, rows.shape[-1]) for rows in arrays]
    result = pl.pallas_call(
        body,
        grid=(2, here),
        in_specs=[block(rows.shape[-1]) for rows in arrays],
        out_specs=block(out_features),
        out_shape=jax.ShapeDtypeStruct((2, 2, 2, here, inner, out_features), low),
        compiler_params=pltpu.CompilerParams(vmem_limit_bytes=32 * 2**20),
        cost_estimate=QUICK,
    )(*arrays)
    return result.reshape(-1, out_features)


def modulate_body(rows_ref, modulation_ref, out_ref):
    values = rows_ref[0, 0].astype(wide)
    center = values - jnp.mean(values, axis=-1, keepdims=True)
    inverse = lax.rsqrt(jnp.mean(center * center, axis=-1, keepdims=True) + norm_eps)
    shift = modulation_ref[0, :, 0:1, :]
    scale = modulation_ref[0, :, 1:2, :]
    out_ref[0, 0] = (center * inverse * (1.0 + scale) + shift).astype(low)


def modulate(rows, modulation):
    sides, seats, here, inner, width = rows.shape
    block = pl.BlockSpec((1, 1, here, inner, width), lambda y, x: (y, x, 0, 0, 0))
    return pl.pallas_call(
        modulate_body,
        grid=(sides, seats),
        in_specs=[
            block,
            pl.BlockSpec((1, here) + modulation.shape[2:], lambda y, x: (y, 0, 0, 0)),
        ],
        out_specs=block,
        out_shape=jax.ShapeDtypeStruct(rows.shape, low),
        compiler_params=pltpu.CompilerParams(vmem_limit_bytes=48 * 2**20),
        cost_estimate=QUICK,
    )(rows, modulation)


def gate_body(hidden_ref, weight_ref, upstream_ref, part_ref, cross_ref):
    part = jnp.dot(hidden_ref[...], weight_ref[...], preferred_element_type=wide)
    part_ref[...] = part.astype(low)
    here, inner, width = upstream_ref.shape[2:]
    cross = upstream_ref[0, 0].astype(wide) * part.reshape(here, inner, width)
    cross = jnp.sum(cross, axis=1)[None]

    @pl.when(pl.program_id(1) == 0)
    def _():
        cross_ref[...] = cross

    @pl.when(pl.program_id(1) > 0)
    def _():
        cross_ref[...] += cross


def gate_sums(hidden, weight, upstream):
    sides, seats, here, inner, width = upstream.shape
    size = here * inner
    return pl.pallas_call(
        gate_body,
        grid=(sides, seats),
        in_specs=[
            pl.BlockSpec((size, hidden.shape[1]), lambda y, x: (y * seats + x, 0)),
            pl.BlockSpec(weight.shape, lambda y, x: (0, 0)),
            pl.BlockSpec((1, 1, here, inner, width), lambda y, x: (y, x, 0, 0, 0)),
        ],
        out_specs=[
            pl.BlockSpec((size, width), lambda y, x: (y * seats + x, 0)),
            pl.BlockSpec((1, here, width), lambda y, x: (y, 0, 0)),
        ],
        out_shape=[
            jax.ShapeDtypeStruct((hidden.shape[0], width), low),
            jax.ShapeDtypeStruct((sides, here, width), wide),
        ],
        compiler_params=pltpu.CompilerParams(vmem_limit_bytes=VMEM_BYTES),
        cost_estimate=QUICK,
    )(hidden, weight, upstream)


def norm_sums_body(grad_ref, weight_ref, rows_ref, part_ref, sums_ref):
    part = jnp.dot(grad_ref[...], weight_ref[...], preferred_element_type=wide)
    part_ref[...] = part.astype(low)
    here, inner, width = rows_ref.shape[2:]
    part = part.reshape(here, inner, width)
    values = rows_ref[0, 0].astype(wide)
    center = values - jnp.mean(values, axis=-1, keepdims=True)
    inverse = lax.rsqrt(jnp.mean(center * center, axis=-1, keepdims=True) + norm_eps)
    shift = jnp.sum(part, axis=1)[None, None]
    scale = jnp.sum(part * (center * inverse), axis=1)[None, None]

    @pl.when(pl.program_id(1) == 0)
    def _():
        sums_ref[0:1] = shift
        sums_ref[1:2] = scale

    @pl.when(pl.program_id(1) > 0)
    def _():
        sums_ref[0:1] += shift
        sums_ref[1:2] += scale


def norm_sums(grads, weight, rows):
    sides, seats, here, inner, width = rows.shape
    size = here * inner
    return pl.pallas_call(
        norm_sums_body,
        grid=(sides, seats),
        in_specs=[
            pl.BlockSpec((size, grads.shape[1]), lambda y, x: (y * seats + x, 0)),
            pl.BlockSpec(weight.shape, lambda y, x: (0, 0)),
            pl.BlockSpec((1, 1, here, inner, width), lambda y, x: (y, x, 0, 0, 0)),
        ],
        out_specs=[
            pl.BlockSpec((size, width), lambda y, x: (y * seats + x, 0)),
            pl.BlockSpec((2, 1, here, width), lambda y, x: (0, y, 0, 0)),
        ],
        out_shape=[
            jax.ShapeDtypeStruct((grads.shape[0], width), low),
            jax.ShapeDtypeStruct((2, sides, here, width), wide),
        ],
        compiler_params=pltpu.CompilerParams(vmem_limit_bytes=VMEM_BYTES),
        cost_estimate=QUICK,
    )(grads, weight, rows)


def finish_body(*refs):
    mlp, grads, refs = refs[:4], refs[4:8], refs[8:]
    tokens_ref, middle_ref, gate_ref, upper_ref, scale_ref, out_ref, grad_ref = refs

    def work(kept, came):
        shape = middle_ref.shape
        mlp_out = (mlp[kept][...].astype(wide) + mlp[came][...].astype(wide)).reshape(shape)
        out_ref[...] = (middle_ref[...] + gate_ref[...] * mlp_out).astype(low)
        grad = (grads[kept][...].astype(wide) + grads[came][...].astype(wide)).reshape(shape)
        normed, inverse = normalize(tokens_ref[...].astype(wide))
        grad = norm_back(grad * (1.0 + scale_ref[...]), normed, inverse)
        grad_ref[...] = (upper_ref[...] + grad).astype(low)

    @pl.when(pl.program_id(0) == 0)
    def _():
        work(0, 2)

    @pl.when(pl.program_id(0) == 1)
    def _():
        work(1, 3)


def finish(mlp, grads, tokens, middle, gate, upper, scale):
    here, inner, width = tokens.shape
    part = pl.BlockSpec(mlp[0].shape, lambda i: (0, 0))
    rows = pl.BlockSpec((here // 2, inner, width), lambda i: (i, 0, 0))
    line = pl.BlockSpec((here // 2, 1, width), lambda i: (i, 0, 0))
    return pl.pallas_call(
        finish_body,
        grid=(2,),
        in_specs=[part] * 8 + [rows, rows, line, rows, line],
        out_specs=[rows, rows],
        out_shape=[jax.ShapeDtypeStruct(tokens.shape, low)] * 2,
        compiler_params=pltpu.CompilerParams(vmem_limit_bytes=VMEM_BYTES),
        cost_estimate=QUICK,
    )(*mlp, *grads, tokens, middle, gate, upper, scale)


def arrange_body(place_ref, *refs, places):
    *pieces, out_ref, sem = refs
    copies = [
        pltpu.make_async_copy(piece, out_ref.at[pl.ds(place(place_ref), piece.shape[0])], sem.at[k])
        for k, (piece, place) in enumerate(zip(pieces, places))
    ]
    for copy in copies:
        copy.start()
    for copy in copies:
        copy.wait()


def arrange(place, pieces, places, count):
    anywhere = pl.BlockSpec(memory_space=pl.ANY)
    return pl.pallas_call(
        functools.partial(arrange_body, places=places),
        in_specs=[pl.BlockSpec(memory_space=pltpu.SMEM)] + [anywhere] * len(pieces),
        out_specs=pl.BlockSpec(memory_space=pltpu.VMEM),
        out_shape=jax.ShapeDtypeStruct((count,) + pieces[0].shape[1:], low),
        scratch_shapes=[pltpu.SemaphoreType.DMA((len(pieces),))],
        compiler_params=pltpu.CompilerParams(vmem_limit_bytes=VMEM_BYTES),
        cost_estimate=QUICK,
    )(place, *pieces)


CHUNK = 512
ROW_BLOCK = 256


def gram_body(core_ref, *refs, near_count, far_count):
    pieces = refs[: near_count + far_count]
    out_ref, near_ref, x_ref, sem, near_sem = refs[near_count + far_count :]
    width = x_ref.shape[1]
    half = width // 2
    tile = out_ref.shape[0]
    step = pl.program_id(0)
    start = core_ref[0] * half

    def column(j):
        return pl.multiple_of((start + j * CHUNK) % width, CHUNK)

    def copies(j):
        part = pl.ds(column(j), CHUNK)
        result, row = [], 0
        for k, piece in enumerate(pieces):
            rows = pl.ds(row, piece.shape[0])
            result.append(
                pltpu.make_async_copy(piece.at[:, part], x_ref.at[rows, part], sem.at[j, k])
            )
            row += piece.shape[0]
        return result

    joined = pltpu.make_async_copy(x_ref.at[pl.ds(0, near_ref.shape[0])], near_ref, near_sem)

    @pl.when(step == 0)
    def _():
        for j in range(width // CHUNK):
            for copy in copies(j):
                copy.start()

    left = pl.ds(pl.multiple_of(start + step * tile, tile), tile)
    for j in range(width // CHUNK):

        @pl.when(step == 0)
        def _():
            for copy in copies(j):
                copy.wait()
            if j == width // CHUNK - 1 and near_count > 1:
                joined.start()

        part = pl.ds(column(j), CHUNK)
        total = lax.dot_general(
            x_ref[:, left], x_ref[:, part], (((0,), (0,)), ((), ())), preferred_element_type=wide
        )
        out_ref[:, part] = total.astype(low)

    if near_count > 1:

        @pl.when(step == pl.num_programs(0) - 1)
        def _():
            joined.wait()


def half_gram(core, near, far):
    width = near[0].shape[1]
    near_rows = sum(piece.shape[0] for piece in near)
    far_rows = sum(piece.shape[0] for piece in far)
    anywhere = pl.BlockSpec(memory_space=pl.ANY)
    kept = near_rows if len(near) > 1 else 16
    half, joined = pl.pallas_call(
        functools.partial(gram_body, near_count=len(near), far_count=len(far)),
        grid=(width // 2 // CHUNK,),
        in_specs=[pl.BlockSpec(memory_space=pltpu.SMEM)] + [anywhere] * (len(near) + len(far)),
        out_specs=[pl.BlockSpec((CHUNK, width), lambda i: (i, 0)), anywhere],
        out_shape=[
            jax.ShapeDtypeStruct((width // 2, width), low),
            jax.ShapeDtypeStruct((kept, width), low),
        ],
        scratch_shapes=[
            pltpu.VMEM((near_rows + far_rows, width), low),
            pltpu.SemaphoreType.DMA((width // CHUNK, len(near) + len(far))),
            pltpu.SemaphoreType.DMA,
        ],
        compiler_params=pltpu.CompilerParams(vmem_limit_bytes=VMEM_BYTES),
        cost_estimate=QUICK,
    )(core, *near, *far)
    return half, joined if len(near) > 1 else near[0]


def polynomial_body(core_ref, rows_ref, mine_ref, other_ref, *refs, scaled):
    *outs, gram_ref, wide_ref, low_ref, factor_ref, sem = refs
    width = rows_ref.shape[1]
    half = width // 2
    first = pl.program_id(0) == 0
    core = core_ref[0]
    places = [pl.multiple_of(core * half, half), pl.multiple_of((1 - core) * half, half)]

    def copies(j):
        part = pl.ds(j * CHUNK, CHUNK)
        return [
            pltpu.make_async_copy(
                source.at[:, part], gram_ref.at[pl.ds(places[k], half), part], sem.at[j, k]
            )
            for k, source in enumerate((mine_ref, other_ref))
        ]

    @pl.when(first)
    def _():
        for j in range(width // CHUNK):
            for copy in copies(j):
                copy.start()

    tiles = [slice(start, start + CHUNK) for start in range(0, width, CHUNK)]
    for j, part in enumerate(tiles):

        @pl.when(first)
        def _():
            for copy in copies(j):
                copy.wait()

        wide_ref[:, part] = jnp.dot(
            rows_ref[...], gram_ref[:, part], preferred_element_type=wide
        )
        if not scaled:
            low_ref[:, part] = wide_ref[:, part].astype(low)

    if scaled:

        @pl.when(first)
        def _():
            trace = jnp.float32(0.0)
            size = 256
            row = lax.broadcasted_iota(jnp.int32, (size, size), 0)
            column = lax.broadcasted_iota(jnp.int32, (size, size), 1)
            for start in range(0, width, size):
                block = gram_ref[start : start + size, start : start + size].astype(wide)
                trace += jnp.sum(jnp.where(row == column, block, 0.0))
            factor_ref[0] = 1.0 / (jnp.sqrt(trace) + 1e-07)

        factor = factor_ref[0]
        cube, squared = factor * factor * factor, factor * factor
        for part in tiles:
            product = wide_ref[:, part] * cube
            wide_ref[:, part] = product
            low_ref[:, part] = product.astype(low)
    else:
        factor = squared = jnp.float32(1.0)
    for part in tiles:
        square = jnp.dot(low_ref[...], gram_ref[:, part], preferred_element_type=wide) * squared
        lead = (coef_one * factor) * rows_ref[:, part].astype(wide)
        result = (lead + coef_two * wide_ref[:, part] + coef_three * square).astype(low)
        if len(outs) == 1:
            outs[0][:, part] = result
        else:
            for k, out_ref in enumerate(outs):

                @pl.when(pl.program_id(0) == k)
                def _():
                    out_ref[:, part] = result


def polynomial(core, rows, mine, other, scaled, blocks=None):
    count, width = rows.shape
    if blocks is not None:
        count = blocks * ROW_BLOCK
    anywhere = pl.BlockSpec(memory_space=pl.ANY)
    block = pl.BlockSpec((ROW_BLOCK, width), lambda i: (i, 0))
    if blocks is None:
        out_specs, out_shape = block, jax.ShapeDtypeStruct((count, width), low)
    else:
        out_specs = [pl.BlockSpec((ROW_BLOCK, width), lambda i: (0, 0))] * blocks
        out_shape = [jax.ShapeDtypeStruct((ROW_BLOCK, width), low)] * blocks
    return pl.pallas_call(
        functools.partial(polynomial_body, scaled=scaled),
        grid=(count // ROW_BLOCK,),
        in_specs=[pl.BlockSpec(memory_space=pltpu.SMEM), block, anywhere, anywhere],
        out_specs=out_specs,
        out_shape=out_shape,
        scratch_shapes=[
            pltpu.VMEM((width, width), low),
            pltpu.VMEM((ROW_BLOCK, width), wide),
            pltpu.VMEM((ROW_BLOCK, width), low),
            pltpu.SMEM((1,), wide),
            pltpu.SemaphoreType.DMA((width // CHUNK, 2)),
        ],
        compiler_params=pltpu.CompilerParams(vmem_limit_bytes=VMEM_BYTES),
        cost_estimate=QUICK,
    )(core, rows, mine, other)


def on_device(
    tokens,
    cotangent,
    bin_ids,
    level_table,
    table_moment,
    matrices,
    matrix_moment,
    modulation_bias,
    bias_moment,
):
    fabric = Fabric()
    planes, plane, seat = fabric.planes, fabric.plane, fabric.seat
    strips = lax.axis_size("strip")
    here, inner, width = tokens.shape
    shard_rows, units, _ = matrices.shape
    images = bin_ids.shape[0]
    table_rows = level_table.shape[0]
    blocks = (units - 10) // 2
    start_down = 4 + blocks
    start_ada = 4 + 2 * blocks
    slot_rows = planes * shard_rows
    valid = bin_ids[0] >= 0
    core = (fabric.me % 2).astype(jnp.int32).reshape(1)
    side = seat // 2 % 2
    peers = HD // shard_rows
    heads = planes // peers
    place = fabric.me % peers

    def flat(values):
        return values.reshape(here * inner, width)

    def whole(pair):
        return jnp.concatenate(pair, axis=0)

    def halves(rows):
        return [rows[: rows.shape[0] // 2], rows[rows.shape[0] // 2 :]]

    def parts(rows, weight):
        near, far = [dot("tj,jk->tk", piece, weight).astype(low) for piece in rows]
        return near, fabric.swap(far, CORE)

    def settled(pair):
        return fabric.settle(*pair).reshape(here, inner, width)

    def both(near):
        return [near, fabric.swap(near, CORE)]

    def over_tokens(left, right):
        return dot("tj,tk->jk", whole(left), whole(right)).astype(low)

    row_ids = fabric.me * table_rows + jnp.arange(table_rows, dtype=jnp.int32)
    selector = (bin_ids[:, None] == row_ids[None, :]).astype(wide)
    in_plane = images // planes
    ada_weight = matrices[:, start_ada:, :].astype(low)

    def modulated(modulation, which):
        return modulation[None, :, None, :, None, which]

    def open_rows(rows):
        return rows.reshape(1, 2, 2, here, inner, width).astype(wide)

    active_rows = jax.nn.silu(level_table).astype(low)
    active = jnp.dot(selector.astype(low), active_rows, preferred_element_type=wide)
    active = fabric.plane_total(active.astype(low))

    def gathered(first, last):
        rows = matrices[:, first:last].astype(low).transpose(1, 0, 2)
        rows = after(rows.reshape((last - first) * shard_rows, width), active)
        return fabric.gather_planes(rows)

    attention = gathered(0, 4)
    up_weight = gathered(4, start_down)
    down_weight = gathered(start_down, start_ada)

    moment = matrix_moment.transpose(1, 0, 2)

    def padded(batch, count):
        spare = count - batch.shape[0]
        if spare == 0:
            return batch
        return jnp.concatenate([batch, jnp.zeros((spare,) + batch.shape[1:], batch.dtype)], axis=0)

    def to_owner(batch, each):
        batch = padded(batch, planes * each)
        return fabric.trade_planes(batch.reshape(planes, each * shard_rows, width))

    def to_rows(batch, count):
        return fabric.trade_planes(batch).reshape(-1, shard_rows, width)[:count]

    def begin(active):
        active = fabric.team_total(active)
        rows, active = hold(flat(tokens), active)
        half = rows.shape[0] // 2
        first, second = rows[:half], rows[half:]
        mod_columns = dot("nk,ruk->nur", active, ada_weight) + modulation_bias[None]
        mod_parts = jnp.broadcast_to(
            mod_columns.reshape(planes, 1, in_plane, 6, shard_rows),
            (planes, TEAM, in_plane, 6, shard_rows),
        ).reshape(fabric.count, in_plane, 6, shard_rows)
        mod_parts = lax.all_to_all(mod_parts, WORLD, split_axis=0, concat_axis=0, tiled=True)
        first_x, second_y, mod_parts = hold(
            fabric.swap(first, ALONG_X), fabric.swap(second, ALONG_Y), mod_parts
        )
        modulation = mod_parts.transpose(1, 2, 0, 3).reshape(2, here, 6, width)
        modulation = jnp.where(seat // 4 == 0, modulation, modulation[::-1])
        first_y, second_x, first_xy, second_xy, modulation = hold(
            fabric.swap(first, ALONG_Y),
            fabric.swap(second, ALONG_X),
            fabric.swap(first_x, ALONG_Y),
            fabric.swap(second_y, ALONG_X),
            modulation,
        )
        near = jnp.concatenate(
            [rows, first_x, second_x, first_y, second_y, first_xy, second_xy], axis=0
        )
        first_in = modulate(near.reshape(2, 2, here, inner, width), modulation)
        first_in = both(first_in.reshape(-1, width))
        return active, modulation, first_in, near

    active, modulation, first_in, tokens_near = fence(valid, begin, active)
    local = modulation[0][:, :, None, :]
    shift_one, scale_one, gate_one = local[:, 0], local[:, 1], local[:, 2]
    shift_two, scale_two, gate_two = local[:, 3], local[:, 4], local[:, 5]

    def mates(offset):
        return [
            (d, d // peers * peers + (d % peers + offset) % peers) for d in range(fabric.count)
        ]

    def attention_forward(attention):
        upstream = fabric.share_begin(flat(cotangent))
        attention = attention.reshape(planes, 4, shard_rows, width)
        pieces = [lax.dynamic_slice_in_dim(attention, place * heads, heads, 0)]
        for offset in range(1, peers):
            target = (place + offset) % peers
            payload = lax.dynamic_slice_in_dim(attention, target * heads, heads, 0)
            pieces.append(lax.ppermute(payload, WORLD, mates(offset)))
        attention = jnp.stack(pieces).transpose(2, 1, 0, 3, 4).reshape(4, heads * HD, width)
        weight_in = attention[:3].reshape(3 * heads * HD, width)
        weight_out = attention[3]
        near, far = [dot("tk,jk->tj", rows, weight_in).astype(low) for rows in first_in]
        projected = whole([near, far]).reshape(2, 2, 2, here, inner, 3 * heads * HD)
        projected, upstream = hold(projected, upstream)
        upstream = fabric.share_last(upstream)
        mixed = over_images(attend_body, here, inner, [projected], heads * HD)
        return weight_in, weight_out, projected, mixed, upstream

    weight_in, weight_out, projected, mixed, upstream = fence(valid, attention_forward, attention)


    def middle_forward(mixed, upstream):
        upstream = whole(upstream)
        branch = fabric.settle_begin(*parts(halves(mixed), weight_out))
        grad_mlp = open_rows(upstream) * modulated(modulation, 5)
        grad_mlp = grad_mlp.astype(low).reshape(-1, width)
        branch, grad_mlp = hold(branch, grad_mlp)
        branch = fabric.settle_end(branch).reshape(here, inner, width)
        middle = tokens.astype(wide) + gate_one * branch
        normed_two, inverse_two = normalize(middle)
        second_in = flat((normed_two * (1.0 + scale_two) + shift_two).astype(low))
        second_in = fabric.share(second_in)
        return (
            branch, middle, normed_two, inverse_two, both(upstream), both(grad_mlp), second_in,
        )

    (
        branch, middle, normed_two, inverse_two, upstream, grad_mlp, second_in,
    ) = fence(valid, middle_forward, mixed, upstream)

    second_in = both(second_in)
    hidden, slope = [], []
    for rows in second_in:
        preact = dot("tk,jk->tj", rows, up_weight)
        cumulative = 0.5 * (1.0 + lax.erf(preact * 0.7071067811865476))
        density = jnp.exp(-0.5 * preact * preact) * 0.3989422804014327
        hidden.append((preact * cumulative).astype(low))
        slope.append(cumulative + preact * density)
    *hidden, down_weight = hold(*hidden, down_weight)
    down_grad = over_tokens(hidden, grad_mlp)
    grad_total = cotangent.astype(wide)

    *grad_mlp, down_grad = hold(*grad_mlp, down_grad)

    down_sum = fabric.reduce_planes(down_grad)

    def turn_back(grad_mlp):
        grad_pre = [
            (dot("tk,jk->tj", grad_mlp[s], down_weight) * slope[s]).astype(low) for s in (0, 1)
        ]
        grad_pre = hold(*grad_pre)

        near, near_too = hold(*parts(grad_pre, up_weight))
        grad_in = fabric.settle_begin(near, near_too)
        far_hidden, near_too = hold(hidden[1], near_too)
        seats = upstream[1].reshape(2, 2, here, inner, width)
        mlp_far, far_gate = gate_sums(far_hidden, down_weight, seats)
        return hold(*grad_in, over_tokens(grad_pre, second_in), mlp_far, far_gate)

    *grad_in, up_grad, mlp_far, far_gate = fence(valid, turn_back, grad_mlp)
    up_sum = fabric.reduce_planes(up_grad)

    def middle_back(grad_in, mlp_far, far_gate):
        grad_in = fabric.settle_end(grad_in).reshape(here, inner, width)
        grad_shift_two = jnp.sum(grad_in, axis=1)
        grad_scale_two = jnp.sum(grad_in * normed_two, axis=1)
        grad_middle = grad_total + norm_back(grad_in * (1.0 + scale_two), normed_two, inverse_two)
        grad_gate_one = jnp.sum(grad_middle * branch, axis=1)
        grad_branch = flat((grad_middle * gate_one).astype(low))
        ready, grad_branch = hold(hidden[0], grad_branch)
        seats = upstream[0].reshape(2, 2, here, inner, width)
        mlp_near, near_gate = gate_sums(ready, down_weight, seats)
        grad_branch = fabric.share(grad_branch, (mlp_near,))
        mlp_too = fabric.swap(mlp_far, CORE)
        grad_gate_two = far_gate + near_gate
        grad_branch = both(grad_branch)
        grad_mixed = whole([dot("tk,jk->tj", rows, weight_out).astype(low) for rows in grad_branch])
        grad_project = over_images(
            attend_back_body, here, inner, [projected, grad_mixed], 3 * heads * HD
        )
        return (
            grad_shift_two, grad_scale_two, grad_middle, grad_gate_one, grad_gate_two, grad_branch,
            grad_project, mlp_near, mlp_too,
        )

    *grad_in, down_sum = hold(*grad_in, down_sum)
    (
        grad_shift_two, grad_scale_two, grad_middle, grad_gate_one, grad_gate_two, grad_branch,
        grad_project, mlp_near, mlp_too,
    ) = fence(valid, middle_back, grad_in, mlp_far, far_gate)

    def fresh(first, grad):
        grad = grad.astype(wide).reshape(-1, shard_rows, width)
        return matrix_decay * moment[first : first + grad.shape[0]] + grad

    up_sum, down_sum, grad_project = hold(up_sum, down_sum, grad_project)

    def dense_momentum():
        return jnp.concatenate([fresh(4, up_sum), fresh(start_down, down_sum)], axis=0)

    dense_rows, grad_project = hold(dense_momentum().astype(low), grad_project)
    dense_rows = to_owner(dense_rows, 2)

    def attention_back(grad_branch, grad_project):
        grads = halves(grad_project)
        seats = [rows.reshape(2, 2, here, inner, width) for rows in both(tokens_near)]
        near, far = [norm_sums(grads[k], weight_in, seats[k]) for k in (0, 1)]
        in_grad = over_tokens([grad_project], first_in).reshape(3, heads * HD, width)
        out_grad = over_tokens([mixed], grad_branch).reshape(1, heads * HD, width)
        attention_grad = jnp.concatenate([in_grad, out_grad], axis=0)
        attention_grad = attention_grad.reshape(4, heads, peers, shard_rows, width)
        attention_grad = attention_grad.transpose(2, 1, 0, 3, 4)
        returned = [attention_grad[0]]
        for offset in range(1, peers):
            returned.append(lax.ppermute(attention_grad[offset], WORLD, mates(peers - offset)))
        attention_grad = jnp.concatenate(returned + returned[:-1], axis=0)
        attention_grad = lax.dynamic_slice_in_dim(
            attention_grad, (peers - place) % peers * heads, planes, 0
        )
        sums = near[1] + far[1]
        own = jnp.stack([grad_gate_one, grad_shift_two, grad_scale_two], axis=0)
        own = jnp.stack([own, jnp.zeros_like(own)], axis=1)
        stacked = jnp.concatenate([sums, own, grad_gate_two[None]], axis=0)
        stacked = jnp.where(seat // 4 == 0, stacked, stacked[:, ::-1])
        stacked = stacked.reshape(6, 2 * here, fabric.count, shard_rows).astype(low)
        stacked = stacked.transpose(2, 1, 0, 3)
        attention_grad = attention_grad.reshape(planes * 4 * shard_rows, width)
        return attention_grad, stacked, near[0], far[0]

    attention_grad, stacked, first_near, first_far = fence(
        valid, attention_back, grad_branch, grad_project
    )
    attention_grad, dense_rows = hold(attention_grad, dense_rows)
    attention_sum = fabric.reduce_planes(attention_grad)

    def two_of(rows):
        rows = rows.reshape(planes, 2, shard_rows, width)
        mine = lax.dynamic_index_in_dim(rows, side, 1, keepdims=False)
        other = lax.dynamic_index_in_dim(rows, 1 - side, 1, keepdims=False)
        return mine.reshape(slot_rows, width), other.reshape(slot_rows, width)

    def joined(mine, other):
        mine = mine.reshape(planes, 1, shard_rows, width)
        other = other.reshape(planes, 1, shard_rows, width)
        rows = jnp.concatenate([mine, other, mine], axis=1)
        return [
            lax.dynamic_slice(
                rows, ((plane - j) % planes, side, 0, 0), (1, 2, shard_rows, width)
            )[0]
            for j in range(planes)
        ]

    def two_units(own, came):
        return fabric.by_plane(own, came).reshape(2 * planes, shard_rows, width)

    def to_holders(stacked):
        return lax.all_to_all(stacked, WORLD, split_axis=0, concat_axis=0, tiled=True)

    def summed_parts(held):
        held = held.reshape(planes, TEAM, 2 * here, 6, shard_rows)
        return jnp.sum(held.astype(wide), axis=1).reshape(images, 6, shard_rows)

    def enter(dense_rows, stacked, first_far):
        d, d_other = two_of(dense_rows)
        d_x, d_y = fabric.swap(d_other, ALONG_X), fabric.swap(d, ALONG_Y)
        held = to_holders(stacked)
        first_too = fabric.swap(first_far, CORE)
        mlp_split = fabric.settle_split(add(mlp_near, mlp_too).astype(low))
        d, d_x, d_y, first_too, mlp_split, held = hold(d, d_x, d_y, first_too, mlp_split, held)
        grad_mod_all = summed_parts(held)
        d_far = [fabric.swap(piece, CORE) for piece in (d, d_x, d_y)]
        ada_momentum = matrix_decay * moment[start_ada:] + jnp.einsum(
            "nur,nk->urk", grad_mod_all, active.astype(wide), precision=highest
        )
        ada_rows = ada_momentum.astype(low)
        ada_momentum, ada_rows, d_far = hold(ada_momentum, ada_rows, d_far)
        return grad_mod_all, ada_momentum, ada_rows, mlp_split, first_too, [d, d_x, d_y], d_far

    grad_mod_all, ada_momentum, ada_rows, mlp_split, first_too, d, d_far = fence(
        valid, enter, dense_rows, stacked, first_far
    )
    ada_rows = to_owner(ada_rows, 2)

    step_size = matrix_rate * 0.2 * math.sqrt(width)

    def steps_one(d, d_far, grad_mod_all, mlp_hops, first_near, first_too):
        first_split = fabric.settle_pieces(add(first_near, first_too).astype(low))
        grad_active = jnp.einsum(
            "nur,ruk->nk", grad_mod_all, ada_weight.astype(wide), precision=highest
        )
        grad_active_core = fabric.swap(grad_active, CORE)
        d_xy, first_split, grad_active_core = hold(
            fabric.swap(d[1], ALONG_Y), first_split, grad_active_core
        )
        grad_active = grad_active + grad_active_core
        d_far_xy, grad_active = hold(fabric.swap(d_xy, CORE), grad_active)
        d, d_far = d + [d_xy], d_far + [d_far_xy]
        grad_active_x = fabric.swap(grad_active, ALONG_X)
        d_half, d = half_gram(core, d, d_far)
        d, d_half, grad_active_x = hold(d, d_half, grad_active_x)
        grad_active = grad_active + grad_active_x
        d_half, d_other, grad_active, mlp_hops = hold(
            d_half, fabric.swap(d_half, CORE), grad_active, mlp_hops
        )
        mlp_came = fabric.settle_hop(*mlp_hops)
        d = polynomial(core, d, d_half, d_other, True)
        d, mlp_came = hold(d, mlp_came)
        return d, grad_active, mlp_came, first_split

    mlp_kept = mlp_split[0]
    d, grad_active, mlp_came, first_split = fence(
        valid, steps_one, d, d_far, grad_mod_all, mlp_split[1], first_near, first_too
    )
    mlp_sum = (*mlp_kept, *mlp_came)
    d, ada_rows, attention_sum = hold(d, ada_rows, attention_sum)

    def steps_two(
        d, ada_rows, attention_sum, mlp_sum, first_split, grad_active, ada_momentum
    ):
        a, a_other = hold(*two_of(ada_rows))
        a_x, a_y = fabric.swap(a_other, ALONG_X), fabric.swap(a, ALONG_Y)
        t_own = padded(fresh(0, attention_sum).astype(low), planes)
        d, d_far, t_own, attention_sum = hold(d, fabric.swap(d, CORE), t_own, attention_sum)

        t_slots = {0: lax.dynamic_index_in_dim(t_own, plane, 0, keepdims=False)}
        t_slots.update(fabric.to_owners(t_own, 0))
        t_slots.update(fabric.to_owners(t_own, 1))
        a_far = fabric.swap(a, CORE)
        d_half, _ = half_gram(core, [d], [d_far])
        d, d_half, t_slots, a_x, a_y, a_far = hold(d, d_half, t_slots, a_x, a_y, a_far)

        a_xy = fabric.swap(a_x, ALONG_Y)
        first_kept, first_hops = first_split
        mlp_sum = fabric.settle_add(mlp_sum)
        d_half, d_other, mlp_sum = hold(d_half, fabric.swap(d_half, CORE), mlp_sum)

        t_last = fabric.to_owners(t_own, 2)
        a_far = [a_far] + [fabric.swap(piece, CORE) for piece in (a_x, a_y)]
        d_rows, d_beside = polynomial(core, d, d_half, d_other, False, 2)
        d_rows, d_beside, t_last, a_far, a_xy = hold(d_rows, d_beside, t_last, a_far, a_xy)

        t_slots.update(t_last)
        t_slots = [t_slots[j] for j in range(planes)]
        t_first = jnp.concatenate(t_slots[: planes // 2], axis=0)
        t_second = jnp.concatenate(t_slots[planes // 2 :], axis=0)
        a_far_xy, t_first, t_second, grad_active = hold(
            fabric.swap(a_xy, CORE), t_first, t_second, grad_active
        )

        d_x = fabric.swap(d_beside, ALONG_X)
        t_second_y = fabric.swap(t_second, ALONG_Y)
        t_first_far, t_second_far = fabric.swap(t_first, CORE), fabric.swap(t_second, CORE)
        grad_active_y = fabric.swap(grad_active, ALONG_Y)
        a_half, a = half_gram(core, [a, a_x, a_y, a_xy], a_far + [a_far_xy])
        a, a_half, t_second_y, t_first_far, t_second_far, d_x, grad_active_y = hold(
            a, a_half, t_second_y, t_first_far, t_second_far, d_x, grad_active_y
        )

        d_slots = joined(d_rows, d_x)
        grad_active = grad_active + grad_active_y
        a_half, a_other, d_slots, grad_active = hold(
            a_half, fabric.swap(a_half, CORE), d_slots, grad_active
        )

        t_first_x, t_first_y = fabric.swap(t_first, ALONG_X), fabric.swap(t_first, ALONG_Y)
        t_second_x = fabric.swap(t_second, ALONG_X)
        d_came = fabric.from_owners(d_slots, 0)
        d_came.update(fabric.from_owners(d_slots, 1))
        a = polynomial(core, a, a_half, a_other, True)
        a, t_first_x, t_first_y, t_second_x, d_came, grad_active = hold(
            a, t_first_x, t_first_y, t_second_x, d_came, grad_active
        )

        grad_active_z = fabric.swap(grad_active, TEAM)
        momentum = jnp.concatenate(
            [fresh(0, attention_sum), dense_momentum(), ada_momentum], axis=0
        ).transpose(1, 0, 2)
        a, a_far, grad_active_z, momentum = hold(
            a, fabric.swap(a, CORE), grad_active_z, momentum
        )
        grad_active = grad_active + grad_active_z

        t_first_xy, t_second_xy = fabric.swap(t_first_x, ALONG_Y), fabric.swap(t_second_y, ALONG_X)
        t_first_x_far, t_second_y_far = fabric.swap(t_first_x, CORE), fabric.swap(t_second_y, CORE)
        grad_active = fabric.planes_over(grad_active)
        a_half, _ = half_gram(core, [a], [a_far])
        a, a_half, t_first_x_far, t_second_y_far, t_first_xy, t_second_xy, grad_active = hold(
            a, a_half, t_first_x_far, t_second_y_far, t_first_xy, t_second_xy, grad_active
        )

        a_half, t_first_y_far, t_second_x_far, t_first_xy_far, t_second_xy_far = hold(
            a_half,
            *[
                fabric.swap(piece, CORE)
                for piece in (t_first_y, t_second_x, t_first_xy, t_second_xy)
            ],
        )

        a_other = fabric.swap(a_half, CORE)
        d_mine = fabric.from_owners([rows[:1] for rows in d_slots], 2)
        first_came = [fabric.settle_hop(*first_hops[0])]
        t_half, t = half_gram(
            core,
            [t_first, t_second, t_first_x, t_second_x, t_first_y, t_second_y, t_first_xy,
             t_second_xy],
            [t_first_far, t_second_far, t_first_x_far, t_second_x_far, t_first_y_far,
             t_second_y_far, t_first_xy_far, t_second_xy_far],
        )
        t, t_half, a_half, a_other, d_mine, first_came = hold(
            t, t_half, a_half, a_other, d_mine, first_came
        )

        d_next = fabric.from_owners([rows[1:] for rows in d_slots], 2)
        first_came = first_came + [fabric.settle_hop(*first_hops[1])]
        t_other = fabric.swap(t_half, CORE)
        a_rows, a_beside = polynomial(core, a, a_half, a_other, False, 2)
        a_rows, a_beside, t_half, t_other, d_next, first_came = hold(
            a_rows, a_beside, t_half, t_other, d_next, first_came
        )

        a_x = fabric.swap(a_beside, ALONG_X)
        a_slots = fabric.slots_of(a_rows.reshape(planes, shard_rows, width))
        a_came = {}
        for group in range(3):
            a_came.update(fabric.from_owners(a_slots, group))
        t = polynomial(core, t, t_half, t_other, True)
        t, a_x, a_came = hold(t, a_x, a_came)

        a_side = fabric.slots_of(a_x.reshape(planes, shard_rows, width))
        first_sum = fabric.settle_joined(first_kept, first_came)
        table_grad = jnp.dot(selector.T, grad_active, precision=highest) * silu_slope(level_table)
        table_momentum = vector_decay * table_moment + table_grad
        table_new = level_table - table_rate * table_momentum
        t, t_far, a_side, first_sum, *tables = hold(
            t, fabric.swap(t, CORE), a_side, first_sum, table_grad, table_momentum, table_new
        )

        side_came = fabric.from_owners(a_side, 0)
        side_came.update(fabric.from_owners(a_side, 1))
        mlp_sum = fabric.settle_last(mlp_sum)
        t_half, _ = half_gram(core, [t], [t_far])
        t, t_half, side_came, mlp_sum = hold(t, t_half, side_came, mlp_sum)

        first_sum = fabric.settle_last(first_sum)
        side_last = fabric.from_owners(a_side, 2)
        t_half, t_other = hold(t_half, fabric.swap(t_half, CORE))

        (t_rows,) = polynomial(core, t, t_half, t_other, False, 1)
        t_rows, side_last, first_sum, mlp_sum = hold(t_rows, side_last, first_sum, mlp_sum)

        side_came.update(side_last)
        t_slots = [t_rows[j * shard_rows : (j + 1) * shard_rows] for j in range(planes)]
        t_came = {}
        for group in (2, 0, 1):
            t_came.update(fabric.from_owners(t_slots, group))
        block_out, input_grad = finish(
            mlp_sum, first_sum, tokens, middle, gate_two, grad_middle, scale_one
        )

        place = jnp.stack([plane, side]).astype(jnp.int32)

        def put(came, base, each, which=lambda side: 0):
            return [
                (
                    rows.reshape(-1, shard_rows, width),
                    lambda ref, distance=distance: base
                    + (ref[0] + distance) % planes * each
                    + which(ref[1]),
                )
                for distance, rows in came.items()
            ]

        near_t = fabric.pieces()[0][0]
        t_came[near_t], d_next, d_mine = hold(t_came[near_t], d_next, d_mine)
        items = put({0: d_slots[0], **d_came, **d_mine}, 0, 2)
        items += put(d_next, 0, 2, lambda side: 1)
        items += put({0: a_slots[0], **a_came}, 2 * planes, 2, lambda side: side)
        items += put({0: a_side[0], **side_came}, 2 * planes, 2, lambda side: 1 - side)
        ortho = arrange(place, *zip(*items), 4 * planes)
        ortho = jnp.concatenate(
            [
                jnp.zeros((4, shard_rows, width), low),
                ortho[: 2 * blocks],
                ortho[2 * planes : 2 * planes + 6],
            ],
            axis=0,
        ).transpose(1, 0, 2)
        matrix_new = matrices - step_size * ortho.astype(wide)
        t_came, block_out, input_grad, matrix_new = hold(
            t_came, block_out, input_grad, matrix_new
        )
        ortho = arrange(place, *zip(*put({0: t_slots[0], **t_came}, 0, 1)), planes)
        ortho = ortho[:4].transpose(1, 0, 2).astype(wide)
        matrix_new = matrix_new.at[:, :4].set(matrices[:, :4] - step_size * ortho)
        return matrix_new, block_out, input_grad, tables, momentum

    matrix_new, block_out, input_grad, tables, momentum = fence(
        valid, steps_two, d, ada_rows, attention_sum, mlp_sum, first_split, grad_active,
        ada_momentum,
    )

    bias_grad = jnp.sum(grad_mod_all, axis=0)
    table_grad, table_momentum, table_new = tables
    bias_momentum = vector_decay * bias_moment + bias_grad
    bias_new = modulation_bias - bias_rate * bias_momentum
    return (
        block_out,
        input_grad,
        table_grad,
        table_momentum,
        table_new,
        momentum,
        matrix_new,
        bias_momentum,
        bias_new,
    )


def solution(mesh):
    whole = P(("img", "strip"), None, None)
    table = P(("img", "strip"), None)
    strip = P("img", "strip", None)
    bias = P(None, ("img", "strip"))
    return jax.shard_map(
        on_device,
        mesh=mesh,
        in_specs=(strip, strip, P(), table, table, whole, whole, bias, bias),
        out_specs=(strip, strip, table, table, table, whole, whole, bias, bias),
        check_vma=False,
    )
```

```python
import functools
import math

import jax
import jax.numpy as jnp
from jax import lax
from jax.experimental import pallas as pl
from jax.experimental.pallas import tpu as pltpu
from jax.sharding import PartitionSpec as P

HEADS = 16
HD = 128

highest = lax.Precision.HIGHEST
norm_eps = 1e-06
coef_one = 3.4445
coef_two = -4.775
coef_three = 2.0315
matrix_decay = 0.95
vector_decay = 0.9
matrix_rate = 0.5
bias_rate = 0.003
table_rate = 0.02

WORLD = ("img", "strip")
CORE, ALONG_X, ALONG_Y = 1, 2, 4
TEAM = 8
low = jnp.bfloat16
wide = jnp.float32


def dot(spec, left, right):
    return jnp.einsum(spec, left, right, preferred_element_type=wide)


def after(value, *earlier):
    return lax.optimization_barrier((value, *earlier))[0]


def after_all(values, *earlier):
    return lax.optimization_barrier((*values, *earlier))[: len(values)]


def hold(*values):
    return lax.optimization_barrier(values)


def fence(flag, body, *operands):
    shapes = jax.eval_shape(body, *operands)
    empty = lambda *_: jax.tree.map(lambda leaf: jnp.zeros(leaf.shape, leaf.dtype), shapes)
    return lax.cond(flag, body, empty, *operands)


def add(left, right):
    return left.astype(wide) + right.astype(wide)


def normalize(values):
    center = values - jnp.mean(values, axis=-1, keepdims=True)
    inverse = lax.rsqrt(jnp.mean(center * center, axis=-1, keepdims=True) + norm_eps)
    return (center * inverse, inverse)


def norm_back(grad_hat, normed, inverse):
    mean_grad = jnp.mean(grad_hat, axis=-1, keepdims=True)
    mean_cross = jnp.mean(grad_hat * normed, axis=-1, keepdims=True)
    return inverse * (grad_hat - mean_grad - normed * mean_cross)


def gelu_slope(values):
    cumulative = 0.5 * (1.0 + lax.erf(values * 0.7071067811865476))
    density = jnp.exp(-0.5 * values * values) * 0.3989422804014327
    return cumulative + values * density


def silu_slope(values):
    logistic = jax.nn.sigmoid(values)
    return logistic * (1.0 + values * (1.0 - logistic))


class Fabric:
    def __init__(self):
        self.count = lax.axis_size("img") * lax.axis_size("strip")
        self.planes = self.count // TEAM
        self.me = lax.axis_index(WORLD)
        self.plane = self.me // TEAM
        self.seat = self.me % TEAM
        self.lines = [
            [plane * TEAM + seat for plane in range(self.planes)] for seat in range(TEAM)
        ]

    def swap(self, value, bit):
        return lax.ppermute(value, WORLD, [(d, d ^ bit) for d in range(self.count)])

    def turn(self, value, offset):
        pairs = [(d, (d + offset * TEAM) % self.count) for d in range(self.count)]
        return lax.ppermute(value, WORLD, pairs)

    def gather_planes(self, shard):
        return lax.all_gather(shard, WORLD, axis=0, tiled=True, axis_index_groups=self.lines)

    def reduce_planes(self, parts):
        return lax.psum_scatter(
            parts, WORLD, scatter_dimension=0, tiled=True, axis_index_groups=self.lines
        )

    def trade_planes(self, blocks):
        return lax.all_to_all(
            blocks, WORLD, split_axis=0, concat_axis=0, tiled=True, axis_index_groups=self.lines
        )

    def pieces(self):
        distances = list(range(1, self.planes))
        return [distances[:1], distances[-1:], distances[1:-1]]

    def to_owners(self, blocks, group):
        return {
            distance: self.turn(
                lax.dynamic_index_in_dim(
                    blocks, (self.plane + distance) % self.planes, 0, keepdims=False
                ),
                distance,
            )
            for distance in self.pieces()[group]
        }

    def from_owners(self, slots, group):
        return {distance: self.turn(slots[distance], -distance) for distance in self.pieces()[group]}

    def slots_of(self, blocks):
        return [
            lax.dynamic_index_in_dim(blocks, (self.plane - j) % self.planes, 0, keepdims=False)
            for j in range(self.planes)
        ]

    def by_plane(self, own, came):
        came = {0: own, **came}
        result = jnp.zeros((self.planes,) + own.shape, own.dtype)
        for distance, block in came.items():
            result = lax.dynamic_update_index_in_dim(
                result, block, (self.plane + distance) % self.planes, 0
            )
        return result

    def team_total(self, value):
        for bit in (CORE, ALONG_X, ALONG_Y):
            value = value + self.swap(value, bit)
        return value

    def planes_over(self, value):
        distance = 2
        while distance < self.planes:
            value = value + self.swap(value, distance * TEAM)
            distance *= 2
        return value

    def plane_total(self, value):
        others = [self.turn(value, offset) for offset in range(1, self.planes)]
        for other in others:
            value = value + other
        return value

    def share(self, rows, between=()):
        parts = self.share_begin(rows)
        if between:
            first_x, second_y = after_all(parts[3:5], *between)
            parts = (*parts[:3], first_x, second_y, *parts[5:])
        return self.share_end(parts)

    def share_begin(self, rows):
        half = rows.shape[0] // 2
        first, second = rows[:half], rows[half:]
        return (
            rows,
            self.swap(first, ALONG_Y),
            self.swap(second, ALONG_X),
            self.swap(first, ALONG_X),
            self.swap(second, ALONG_Y),
        )

    def share_end(self, parts):
        return jnp.concatenate(self.share_last(parts), axis=0)

    def share_last(self, parts):
        rows, first_y, second_x, first_x, second_y = parts
        first_xy = self.swap(first_x, ALONG_Y)
        second_xy = self.swap(second_y, ALONG_X)
        return [rows, first_x, second_x, first_y, second_y, first_xy, second_xy]

    def settle(self, near, near_too, beside=None):
        if beside is None:
            return self.settle_end(self.settle_begin(near, near_too))
        parts = self.settle_begin(near, near_too)
        *parts, done = hold(*parts, beside())
        return self.settle_end(parts), done

    def settle_begin(self, near, near_too):
        return self.settle_hops(add(near, near_too).astype(low))

    def settle_pieces(self, near):
        size, width = near.shape[0] // 8, near.shape[-1]
        near = near.reshape(2, 2, 2, size, width)
        first, second = near[:, :, 0], near[:, :, 1]
        return (first[:, 0], second[0]), [(first[k, 1], second[1, k]) for k in (0, 1)]

    def settle_split(self, near):
        size, width = near.shape[0] // 8, near.shape[-1]
        near = near.reshape(2, 2, 2, size, width)
        first, second = near[:, :, 0], near[:, :, 1]
        return (first[:, 0], second[0]), (first[:, 1], second[1])

    def settle_hop(self, first, second):
        return self.swap(first, ALONG_X), self.swap(second, ALONG_Y)

    def settle_joined(self, kept, hops):
        first, second = kept
        (first_a, second_a), (first_b, second_b) = hops
        return (
            (add(first[0], first_a).astype(low), add(first[1], first_b).astype(low)),
            (add(second[0], second_a).astype(low), add(second[1], second_b).astype(low)),
        )

    def settle_hops(self, near):
        size, width = near.shape[0] // 8, near.shape[-1]
        near = near.reshape(2, 2, 2, size, width)
        first, second = near[:, :, 0], near[:, :, 1]
        first_x = self.swap(first[:, 1], ALONG_X)
        second_y = self.swap(second[1], ALONG_Y)
        return first[:, 0], second[0], first_x, second_y

    def settle_end(self, parts):
        return self.settle_sum(self.settle_last(self.settle_add(parts)))

    def settle_add(self, parts):
        first, second, first_x, second_y = parts
        return (
            [add(first[k], first_x[k]).astype(low) for k in (0, 1)],
            [add(second[k], second_y[k]).astype(low) for k in (0, 1)],
        )

    def settle_last(self, parts):
        first, second = parts
        first_y, second_x = self.swap(first[1], ALONG_Y), self.swap(second[1], ALONG_X)
        return first[0], second[0], first_y, second_x

    def settle_sum(self, parts):
        first, second, first_y, second_x = parts
        return jnp.concatenate([add(first, first_y), add(second, second_x)], axis=0)


VMEM_BYTES = 60 * 2**20
QUICK = pl.CostEstimate(flops=1, bytes_accessed=1, transcendentals=0)


def attend_body(projected_ref, mixed_ref):
    size = mixed_ref.shape[-1]
    shape = mixed_ref.shape[:-1] + (HD,)
    tokens = math.prod(shape[:-1])
    for first in range(0, size, HD):

        def read(unit):
            block = projected_ref[..., unit * size + first : unit * size + first + HD]
            return block.reshape(tokens, HD)

        scores = lax.dot_general(
            read(0), read(1), (((1,), (1,)), ((), ())), preferred_element_type=wide
        ) * HD ** (-0.5)
        exponent = jnp.exp(scores - jnp.max(scores, axis=-1, keepdims=True))
        probs = (exponent / jnp.sum(exponent, axis=-1, keepdims=True)).astype(low)
        mixed = jnp.dot(probs, read(2), preferred_element_type=wide).astype(low)
        mixed_ref[..., first : first + HD] = mixed.reshape(shape)


def attend_back_body(projected_ref, grad_ref, out_ref):
    size = grad_ref.shape[-1]
    shape = grad_ref.shape[:-1] + (HD,)
    tokens = math.prod(shape[:-1])
    factor = HD ** (-0.5)
    across = (((1,), (1,)), ((), ()))
    down = (((0,), (0,)), ((), ()))
    for first in range(0, size, HD):

        def read(unit):
            block = projected_ref[..., unit * size + first : unit * size + first + HD]
            return block.reshape(tokens, HD)

        def write(unit, value):
            part = slice(unit * size + first, unit * size + first + HD)
            out_ref[..., part] = value.astype(low).reshape(shape)

        query, keys_all, values_all = read(0), read(1), read(2)
        grad_heads = grad_ref[..., first : first + HD].reshape(tokens, HD)
        scores = lax.dot_general(query, keys_all, across, preferred_element_type=wide) * factor
        exponent = jnp.exp(scores - jnp.max(scores, axis=-1, keepdims=True))
        probs = exponent / jnp.sum(exponent, axis=-1, keepdims=True)
        grad_probs = lax.dot_general(grad_heads, values_all, across, preferred_element_type=wide)
        cross = jnp.sum(probs * grad_probs, axis=-1, keepdims=True)
        grad_scores = (probs * (grad_probs - cross)).astype(low)
        write(0, jnp.dot(grad_scores, keys_all, preferred_element_type=wide) * factor)
        write(1, lax.dot_general(grad_scores, query, down, preferred_element_type=wide) * factor)
        write(2, lax.dot_general(probs.astype(low), grad_heads, down, preferred_element_type=wide))


def over_images(body, here, inner, arrays, out_features):
    def block(features):
        return pl.BlockSpec(
            (2, 1, 2, 1, inner, features), lambda side, image: (0, side, 0, image, 0, 0)
        )

    arrays = [rows.reshape(2, 2, 2, here, inner, rows.shape[-1]) for rows in arrays]
    result = pl.pallas_call(
        body,
        grid=(2, here),
        in_specs=[block(rows.shape[-1]) for rows in arrays],
        out_specs=block(out_features),
        out_shape=jax.ShapeDtypeStruct((2, 2, 2, here, inner, out_features), low),
        compiler_params=pltpu.CompilerParams(vmem_limit_bytes=32 * 2**20),
        cost_estimate=QUICK,
    )(*arrays)
    return result.reshape(-1, out_features)


def modulate_body(rows_ref, modulation_ref, out_ref):
    values = rows_ref[0, 0].astype(wide)
    center = values - jnp.mean(values, axis=-1, keepdims=True)
    inverse = lax.rsqrt(jnp.mean(center * center, axis=-1, keepdims=True) + norm_eps)
    shift = modulation_ref[0, :, 0:1, :]
    scale = modulation_ref[0, :, 1:2, :]
    out_ref[0, 0] = (center * inverse * (1.0 + scale) + shift).astype(low)


def modulate(rows, modulation):
    sides, seats, here, inner, width = rows.shape
    block = pl.BlockSpec((1, 1, here, inner, width), lambda y, x: (y, x, 0, 0, 0))
    return pl.pallas_call(
        modulate_body,
        grid=(sides, seats),
        in_specs=[
            block,
            pl.BlockSpec((1, here) + modulation.shape[2:], lambda y, x: (y, 0, 0, 0)),
        ],
        out_specs=block,
        out_shape=jax.ShapeDtypeStruct(rows.shape, low),
        compiler_params=pltpu.CompilerParams(vmem_limit_bytes=48 * 2**20),
        cost_estimate=QUICK,
    )(rows, modulation)


def gate_body(hidden_ref, weight_ref, upstream_ref, part_ref, cross_ref):
    part = jnp.dot(hidden_ref[...], weight_ref[...], preferred_element_type=wide)
    part_ref[...] = part.astype(low)
    here, inner, width = upstream_ref.shape[2:]
    cross = upstream_ref[0, 0].astype(wide) * part.reshape(here, inner, width)
    cross = jnp.sum(cross, axis=1)[None]

    @pl.when(pl.program_id(1) == 0)
    def _():
        cross_ref[...] = cross

    @pl.when(pl.program_id(1) > 0)
    def _():
        cross_ref[...] += cross


def gate_sums(hidden, weight, upstream):
    sides, seats, here, inner, width = upstream.shape
    size = here * inner
    return pl.pallas_call(
        gate_body,
        grid=(sides, seats),
        in_specs=[
            pl.BlockSpec((size, hidden.shape[1]), lambda y, x: (y * seats + x, 0)),
            pl.BlockSpec(weight.shape, lambda y, x: (0, 0)),
            pl.BlockSpec((1, 1, here, inner, width), lambda y, x: (y, x, 0, 0, 0)),
        ],
        out_specs=[
            pl.BlockSpec((size, width), lambda y, x: (y * seats + x, 0)),
            pl.BlockSpec((1, here, width), lambda y, x: (y, 0, 0)),
        ],
        out_shape=[
            jax.ShapeDtypeStruct((hidden.shape[0], width), low),
            jax.ShapeDtypeStruct((sides, here, width), wide),
        ],
        compiler_params=pltpu.CompilerParams(vmem_limit_bytes=VMEM_BYTES),
        cost_estimate=QUICK,
    )(hidden, weight, upstream)


def norm_sums_body(grad_ref, weight_ref, rows_ref, part_ref, sums_ref):
    part = jnp.dot(grad_ref[...], weight_ref[...], preferred_element_type=wide)
    part_ref[...] = part.astype(low)
    here, inner, width = rows_ref.shape[2:]
    part = part.reshape(here, inner, width)
    values = rows_ref[0, 0].astype(wide)
    center = values - jnp.mean(values, axis=-1, keepdims=True)
    inverse = lax.rsqrt(jnp.mean(center * center, axis=-1, keepdims=True) + norm_eps)
    shift = jnp.sum(part, axis=1)[None, None]
    scale = jnp.sum(part * (center * inverse), axis=1)[None, None]

    @pl.when(pl.program_id(1) == 0)
    def _():
        sums_ref[0:1] = shift
        sums_ref[1:2] = scale

    @pl.when(pl.program_id(1) > 0)
    def _():
        sums_ref[0:1] += shift
        sums_ref[1:2] += scale


def norm_sums(grads, weight, rows):
    sides, seats, here, inner, width = rows.shape
    size = here * inner
    return pl.pallas_call(
        norm_sums_body,
        grid=(sides, seats),
        in_specs=[
            pl.BlockSpec((size, grads.shape[1]), lambda y, x: (y * seats + x, 0)),
            pl.BlockSpec(weight.shape, lambda y, x: (0, 0)),
            pl.BlockSpec((1, 1, here, inner, width), lambda y, x: (y, x, 0, 0, 0)),
        ],
        out_specs=[
            pl.BlockSpec((size, width), lambda y, x: (y * seats + x, 0)),
            pl.BlockSpec((2, 1, here, width), lambda y, x: (0, y, 0, 0)),
        ],
        out_shape=[
            jax.ShapeDtypeStruct((grads.shape[0], width), low),
            jax.ShapeDtypeStruct((2, sides, here, width), wide),
        ],
        compiler_params=pltpu.CompilerParams(vmem_limit_bytes=VMEM_BYTES),
        cost_estimate=QUICK,
    )(grads, weight, rows)


def finish_body(*refs):
    mlp, grads, refs = refs[:4], refs[4:8], refs[8:]
    tokens_ref, middle_ref, gate_ref, upper_ref, scale_ref, out_ref, grad_ref = refs

    def work(kept, came):
        shape = middle_ref.shape
        mlp_out = (mlp[kept][...].astype(wide) + mlp[came][...].astype(wide)).reshape(shape)
        out_ref[...] = (middle_ref[...] + gate_ref[...] * mlp_out).astype(low)
        grad = (grads[kept][...].astype(wide) + grads[came][...].astype(wide)).reshape(shape)
        normed, inverse = normalize(tokens_ref[...].astype(wide))
        grad = norm_back(grad * (1.0 + scale_ref[...]), normed, inverse)
        grad_ref[...] = (upper_ref[...] + grad).astype(low)

    @pl.when(pl.program_id(0) == 0)
    def _():
        work(0, 2)

    @pl.when(pl.program_id(0) == 1)
    def _():
        work(1, 3)


def finish(mlp, grads, tokens, middle, gate, upper, scale):
    here, inner, width = tokens.shape
    part = pl.BlockSpec(mlp[0].shape, lambda i: (0, 0))
    rows = pl.BlockSpec((here // 2, inner, width), lambda i: (i, 0, 0))
    line = pl.BlockSpec((here // 2, 1, width), lambda i: (i, 0, 0))
    return pl.pallas_call(
        finish_body,
        grid=(2,),
        in_specs=[part] * 8 + [rows, rows, line, rows, line],
        out_specs=[rows, rows],
        out_shape=[jax.ShapeDtypeStruct(tokens.shape, low)] * 2,
        compiler_params=pltpu.CompilerParams(vmem_limit_bytes=VMEM_BYTES),
        cost_estimate=QUICK,
    )(*mlp, *grads, tokens, middle, gate, upper, scale)


def arrange_body(place_ref, *refs, places):
    *pieces, out_ref, sem = refs
    copies = [
        pltpu.make_async_copy(piece, out_ref.at[pl.ds(place(place_ref), piece.shape[0])], sem.at[k])
        for k, (piece, place) in enumerate(zip(pieces, places))
    ]
    for copy in copies:
        copy.start()
    for copy in copies:
        copy.wait()


def arrange(place, pieces, places, count):
    anywhere = pl.BlockSpec(memory_space=pl.ANY)
    return pl.pallas_call(
        functools.partial(arrange_body, places=places),
        in_specs=[pl.BlockSpec(memory_space=pltpu.SMEM)] + [anywhere] * len(pieces),
        out_specs=pl.BlockSpec(memory_space=pltpu.VMEM),
        out_shape=jax.ShapeDtypeStruct((count,) + pieces[0].shape[1:], low),
        scratch_shapes=[pltpu.SemaphoreType.DMA((len(pieces),))],
        compiler_params=pltpu.CompilerParams(vmem_limit_bytes=VMEM_BYTES),
        cost_estimate=QUICK,
    )(place, *pieces)


CHUNK = 512
ROW_BLOCK = 256


def gram_body(core_ref, *refs, near_count, far_count):
    pieces = refs[: near_count + far_count]
    out_ref, near_ref, x_ref, sem, near_sem = refs[near_count + far_count :]
    width = x_ref.shape[1]
    half = width // 2
    tile = out_ref.shape[0]
    step = pl.program_id(0)
    start = core_ref[0] * half

    def column(j):
        return pl.multiple_of((start + j * CHUNK) % width, CHUNK)

    def copies(j):
        part = pl.ds(column(j), CHUNK)
        result, row = [], 0
        for k, piece in enumerate(pieces):
            rows = pl.ds(row, piece.shape[0])
            result.append(
                pltpu.make_async_copy(piece.at[:, part], x_ref.at[rows, part], sem.at[j, k])
            )
            row += piece.shape[0]
        return result

    joined = pltpu.make_async_copy(x_ref.at[pl.ds(0, near_ref.shape[0])], near_ref, near_sem)

    @pl.when(step == 0)
    def _():
        for j in range(width // CHUNK):
            for copy in copies(j):
                copy.start()

    left = pl.ds(pl.multiple_of(start + step * tile, tile), tile)
    for j in range(width // CHUNK):

        @pl.when(step == 0)
        def _():
            for copy in copies(j):
                copy.wait()
            if j == width // CHUNK - 1 and near_count > 1:
                joined.start()

        part = pl.ds(column(j), CHUNK)
        total = lax.dot_general(
            x_ref[:, left], x_ref[:, part], (((0,), (0,)), ((), ())), preferred_element_type=wide
        )
        out_ref[:, part] = total.astype(low)

    if near_count > 1:

        @pl.when(step == pl.num_programs(0) - 1)
        def _():
            joined.wait()


def half_gram(core, near, far):
    width = near[0].shape[1]
    near_rows = sum(piece.shape[0] for piece in near)
    far_rows = sum(piece.shape[0] for piece in far)
    anywhere = pl.BlockSpec(memory_space=pl.ANY)
    kept = near_rows if len(near) > 1 else 16
    half, joined = pl.pallas_call(
        functools.partial(gram_body, near_count=len(near), far_count=len(far)),
        grid=(width // 2 // CHUNK,),
        in_specs=[pl.BlockSpec(memory_space=pltpu.SMEM)] + [anywhere] * (len(near) + len(far)),
        out_specs=[pl.BlockSpec((CHUNK, width), lambda i: (i, 0)), anywhere],
        out_shape=[
            jax.ShapeDtypeStruct((width // 2, width), low),
            jax.ShapeDtypeStruct((kept, width), low),
        ],
        scratch_shapes=[
            pltpu.VMEM((near_rows + far_rows, width), low),
            pltpu.SemaphoreType.DMA((width // CHUNK, len(near) + len(far))),
            pltpu.SemaphoreType.DMA,
        ],
        compiler_params=pltpu.CompilerParams(vmem_limit_bytes=VMEM_BYTES),
        cost_estimate=QUICK,
    )(core, *near, *far)
    return half, joined if len(near) > 1 else near[0]


def polynomial_body(core_ref, rows_ref, mine_ref, other_ref, *refs, scaled):
    *outs, gram_ref, wide_ref, low_ref, factor_ref, sem = refs
    width = rows_ref.shape[1]
    half = width // 2
    first = pl.program_id(0) == 0
    core = core_ref[0]
    places = [pl.multiple_of(core * half, half), pl.multiple_of((1 - core) * half, half)]

    def copies(j):
        part = pl.ds(j * CHUNK, CHUNK)
        return [
            pltpu.make_async_copy(
                source.at[:, part], gram_ref.at[pl.ds(places[k], half), part], sem.at[j, k]
            )
            for k, source in enumerate((mine_ref, other_ref))
        ]

    @pl.when(first)
    def _():
        for j in range(width // CHUNK):
            for copy in copies(j):
                copy.start()

    tiles = [slice(start, start + CHUNK) for start in range(0, width, CHUNK)]
    for j, part in enumerate(tiles):

        @pl.when(first)
        def _():
            for copy in copies(j):
                copy.wait()

        wide_ref[:, part] = jnp.dot(
            rows_ref[...], gram_ref[:, part], preferred_element_type=wide
        )
        if not scaled:
            low_ref[:, part] = wide_ref[:, part].astype(low)

    if scaled:

        @pl.when(first)
        def _():
            trace = jnp.float32(0.0)
            size = 256
            row = lax.broadcasted_iota(jnp.int32, (size, size), 0)
            column = lax.broadcasted_iota(jnp.int32, (size, size), 1)
            for start in range(0, width, size):
                block = gram_ref[start : start + size, start : start + size].astype(wide)
                trace += jnp.sum(jnp.where(row == column, block, 0.0))
            factor_ref[0] = 1.0 / (jnp.sqrt(trace) + 1e-07)

        factor = factor_ref[0]
        cube, squared = factor * factor * factor, factor * factor
        for part in tiles:
            product = wide_ref[:, part] * cube
            wide_ref[:, part] = product
            low_ref[:, part] = product.astype(low)
    else:
        factor = squared = jnp.float32(1.0)
    for part in tiles:
        square = jnp.dot(low_ref[...], gram_ref[:, part], preferred_element_type=wide) * squared
        lead = (coef_one * factor) * rows_ref[:, part].astype(wide)
        result = (lead + coef_two * wide_ref[:, part] + coef_three * square).astype(low)
        if len(outs) == 1:
            outs[0][:, part] = result
        else:
            for k, out_ref in enumerate(outs):

                @pl.when(pl.program_id(0) == k)
                def _():
                    out_ref[:, part] = result


def polynomial(core, rows, mine, other, scaled, blocks=None):
    count, width = rows.shape
    if blocks is not None:
        count = blocks * ROW_BLOCK
    anywhere = pl.BlockSpec(memory_space=pl.ANY)
    block = pl.BlockSpec((ROW_BLOCK, width), lambda i: (i, 0))
    if blocks is None:
        out_specs, out_shape = block, jax.ShapeDtypeStruct((count, width), low)
    else:
        out_specs = [pl.BlockSpec((ROW_BLOCK, width), lambda i: (0, 0))] * blocks
        out_shape = [jax.ShapeDtypeStruct((ROW_BLOCK, width), low)] * blocks
    return pl.pallas_call(
        functools.partial(polynomial_body, scaled=scaled),
        grid=(count // ROW_BLOCK,),
        in_specs=[pl.BlockSpec(memory_space=pltpu.SMEM), block, anywhere, anywhere],
        out_specs=out_specs,
        out_shape=out_shape,
        scratch_shapes=[
            pltpu.VMEM((width, width), low),
            pltpu.VMEM((ROW_BLOCK, width), wide),
            pltpu.VMEM((ROW_BLOCK, width), low),
            pltpu.SMEM((1,), wide),
            pltpu.SemaphoreType.DMA((width // CHUNK, 2)),
        ],
        compiler_params=pltpu.CompilerParams(vmem_limit_bytes=VMEM_BYTES),
        cost_estimate=QUICK,
    )(core, rows, mine, other)


def on_device(
    tokens,
    cotangent,
    bin_ids,
    level_table,
    table_moment,
    matrices,
    matrix_moment,
    modulation_bias,
    bias_moment,
):
    fabric = Fabric()
    planes, plane, seat = fabric.planes, fabric.plane, fabric.seat
    strips = lax.axis_size("strip")
    here, inner, width = tokens.shape
    shard_rows, units, _ = matrices.shape
    images = bin_ids.shape[0]
    table_rows = level_table.shape[0]
    blocks = (units - 10) // 2
    start_down = 4 + blocks
    start_ada = 4 + 2 * blocks
    slot_rows = planes * shard_rows
    valid = bin_ids[0] >= 0
    core = (fabric.me % 2).astype(jnp.int32).reshape(1)
    side = seat // 2 % 2
    peers = HD // shard_rows
    heads = planes // peers
    place = fabric.me % peers

    def flat(values):
        return values.reshape(here * inner, width)

    def whole(pair):
        return jnp.concatenate(pair, axis=0)

    def halves(rows):
        return [rows[: rows.shape[0] // 2], rows[rows.shape[0] // 2 :]]

    def parts(rows, weight):
        near, far = [dot("tj,jk->tk", piece, weight).astype(low) for piece in rows]
        return near, fabric.swap(far, CORE)

    def settled(pair):
        return fabric.settle(*pair).reshape(here, inner, width)

    def both(near):
        return [near, fabric.swap(near, CORE)]

    def over_tokens(left, right):
        return dot("tj,tk->jk", whole(left), whole(right)).astype(low)

    row_ids = fabric.me * table_rows + jnp.arange(table_rows, dtype=jnp.int32)
    selector = (bin_ids[:, None] == row_ids[None, :]).astype(wide)
    in_plane = images // planes
    ada_weight = matrices[:, start_ada:, :].astype(low)

    def modulated(modulation, which):
        return modulation[None, :, None, :, None, which]

    def open_rows(rows):
        return rows.reshape(1, 2, 2, here, inner, width).astype(wide)

    active_rows = jax.nn.silu(level_table).astype(low)
    active = jnp.dot(selector.astype(low), active_rows, preferred_element_type=wide)
    active = fabric.plane_total(active.astype(low))

    def gathered(first, last):
        rows = matrices[:, first:last].astype(low).transpose(1, 0, 2)
        rows = after(rows.reshape((last - first) * shard_rows, width), active)
        return fabric.gather_planes(rows)

    attention = gathered(0, 4)
    up_weight = gathered(4, start_down)
    down_weight = gathered(start_down, start_ada)

    moment = matrix_moment.transpose(1, 0, 2)

    def padded(batch, count):
        spare = count - batch.shape[0]
        if spare == 0:
            return batch
        return jnp.concatenate([batch, jnp.zeros((spare,) + batch.shape[1:], batch.dtype)], axis=0)

    def to_owner(batch, each):
        batch = padded(batch, planes * each)
        return fabric.trade_planes(batch.reshape(planes, each * shard_rows, width))

    def to_rows(batch, count):
        return fabric.trade_planes(batch).reshape(-1, shard_rows, width)[:count]

    def begin(active):
        active = fabric.team_total(active)
        rows, active = hold(flat(tokens), active)
        half = rows.shape[0] // 2
        first, second = rows[:half], rows[half:]
        mod_columns = dot("nk,ruk->nur", active, ada_weight) + modulation_bias[None]
        mod_parts = jnp.broadcast_to(
            mod_columns.reshape(planes, 1, in_plane, 6, shard_rows),
            (planes, TEAM, in_plane, 6, shard_rows),
        ).reshape(fabric.count, in_plane, 6, shard_rows)
        mod_parts = lax.all_to_all(mod_parts, WORLD, split_axis=0, concat_axis=0, tiled=True)
        first_x, second_y, mod_parts = hold(
            fabric.swap(first, ALONG_X), fabric.swap(second, ALONG_Y), mod_parts
        )
        modulation = mod_parts.transpose(1, 2, 0, 3).reshape(2, here, 6, width)
        modulation = jnp.where(seat // 4 == 0, modulation, modulation[::-1])
        first_y, second_x, first_xy, second_xy, modulation = hold(
            fabric.swap(first, ALONG_Y),
            fabric.swap(second, ALONG_X),
            fabric.swap(first_x, ALONG_Y),
            fabric.swap(second_y, ALONG_X),
            modulation,
        )
        near = jnp.concatenate(
            [rows, first_x, second_x, first_y, second_y, first_xy, second_xy], axis=0
        )
        first_in = modulate(near.reshape(2, 2, here, inner, width), modulation)
        first_in = both(first_in.reshape(-1, width))
        return active, modulation, first_in, near

    active, modulation, first_in, tokens_near = fence(valid, begin, active)
    local = modulation[0][:, :, None, :]
    shift_one, scale_one, gate_one = local[:, 0], local[:, 1], local[:, 2]
    shift_two, scale_two, gate_two = local[:, 3], local[:, 4], local[:, 5]

    def mates(offset):
        return [
            (d, d // peers * peers + (d % peers + offset) % peers) for d in range(fabric.count)
        ]

    def attention_forward(attention):
        upstream = fabric.share_begin(flat(cotangent))
        attention = attention.reshape(planes, 4, shard_rows, width)
        pieces = [lax.dynamic_slice_in_dim(attention, place * heads, heads, 0)]
        for offset in range(1, peers):
            target = (place + offset) % peers
            payload = lax.dynamic_slice_in_dim(attention, target * heads, heads, 0)
            pieces.append(lax.ppermute(payload, WORLD, mates(offset)))
        attention = jnp.stack(pieces).transpose(2, 1, 0, 3, 4).reshape(4, heads * HD, width)
        weight_in = attention[:3].reshape(3 * heads * HD, width)
        weight_out = attention[3]
        near, far = [dot("tk,jk->tj", rows, weight_in).astype(low) for rows in first_in]
        projected = whole([near, far]).reshape(2, 2, 2, here, inner, 3 * heads * HD)
        projected, upstream = hold(projected, upstream)
        upstream = fabric.share_last(upstream)
        mixed = over_images(attend_body, here, inner, [projected], heads * HD)
        return weight_in, weight_out, projected, mixed, upstream

    weight_in, weight_out, projected, mixed, upstream = fence(valid, attention_forward, attention)


    def middle_forward(mixed, upstream):
        upstream = whole(upstream)
        branch = fabric.settle_begin(*parts(halves(mixed), weight_out))
        grad_mlp = open_rows(upstream) * modulated(modulation, 5)
        grad_mlp = grad_mlp.astype(low).reshape(-1, width)
        branch, grad_mlp = hold(branch, grad_mlp)
        branch = fabric.settle_end(branch).reshape(here, inner, width)
        middle = tokens.astype(wide) + gate_one * branch
        normed_two, inverse_two = normalize(middle)
        second_in = flat((normed_two * (1.0 + scale_two) + shift_two).astype(low))
        second_in = fabric.share(second_in)
        return (
            branch, middle, normed_two, inverse_two, both(upstream), both(grad_mlp), second_in,
        )

    (
        branch, middle, normed_two, inverse_two, upstream, grad_mlp, second_in,
    ) = fence(valid, middle_forward, mixed, upstream)

    second_in = both(second_in)
    hidden, slope = [], []
    for rows in second_in:
        preact = dot("tk,jk->tj", rows, up_weight)
        cumulative = 0.5 * (1.0 + lax.erf(preact * 0.7071067811865476))
        density = jnp.exp(-0.5 * preact * preact) * 0.3989422804014327
        hidden.append((preact * cumulative).astype(low))
        slope.append(cumulative + preact * density)
    *hidden, down_weight = hold(*hidden, down_weight)
    down_grad = over_tokens(hidden, grad_mlp)
    grad_total = cotangent.astype(wide)

    *grad_mlp, down_grad = hold(*grad_mlp, down_grad)

    down_sum = fabric.reduce_planes(down_grad)

    def turn_back(grad_mlp):
        grad_pre = [
            (dot("tk,jk->tj", grad_mlp[s], down_weight) * slope[s]).astype(low) for s in (0, 1)
        ]
        grad_pre = hold(*grad_pre)

        near, near_too = hold(*parts(grad_pre, up_weight))
        grad_in = fabric.settle_begin(near, near_too)
        far_hidden, near_too = hold(hidden[1], near_too)
        seats = upstream[1].reshape(2, 2, here, inner, width)
        mlp_far, far_gate = gate_sums(far_hidden, down_weight, seats)
        return hold(*grad_in, over_tokens(grad_pre, second_in), mlp_far, far_gate)

    *grad_in, up_grad, mlp_far, far_gate = fence(valid, turn_back, grad_mlp)
    up_sum = fabric.reduce_planes(up_grad)

    def middle_back(grad_in, mlp_far, far_gate):
        grad_in = fabric.settle_end(grad_in).reshape(here, inner, width)
        grad_shift_two = jnp.sum(grad_in, axis=1)
        grad_scale_two = jnp.sum(grad_in * normed_two, axis=1)
        grad_middle = grad_total + norm_back(grad_in * (1.0 + scale_two), normed_two, inverse_two)
        grad_gate_one = jnp.sum(grad_middle * branch, axis=1)
        grad_branch = flat((grad_middle * gate_one).astype(low))
        ready, grad_branch = hold(hidden[0], grad_branch)
        seats = upstream[0].reshape(2, 2, here, inner, width)
        mlp_near, near_gate = gate_sums(ready, down_weight, seats)
        grad_branch = fabric.share(grad_branch, (mlp_near,))
        mlp_too = fabric.swap(mlp_far, CORE)
        grad_gate_two = far_gate + near_gate
        grad_branch = both(grad_branch)
        grad_mixed = whole([dot("tk,jk->tj", rows, weight_out).astype(low) for rows in grad_branch])
        grad_project = over_images(
            attend_back_body, here, inner, [projected, grad_mixed], 3 * heads * HD
        )
        return (
            grad_shift_two, grad_scale_two, grad_middle, grad_gate_one, grad_gate_two, grad_branch,
            grad_project, mlp_near, mlp_too,
        )

    *grad_in, down_sum = hold(*grad_in, down_sum)
    (
        grad_shift_two, grad_scale_two, grad_middle, grad_gate_one, grad_gate_two, grad_branch,
        grad_project, mlp_near, mlp_too,
    ) = fence(valid, middle_back, grad_in, mlp_far, far_gate)

    def fresh(first, grad):
        grad = grad.astype(wide).reshape(-1, shard_rows, width)
        return matrix_decay * moment[first : first + grad.shape[0]] + grad

    up_sum, down_sum, grad_project = hold(up_sum, down_sum, grad_project)

    def dense_momentum():
        return jnp.concatenate([fresh(4, up_sum), fresh(start_down, down_sum)], axis=0)

    dense_rows, grad_project = hold(dense_momentum().astype(low), grad_project)
    dense_rows = to_owner(dense_rows, 2)

    def attention_back(grad_branch, grad_project):
        grads = halves(grad_project)
        seats = [rows.reshape(2, 2, here, inner, width) for rows in both(tokens_near)]
        near, far = [norm_sums(grads[k], weight_in, seats[k]) for k in (0, 1)]
        in_grad = over_tokens([grad_project], first_in).reshape(3, heads * HD, width)
        out_grad = over_tokens([mixed], grad_branch).reshape(1, heads * HD, width)
        attention_grad = jnp.concatenate([in_grad, out_grad], axis=0)
        attention_grad = attention_grad.reshape(4, heads, peers, shard_rows, width)
        attention_grad = attention_grad.transpose(2, 1, 0, 3, 4)
        returned = [attention_grad[0]]
        for offset in range(1, peers):
            returned.append(lax.ppermute(attention_grad[offset], WORLD, mates(peers - offset)))
        attention_grad = jnp.concatenate(returned + returned[:-1], axis=0)
        attention_grad = lax.dynamic_slice_in_dim(
            attention_grad, (peers - place) % peers * heads, planes, 0
        )
        sums = near[1] + far[1]
        own = jnp.stack([grad_gate_one, grad_shift_two, grad_scale_two], axis=0)
        own = jnp.stack([own, jnp.zeros_like(own)], axis=1)
        stacked = jnp.concatenate([sums, own, grad_gate_two[None]], axis=0)
        stacked = jnp.where(seat // 4 == 0, stacked, stacked[:, ::-1])
        stacked = stacked.reshape(6, 2 * here, fabric.count, shard_rows).astype(low)
        stacked = stacked.transpose(2, 1, 0, 3)
        attention_grad = attention_grad.reshape(planes * 4 * shard_rows, width)
        return attention_grad, stacked, near[0], far[0]

    attention_grad, stacked, first_near, first_far = fence(
        valid, attention_back, grad_branch, grad_project
    )
    attention_grad, dense_rows = hold(attention_grad, dense_rows)
    attention_sum = fabric.reduce_planes(attention_grad)

    def two_of(rows):
        rows = rows.reshape(planes, 2, shard_rows, width)
        mine = lax.dynamic_index_in_dim(rows, side, 1, keepdims=False)
        other = lax.dynamic_index_in_dim(rows, 1 - side, 1, keepdims=False)
        return mine.reshape(slot_rows, width), other.reshape(slot_rows, width)

    def joined(mine, other):
        mine = mine.reshape(planes, 1, shard_rows, width)
        other = other.reshape(planes, 1, shard_rows, width)
        rows = jnp.concatenate([mine, other, mine], axis=1)
        return [
            lax.dynamic_slice(
                rows, ((plane - j) % planes, side, 0, 0), (1, 2, shard_rows, width)
            )[0]
            for j in range(planes)
        ]

    def two_units(own, came):
        return fabric.by_plane(own, came).reshape(2 * planes, shard_rows, width)

    def to_holders(stacked):
        return lax.all_to_all(stacked, WORLD, split_axis=0, concat_axis=0, tiled=True)

    def summed_parts(held):
        held = held.reshape(planes, TEAM, 2 * here, 6, shard_rows)
        return jnp.sum(held.astype(wide), axis=1).reshape(images, 6, shard_rows)

    def enter(dense_rows, stacked, first_far):
        d, d_other = two_of(dense_rows)
        d_x, d_y = fabric.swap(d_other, ALONG_X), fabric.swap(d, ALONG_Y)
        held = to_holders(stacked)
        first_too = fabric.swap(first_far, CORE)
        mlp_split = fabric.settle_split(add(mlp_near, mlp_too).astype(low))
        d, d_x, d_y, first_too, mlp_split, held = hold(d, d_x, d_y, first_too, mlp_split, held)
        grad_mod_all = summed_parts(held)
        d_far = [fabric.swap(piece, CORE) for piece in (d, d_x, d_y)]
        ada_momentum = matrix_decay * moment[start_ada:] + jnp.einsum(
            "nur,nk->urk", grad_mod_all, active.astype(wide), precision=highest
        )
        ada_rows = ada_momentum.astype(low)
        ada_momentum, ada_rows, d_far = hold(ada_momentum, ada_rows, d_far)
        return grad_mod_all, ada_momentum, ada_rows, mlp_split, first_too, [d, d_x, d_y], d_far

    grad_mod_all, ada_momentum, ada_rows, mlp_split, first_too, d, d_far = fence(
        valid, enter, dense_rows, stacked, first_far
    )
    ada_rows = to_owner(ada_rows, 2)

    step_size = matrix_rate * 0.2 * math.sqrt(width)

    first_split = fabric.settle_pieces(
        add(after(first_near, ada_momentum), first_too).astype(low)
    )
    d_xy, first_split = hold(fabric.swap(d[1], ALONG_Y), first_split)

    def steps_one(d, d_xy, d_far, grad_mod_all, mlp_hops):
        grad_active = jnp.einsum(
            "nur,ruk->nk", grad_mod_all, ada_weight.astype(wide), precision=highest
        )
        grad_active_core = fabric.swap(grad_active, CORE)
        d_far_xy, grad_active_core = hold(fabric.swap(d_xy, CORE), grad_active_core)
        grad_active = grad_active + grad_active_core
        d, d_far = d + [d_xy], d_far + [d_far_xy]
        grad_active_x = fabric.swap(grad_active, ALONG_X)
        d_half, d = half_gram(core, d, d_far)
        d, d_half, grad_active_x = hold(d, d_half, grad_active_x)
        grad_active = grad_active + grad_active_x
        d_half, d_other, grad_active, mlp_hops = hold(
            d_half, fabric.swap(d_half, CORE), grad_active, mlp_hops
        )
        mlp_came = fabric.settle_hop(*mlp_hops)
        d = polynomial(core, d, d_half, d_other, True)
        d, mlp_came = hold(d, mlp_came)
        return d, grad_active, mlp_came

    mlp_kept = mlp_split[0]
    d, grad_active, mlp_came = fence(
        valid, steps_one, d, d_xy, d_far, grad_mod_all, mlp_split[1]
    )
    mlp_sum = (*mlp_kept, *mlp_came)
    d, ada_rows, attention_sum = hold(d, ada_rows, attention_sum)

    def steps_two(
        d, ada_rows, attention_sum, mlp_sum, first_split, grad_active, ada_momentum
    ):
        a, a_other = hold(*two_of(ada_rows))
        a_x, a_y = fabric.swap(a_other, ALONG_X), fabric.swap(a, ALONG_Y)
        t_own = padded(fresh(0, attention_sum).astype(low), planes)
        d, d_far, t_own, attention_sum = hold(d, fabric.swap(d, CORE), t_own, attention_sum)

        t_slots = {0: lax.dynamic_index_in_dim(t_own, plane, 0, keepdims=False)}
        t_slots.update(fabric.to_owners(t_own, 0))
        t_slots.update(fabric.to_owners(t_own, 1))
        a_far = fabric.swap(a, CORE)
        d_half, _ = half_gram(core, [d], [d_far])
        d, d_half, t_slots, a_x, a_y, a_far = hold(d, d_half, t_slots, a_x, a_y, a_far)

        a_xy = fabric.swap(a_x, ALONG_Y)
        first_kept, first_hops = first_split
        mlp_sum = fabric.settle_add(mlp_sum)
        d_half, d_other, mlp_sum = hold(d_half, fabric.swap(d_half, CORE), mlp_sum)

        t_last = fabric.to_owners(t_own, 2)
        a_far = [a_far] + [fabric.swap(piece, CORE) for piece in (a_x, a_y)]
        d_rows, d_beside = polynomial(core, d, d_half, d_other, False, 2)
        d_rows, d_beside, t_last, a_far, a_xy = hold(d_rows, d_beside, t_last, a_far, a_xy)

        t_slots.update(t_last)
        t_slots = [t_slots[j] for j in range(planes)]
        t_first = jnp.concatenate(t_slots[: planes // 2], axis=0)
        t_second = jnp.concatenate(t_slots[planes // 2 :], axis=0)
        a_far_xy, t_first, t_second, grad_active = hold(
            fabric.swap(a_xy, CORE), t_first, t_second, grad_active
        )

        d_x = fabric.swap(d_beside, ALONG_X)
        t_second_y = fabric.swap(t_second, ALONG_Y)
        t_first_far, t_second_far = fabric.swap(t_first, CORE), fabric.swap(t_second, CORE)
        grad_active_y = fabric.swap(grad_active, ALONG_Y)
        a_half, a = half_gram(core, [a, a_x, a_y, a_xy], a_far + [a_far_xy])
        a, a_half, t_second_y, t_first_far, t_second_far, d_x, grad_active_y = hold(
            a, a_half, t_second_y, t_first_far, t_second_far, d_x, grad_active_y
        )

        d_slots = joined(d_rows, d_x)
        grad_active = grad_active + grad_active_y
        a_half, a_other, d_slots, grad_active = hold(
            a_half, fabric.swap(a_half, CORE), d_slots, grad_active
        )

        t_first_x, t_first_y = fabric.swap(t_first, ALONG_X), fabric.swap(t_first, ALONG_Y)
        t_second_x = fabric.swap(t_second, ALONG_X)
        d_came = fabric.from_owners(d_slots, 0)
        d_came.update(fabric.from_owners(d_slots, 1))
        a = polynomial(core, a, a_half, a_other, True)
        a, t_first_x, t_first_y, t_second_x, d_came, grad_active = hold(
            a, t_first_x, t_first_y, t_second_x, d_came, grad_active
        )

        grad_active_z = fabric.swap(grad_active, TEAM)
        momentum = jnp.concatenate(
            [fresh(0, attention_sum), dense_momentum(), ada_momentum], axis=0
        ).transpose(1, 0, 2)
        a, a_far, grad_active_z, momentum = hold(
            a, fabric.swap(a, CORE), grad_active_z, momentum
        )
        grad_active = grad_active + grad_active_z

        t_first_xy, t_second_xy = fabric.swap(t_first_x, ALONG_Y), fabric.swap(t_second_y, ALONG_X)
        t_first_x_far, t_second_y_far = fabric.swap(t_first_x, CORE), fabric.swap(t_second_y, CORE)
        grad_active = fabric.planes_over(grad_active)
        a_half, _ = half_gram(core, [a], [a_far])
        a, a_half, t_first_x_far, t_second_y_far, t_first_xy, t_second_xy, grad_active = hold(
            a, a_half, t_first_x_far, t_second_y_far, t_first_xy, t_second_xy, grad_active
        )

        a_half, t_first_y_far, t_second_x_far, t_first_xy_far, t_second_xy_far = hold(
            a_half,
            *[
                fabric.swap(piece, CORE)
                for piece in (t_first_y, t_second_x, t_first_xy, t_second_xy)
            ],
        )

        a_other = fabric.swap(a_half, CORE)
        d_mine = fabric.from_owners([rows[:1] for rows in d_slots], 2)
        first_came = [fabric.settle_hop(*first_hops[0])]
        t_half, t = half_gram(
            core,
            [t_first, t_second, t_first_x, t_second_x, t_first_y, t_second_y, t_first_xy,
             t_second_xy],
            [t_first_far, t_second_far, t_first_x_far, t_second_x_far, t_first_y_far,
             t_second_y_far, t_first_xy_far, t_second_xy_far],
        )
        t, t_half, a_half, a_other, d_mine, first_came = hold(
            t, t_half, a_half, a_other, d_mine, first_came
        )

        d_next = fabric.from_owners([rows[1:] for rows in d_slots], 2)
        first_came = first_came + [fabric.settle_hop(*first_hops[1])]
        t_other = fabric.swap(t_half, CORE)
        a_rows, a_beside = polynomial(core, a, a_half, a_other, False, 2)
        a_rows, a_beside, t_half, t_other, d_next, first_came = hold(
            a_rows, a_beside, t_half, t_other, d_next, first_came
        )

        a_x = fabric.swap(a_beside, ALONG_X)
        a_slots = fabric.slots_of(a_rows.reshape(planes, shard_rows, width))
        a_came = {}
        for group in range(3):
            a_came.update(fabric.from_owners(a_slots, group))
        t = polynomial(core, t, t_half, t_other, True)
        t, a_x, a_came = hold(t, a_x, a_came)

        a_side = fabric.slots_of(a_x.reshape(planes, shard_rows, width))
        first_sum = fabric.settle_joined(first_kept, first_came)
        table_grad = jnp.dot(selector.T, grad_active, precision=highest) * silu_slope(level_table)
        table_momentum = vector_decay * table_moment + table_grad
        table_new = level_table - table_rate * table_momentum
        t, t_far, a_side, first_sum, *tables = hold(
            t, fabric.swap(t, CORE), a_side, first_sum, table_grad, table_momentum, table_new
        )

        side_came = fabric.from_owners(a_side, 0)
        side_came.update(fabric.from_owners(a_side, 1))
        mlp_sum = fabric.settle_last(mlp_sum)
        t_half, _ = half_gram(core, [t], [t_far])
        t, t_half, side_came, mlp_sum = hold(t, t_half, side_came, mlp_sum)

        first_sum = fabric.settle_last(first_sum)
        side_last = fabric.from_owners(a_side, 2)
        t_half, t_other = hold(t_half, fabric.swap(t_half, CORE))

        (t_rows,) = polynomial(core, t, t_half, t_other, False, 1)
        t_rows, side_last, first_sum, mlp_sum = hold(t_rows, side_last, first_sum, mlp_sum)

        side_came.update(side_last)
        t_slots = [t_rows[j * shard_rows : (j + 1) * shard_rows] for j in range(planes)]
        t_came = {}
        for group in (2, 0, 1):
            t_came.update(fabric.from_owners(t_slots, group))
        block_out, input_grad = finish(
            mlp_sum, first_sum, tokens, middle, gate_two, grad_middle, scale_one
        )

        place = jnp.stack([plane, side]).astype(jnp.int32)

        def put(came, base, each, which=lambda side: 0):
            return [
                (
                    rows.reshape(-1, shard_rows, width),
                    lambda ref, distance=distance: base
                    + (ref[0] + distance) % planes * each
                    + which(ref[1]),
                )
                for distance, rows in came.items()
            ]

        near_t = fabric.pieces()[0][0]
        t_came[near_t], d_next, d_mine = hold(t_came[near_t], d_next, d_mine)
        items = put({0: d_slots[0], **d_came, **d_mine}, 0, 2)
        items += put(d_next, 0, 2, lambda side: 1)
        items += put({0: a_slots[0], **a_came}, 2 * planes, 2, lambda side: side)
        items += put({0: a_side[0], **side_came}, 2 * planes, 2, lambda side: 1 - side)
        ortho = arrange(place, *zip(*items), 4 * planes)
        ortho = jnp.concatenate(
            [
                jnp.zeros((4, shard_rows, width), low),
                ortho[: 2 * blocks],
                ortho[2 * planes : 2 * planes + 6],
            ],
            axis=0,
        ).transpose(1, 0, 2)
        matrix_new = matrices - step_size * ortho.astype(wide)
        t_came, block_out, input_grad, matrix_new = hold(
            t_came, block_out, input_grad, matrix_new
        )
        ortho = arrange(place, *zip(*put({0: t_slots[0], **t_came}, 0, 1)), planes)
        ortho = ortho[:4].transpose(1, 0, 2).astype(wide)
        matrix_new = matrix_new.at[:, :4].set(matrices[:, :4] - step_size * ortho)
        return matrix_new, block_out, input_grad, tables, momentum

    matrix_new, block_out, input_grad, tables, momentum = fence(
        valid, steps_two, d, ada_rows, attention_sum, mlp_sum, first_split, grad_active,
        ada_momentum,
    )

    bias_grad = jnp.sum(grad_mod_all, axis=0)
    table_grad, table_momentum, table_new = tables
    bias_momentum = vector_decay * bias_moment + bias_grad
    bias_new = modulation_bias - bias_rate * bias_momentum
    return (
        block_out,
        input_grad,
        table_grad,
        table_momentum,
        table_new,
        momentum,
        matrix_new,
        bias_momentum,
        bias_new,
    )


def solution(mesh):
    whole = P(("img", "strip"), None, None)
    table = P(("img", "strip"), None)
    strip = P("img", "strip", None)
    bias = P(None, ("img", "strip"))
    return jax.shard_map(
        on_device,
        mesh=mesh,
        in_specs=(strip, strip, P(), table, table, whole, whole, bias, bias),
        out_specs=(strip, strip, table, table, table, whole, whole, bias, bias),
        check_vma=False,
    )
```
